32 devices in a mesh: dp: 4 (over y, x), mp: 8 (over z, core).
Axes of the slice: x: 2, y: 2, z: 4, core: 2. Of those that a mesh axis runs over, the one named last changes fastest.
Arguments:
- tokens: bfloat16 [32768, 1024], P(('dp', 'mp')), may hold values from -6 to 6
- cotangent: bfloat16 [32768, 1024], P(('dp', 'mp')), may hold values from -6 to 6
- first_norm_gain: float32 [1024], replicated, may hold values from 0.25 to 1.75
- query_key_value_weight: bfloat16 [1024, 16, 192], P(None, 'mp'), may hold values from -0.1875 to 0.1875
- output_matrix: bfloat16 [16, 64, 1024], P('mp'), may hold values from -1.5 to 1.5
- second_norm_gain: float32 [1024], replicated, may hold values from 0.25 to 1.75
- up_matrix: bfloat16 [4096, 1024], P('mp'), may hold values from -0.1875 to 0.1875
- down_matrix: bfloat16 [4096, 1024], P('mp'), may hold values from -0.09375 to 0.09375
- query_down_factor: float32 [1024, 4], replicated, may hold values from -0.1875 to 0.1875
- query_adapter_up: float32 [4, 1024], replicated, may hold values from -0.3 to 0.3
- value_down_factor: float32 [1024, 4], replicated, may hold values from -0.1875 to 0.1875
- value_adapter_up: float32 [4, 1024], replicated, may hold values from -0.3 to 0.3
- counts: int32 [4, 4], P('dp'), may hold values from 2 to 8, as said below
- lengths: int32 [4, 20], P('dp'), may hold values from 65 to 1024, as said below
Outputs:
- output: bfloat16 [32768, 1024], P(('dp', 'mp'))
- input_grad: bfloat16 [32768, 1024], P(('dp', 'mp'))
- grad_a_q: float32 [1024, 4], replicated
- grad_b_q: float32 [4, 1024], replicated
- grad_a_v: float32 [1024, 4], replicated
- grad_b_v: float32 [4, 1024], replicated
The draws below stay inside these ranges and needn't reach their ends.
Inputs may be any that keep to these rules, and one draw needn't show every extreme that they name: `counts`: each bucket's count lies between half its slots, rounded up, and all of them (4 slots, 8 for bucket 3); in every bucket some group has all its slots live. `lengths`: an item's length is more than half of its bucket's slot length and at most all of it; slot 0 is full in every group. Lengths of slots beyond a bucket's count are present but unused.
All inputs are finite; a program needn't handle non-finite values.
Results may differ from the reference program's by a relative error of at most 0.02.
Values may be sent and summed in bfloat16 or wider, within the bound.
No kernel may reach another device: no remote copies, remote signals or barrier semaphores. Data moves between devices by JAX's collectives and lax.ppermute only.
A program may use at most 256 MiB of HBM per device.

```python
import math
import jax
import jax.numpy as jnp
from jax import lax

MODEL_DIM = 1024
ATTENTION_HEADS = 16
HEAD_WIDTH = 64
FF = 4096
ADAPTER_RANK = 4
BASE_LEN = 128
ITEMS = 4
GROUP_TOK = 8192
TOKENS = 32768


def draw_counts(key, part):
    key = jax.random.fold_in(key, 11)
    groups = TOKENS // GROUP_TOK
    limits = jnp.array([ITEMS, ITEMS, ITEMS, 2 * ITEMS], dtype=jnp.int32)
    lowest = (limits + 1) // 2
    raw_draw = jax.random.randint(jax.random.fold_in(key, 1), (groups, 4), 0, 1 << 20)
    counts = lowest[None, :] + raw_draw % (limits - lowest + 1)[None, :]
    full_group = jax.random.randint(jax.random.fold_in(key, 2), (4,), 0, groups)
    group_ids = jnp.arange(groups, dtype=jnp.int32)[:, None]
    counts = jnp.where(group_ids == full_group[None, :], limits[None, :], counts)
    least_group = (full_group + 1) % groups
    counts = jnp.where(group_ids == least_group[None, :], lowest[None, :], counts)
    return counts.astype(jnp.int32)


def draw_lengths(key, part):
    key = jax.random.fold_in(key, 23)
    groups = TOKENS // GROUP_TOK
    slot_ids = jnp.arange(5 * ITEMS, dtype=jnp.int32)
    bucket_len = jnp.where(slot_ids < ITEMS, 8 * BASE_LEN, jnp.where(slot_ids < 2 * ITEMS, 4 * BASE_LEN, jnp.where(slot_ids < 3 * ITEMS, 2 * BASE_LEN, BASE_LEN)))
    lowest = bucket_len // 2 + 1
    raw_draw = jax.random.randint(jax.random.fold_in(key, 1), (groups, 5 * ITEMS), 0, 1 << 20)
    lengths = lowest[None, :] + raw_draw % (bucket_len - lowest + 1)[None, :]
    leading = slot_ids == 0
    lengths = jnp.where(leading[None, :], bucket_len[None, :], lengths)
    pick_group = jax.random.randint(jax.random.fold_in(key, 2), (), 0, groups)
    pick_slot = 3 * ITEMS + 1 + jax.random.randint(jax.random.fold_in(key, 3), (), 0, 2 * ITEMS - 1)
    target = (jnp.arange(groups, dtype=jnp.int32)[:, None] == pick_group) & (slot_ids[None, :] == pick_slot)
    return jnp.where(target, BASE_LEN // 2 + 1, lengths).astype(jnp.int32)


def block_levels(stream_key, shape, split, low, largest):
    loudness = 1.0
    for axis_at, blocks in split:
        draws = jax.random.uniform(jax.random.fold_in(jax.random.fold_in(stream_key, 6), axis_at), (blocks,), jnp.float32, low / len(split), largest / len(split))
        loudness = loudness * jnp.repeat(jnp.exp(draws), shape[axis_at] // blocks).reshape((-1,) + (1,) * (len(shape) - 1 - axis_at))
    return loudness


def centred(rng, extent, deviation, limit, cuts=(), kind=jnp.bfloat16):
    values = deviation * jax.random.normal(rng, extent, jnp.float32)
    if cuts:
        values = values * block_levels(rng, extent, cuts, -0.22, 0.18)
    return jnp.clip(values, -limit, limit).astype(kind)


def setup_inputs(seed: int = 0) -> dict:
    seeds = jax.random.split(jax.random.key(seed), 15)
    tokens = centred(seeds[0], (TOKENS, MODEL_DIM), 1.0, 6.0, ((0, 32),))
    cotangent = centred(seeds[1], (TOKENS, MODEL_DIM), 1.0, 6.0, ((0, 32),))
    first_norm_gain = jnp.clip(1.0 + 0.15 * jax.random.normal(seeds[2], (MODEL_DIM,), jnp.float32), 0.25, 1.75)
    query_key_value_weight = centred(seeds[3], (MODEL_DIM, ATTENTION_HEADS, 3 * HEAD_WIDTH), MODEL_DIM ** -0.5, 0.1875, ((1, 8),))
    output_matrix = centred(seeds[4], (ATTENTION_HEADS, HEAD_WIDTH, MODEL_DIM), (MODEL_DIM // 64) ** -0.5, 1.5, ((0, 8),))
    second_norm_gain = jnp.clip(1.0 + 0.15 * jax.random.normal(seeds[5], (MODEL_DIM,), jnp.float32), 0.25, 1.75)
    up_matrix = centred(seeds[6], (FF, MODEL_DIM), MODEL_DIM ** -0.5, 0.1875, ((0, 8),))
    down_matrix = centred(seeds[7], (FF, MODEL_DIM), FF ** -0.5, 0.09375, ((0, 8),))
    query_down_factor = centred(seeds[8], (MODEL_DIM, ADAPTER_RANK), MODEL_DIM ** -0.5, 0.1875, (), jnp.float32)
    query_adapter_up = centred(seeds[9], (ADAPTER_RANK, MODEL_DIM), 0.05, 0.3, (), jnp.float32)
    value_down_factor = centred(seeds[10], (MODEL_DIM, ADAPTER_RANK), MODEL_DIM ** -0.5, 0.1875, (), jnp.float32)
    value_adapter_up = centred(seeds[11], (ADAPTER_RANK, MODEL_DIM), 0.05, 0.3, (), jnp.float32)
    counts = draw_counts(jax.random.fold_in(seeds[14], 71), 0)
    lengths = draw_lengths(jax.random.fold_in(seeds[14], 71), 0)
    return dict(tokens=tokens, cotangent=cotangent, first_norm_gain=first_norm_gain, query_key_value_weight=query_key_value_weight, output_matrix=output_matrix, second_norm_gain=second_norm_gain, up_matrix=up_matrix, down_matrix=down_matrix, query_down_factor=query_down_factor, query_adapter_up=query_adapter_up, value_down_factor=value_down_factor, value_adapter_up=value_adapter_up, counts=counts, lengths=lengths)


norm_eps = 1e-05
adapter_scale = 8.0
top_precision = lax.Precision.HIGHEST
masked_score = -1e+30

@jax.custom_vjp
def low(v):
    return lax.optimization_barrier(v.astype(jnp.bfloat16)).astype(jnp.float32)

@jax.custom_vjp
def low_back(v):
    return v

def low_keep(v):
    return (low(v), None)

def low_pass(kept, grad):
    return (grad,)

def back_keep(v):
    return (v, None)

def back_low(kept, grad):
    return (low(grad),)
low.defvjp(low_keep, low_pass)
low_back.defvjp(back_keep, back_low)

def bucket_table():
    return [(8 * BASE_LEN, ITEMS, 0), (4 * BASE_LEN, ITEMS, ITEMS), (2 * BASE_LEN, ITEMS, 2 * ITEMS), (BASE_LEN, 2 * ITEMS, 3 * ITEMS)]

def token_valid(counts, lengths):
    pieces = []
    for bucket, (length, number, offset) in enumerate(bucket_table()):
        slot_ids = jnp.arange(number, dtype=jnp.int32)
        living = slot_ids < counts[bucket]
        places = jnp.arange(length, dtype=jnp.int32)
        inside = places[None, :] < lengths[offset:offset + number][:, None]
        pieces.append(jnp.logical_and(living[:, None], inside).reshape(-1))
    return jnp.concatenate(pieces).astype(jnp.float32)

def layer_norm(values, norm_gain):
    center = values - lax.optimization_barrier(jnp.mean(values, axis=-1, keepdims=True))
    spread = lax.optimization_barrier(jnp.mean(center * center, axis=-1, keepdims=True))
    return center * lax.rsqrt(spread + norm_eps) * norm_gain

def gelu_tanh(values):
    return jax.nn.gelu(values, approximate=True)

def item_attention(query_vectors, key_rows, rows_of_values, valid_rows):
    length = query_vectors.shape[0]
    scores = low_back(jnp.einsum('qhd,khd->hqk', query_vectors, key_rows, precision=top_precision) * (1.0 / math.sqrt(HEAD_WIDTH)))
    places = jnp.arange(length, dtype=jnp.int32)
    causal = places[:, None] >= places[None, :]
    diagonal = places[:, None] == places[None, :]
    allowed = jnp.logical_and(causal, jnp.logical_or(valid_rows[None, :] > 0.0, diagonal))
    scores = jnp.where(allowed[None], scores, masked_score)
    row_max = lax.optimization_barrier(jnp.max(scores, axis=-1, keepdims=True))
    raised = jnp.exp(scores - row_max)
    softmax_out = low(raised / lax.optimization_barrier(jnp.sum(raised, axis=-1, keepdims=True)))
    return jnp.einsum('hqk,khd->qhd', softmax_out, rows_of_values, precision=top_precision)

def attention(query_vectors, key_rows, rows_of_values, valid_rows):
    outputs = []
    row_start = 0
    for length, number, offset in bucket_table():
        region = length * number
        packed = tuple((lax.slice_in_dim(array, row_start, row_start + region).reshape((number, length) + array.shape[1:]) for array in (query_vectors, key_rows, rows_of_values, valid_rows)))
        result = lax.map(jax.checkpoint(lambda items: item_attention(*items)), packed)
        outputs.append(result.reshape((region,) + query_vectors.shape[1:]))
        row_start = row_start + region
    return jnp.concatenate(outputs, axis=0)

def forward_group(inputs, adapter_factors, weights, valid_rows):
    query_down_factor, query_adapter_up, value_down_factor, value_adapter_up = adapter_factors
    first_norm_gain, query_key_value_weight, output_matrix, second_norm_gain, up_matrix, down_matrix = weights
    rows_of_group = inputs.shape[0]
    first_normed = low(layer_norm(inputs, first_norm_gain))
    projected_rows = jnp.dot(first_normed, query_key_value_weight.reshape(MODEL_DIM, 3 * MODEL_DIM), precision=top_precision).reshape(rows_of_group, ATTENTION_HEADS, 3, HEAD_WIDTH)
    query_reduced = jnp.dot(first_normed, query_down_factor, precision=top_precision)
    value_reduced = jnp.dot(first_normed, value_down_factor, precision=top_precision)
    query_vectors = projected_rows[:, :, 0] + adapter_scale * jnp.dot(query_reduced, query_adapter_up, precision=top_precision).reshape(rows_of_group, ATTENTION_HEADS, HEAD_WIDTH)
    key_rows = projected_rows[:, :, 1]
    rows_of_values = projected_rows[:, :, 2] + adapter_scale * jnp.dot(value_reduced, value_adapter_up, precision=top_precision).reshape(rows_of_group, ATTENTION_HEADS, HEAD_WIDTH)
    query_vectors = low(low_back(query_vectors))
    key_rows = low(low_back(key_rows))
    rows_of_values = low(low_back(rows_of_values))
    attended = low(low_back(attention(query_vectors, key_rows, rows_of_values, valid_rows)))
    attn_sum = low_back(jnp.dot(attended.reshape(rows_of_group, MODEL_DIM), output_matrix.reshape(MODEL_DIM, MODEL_DIM), precision=top_precision))
    mid = inputs + attn_sum
    normed_two = low(layer_norm(mid, second_norm_gain))
    hidden_pre = low_back(jnp.dot(normed_two, up_matrix.T, precision=top_precision))
    hidden = low(gelu_tanh(hidden_pre))
    mlp_sum = low_back(jnp.dot(hidden, down_matrix, precision=top_precision))
    return (mid + mlp_sum) * valid_rows[:, None]

def reference(tokens, cotangent, first_norm_gain, query_key_value_weight, output_matrix, second_norm_gain, up_matrix, down_matrix, query_down_factor, query_adapter_up, value_down_factor, value_adapter_up, counts, lengths):
    groups = counts.shape[0]
    weights = tuple((weight_matrix.astype(jnp.float32) for weight_matrix in (first_norm_gain, query_key_value_weight, output_matrix, second_norm_gain, up_matrix, down_matrix)))
    adapter_factors = tuple((weight_matrix.astype(jnp.float32) for weight_matrix in (query_down_factor, query_adapter_up, value_down_factor, value_adapter_up)))
    grouped_inputs = tokens.astype(jnp.float32).reshape(groups, GROUP_TOK, MODEL_DIM)
    grouped_grads = cotangent.astype(jnp.float32).reshape(groups, GROUP_TOK, MODEL_DIM)

    def one_group(packed):
        inputs, grad_output, group_counts, group_lengths = packed
        valid_rows = token_valid(group_counts, group_lengths)

        def forward(values, adapter_set):
            return forward_group(values, adapter_set, weights, valid_rows)
        output, pullback = jax.vjp(forward, inputs, adapter_factors)
        grad_inputs, grad_adapters = pullback(grad_output)
        return (output, grad_inputs, grad_adapters)
    outputs, grad_inputs, grad_adapters = lax.map(one_group, (grouped_inputs, grouped_grads, counts, lengths))
    summed = [lax.optimization_barrier(jnp.sum(gradient, axis=0)) for gradient in grad_adapters]
    return (outputs.reshape(TOKENS, MODEL_DIM).astype(jnp.bfloat16), grad_inputs.reshape(TOKENS, MODEL_DIM).astype(jnp.bfloat16), summed[0], summed[1], summed[2], summed[3])
```

```python
import functools
import math

import jax
import jax.numpy as jnp
import numpy as np
from jax import lax
from jax.experimental import pallas as pl
from jax.experimental.pallas import tpu as pltpu
from jax.sharding import PartitionSpec as P

BASE_LEN = 128
ITEMS = 4
BLOCK = 256
VMEM_LIMIT = 56 * 1024 * 1024

norm_eps = 1e-05
adapter_scale = 8.0
top_precision = lax.Precision.HIGHEST
masked_score = -1e30
f32 = jnp.float32
bf16 = jnp.bfloat16


def dot_nn(a, b):
    return lax.dot_general(a, b, (((1,), (0,)), ((), ())), preferred_element_type=f32)


def dot_nt(a, b):
    return lax.dot_general(a, b, (((1,), (1,)), ((), ())), preferred_element_type=f32)


def dot_tn(a, b):
    return lax.dot_general(a, b, (((0,), (0,)), ((), ())), preferred_element_type=f32)


def split_hi_lo(v):
    hi = v.astype(bf16)
    return hi, (v - hi.astype(f32)).astype(bf16)


def whole(a):
    return pl.BlockSpec(a.shape, lambda *i: (0,) * a.ndim)


def params():
    return pltpu.CompilerParams(vmem_limit_bytes=VMEM_LIMIT)


def attn_fwd_kernel(n_ref, w_ref, e_ref, lr_ref, kaug_ref, qaug_ref, bias_ref, qkv_ref, o_ref, lse_ref):
    rows = n_ref.shape[0]
    w = w_ref[0].reshape(384, w_ref.shape[3])
    res = dot_nt(w, n_ref[...]) + dot_nn(e_ref[0], lr_ref[...])
    low = res.astype(bf16)
    for h in range(2):
        a, b = h * 192, h * 192 + 96
        q = jnp.concatenate([low[a : a + 32], low[b : b + 32]], axis=0) * bf16(0.125)
        k = jnp.concatenate([low[a + 32 : a + 64], low[b + 32 : b + 64]], axis=0)
        v = jnp.concatenate([low[a + 64 : a + 96], low[b + 64 : b + 96]], axis=0)
        qkv_ref[0, h * 192 : h * 192 + 64] = q
        qkv_ref[0, h * 192 + 64 : h * 192 + 128] = k
        qkv_ref[0, h * 192 + 128 : h * 192 + 192] = v
        qa = jnp.concatenate([q, qaug_ref[...]], axis=0)
        ka = jnp.concatenate([k, kaug_ref[...]], axis=0)
        for ib in range(rows // BLOCK):
            here = slice(ib * BLOCK, (ib + 1) * BLOCK)
            upto = (ib + 1) * BLOCK
            s = dot_tn(ka[:, :upto], qa[:, here])
            diag = s[ib * BLOCK :] + bias_ref[ib]
            s = jnp.concatenate([s[: ib * BLOCK], diag], axis=0) if ib else diag
            top = jnp.max(s, axis=0, keepdims=True)
            p = jnp.exp(s - top)
            total = jnp.sum(p, axis=0, keepdims=True)
            o = dot_nn(v[:, :upto], p.astype(bf16)) * (1.0 / total)
            o_ref[0, h * 64 : (h + 1) * 64, here] = o.astype(bf16)
            lse_ref[0, h : h + 1, here] = top + jnp.log(total)


def attn_fwd(normed, w, e, lr, kaug, qaug, bias):
    shards = w.shape[0]
    rows, width = normed.shape
    return pl.pallas_call(
        attn_fwd_kernel,
        grid=(shards,),
        in_specs=[
            whole(normed),
            pl.BlockSpec((1, 4, 96, width), lambda i: (i, 0, 0, 0)),
            pl.BlockSpec((1,) + e.shape[1:], lambda i: (i, 0, 0)),
            whole(lr), whole(kaug), whole(qaug), whole(bias),
        ],
        out_specs=[
            pl.BlockSpec((1, 384, rows), lambda i: (i, 0, 0)),
            pl.BlockSpec((1, 128, rows), lambda i: (i, 0, 0)),
            pl.BlockSpec((1, 2, rows), lambda i: (i, 0, 0)),
        ],
        out_shape=[
            jax.ShapeDtypeStruct((shards, 384, rows), bf16),
            jax.ShapeDtypeStruct((shards, 128, rows), bf16),
            jax.ShapeDtypeStruct((shards, 2, rows), f32),
        ],
        compiler_params=params(),
    )(normed, w, e, lr, kaug, qaug, bias)


def norm_stats(v):
    center = v - jnp.mean(v, axis=-1, keepdims=True)
    r = lax.rsqrt(jnp.mean(center * center, axis=-1, keepdims=True) + norm_eps)
    return center * r, r


def norm_back(n, r, f):
    return r * (f - jnp.mean(f, axis=-1, keepdims=True) - n * jnp.mean(f * n, axis=-1, keepdims=True))


def out_proj_kernel(o_ref, w_ref, x_ref, gain_ref, mid_ref, n_ref):
    width = x_ref.shape[1]
    o = o_ref[...].reshape(width, BLOCK)
    w = w_ref[...].reshape(width, width)
    mid = x_ref[...].astype(f32) + dot_tn(o, w)
    n, r = norm_stats(mid)
    mid_ref[...] = mid
    n_ref[...] = (n * gain_ref[...]).astype(bf16)


def out_proj(o, w, x, gain):
    rows, width = x.shape
    shards = o.shape[0]
    blk = pl.BlockSpec((BLOCK, width), lambda i: (i, 0))
    return pl.pallas_call(
        out_proj_kernel,
        grid=(rows // BLOCK,),
        in_specs=[
            pl.BlockSpec((shards, 128, BLOCK), lambda i: (0, 0, i)),
            pl.BlockSpec((shards, 4, 32, width), lambda i: (0, 0, 3, 0)),
            blk,
            whole(gain),
        ],
        out_specs=[blk, blk],
        out_shape=[jax.ShapeDtypeStruct((rows, width), f32), jax.ShapeDtypeStruct((rows, width), bf16)],
        compiler_params=params(),
    )(o, w, x, gain)


GELU_C = math.sqrt(2.0 / math.pi)


def mlp_kernel(n_ref, g_ref, b_ref, mid_ref, valid_ref, gain_ref, wo_ref, out_ref, gmid_ref, do_ref, mlp_acc, gnt_acc, *, chunk):
    step = pl.program_id(0)
    rows, width = n_ref.shape

    @pl.when(step == 0)
    def _():
        mlp_acc[...] = jnp.zeros_like(mlp_acc)
        gnt_acc[...] = jnp.zeros_like(gnt_acc)

    up = b_ref[0, :, :128].reshape(512, width)
    down = b_ref[0, :, 128:].reshape(512, width)

    @pl.loop(0, rows // chunk)
    def _(c):
        at = pl.ds(pl.multiple_of(c * chunk, chunk), chunk)
        u = dot_nt(n_ref[at, :], up)
        gh = dot_nt(g_ref[at, :], down)
        uu = u * u
        th = jnp.tanh(u * (GELU_C + (GELU_C * 0.044715) * uu))
        half = 0.5 + 0.5 * th
        hidden = u * half
        slope = half + (0.5 * u) * (1.0 - th * th) * (GELU_C + (3.0 * 0.044715 * GELU_C) * uu)
        mlp_acc[at, :] += dot_nn(hidden.astype(bf16), down)
        gnt_acc[at, :] += dot_nn((gh * slope).astype(bf16), up)

    @pl.when(step == pl.num_programs(0) - 1)
    def _():
        wo = wo_ref[...].reshape(width, width)

        @pl.loop(0, rows // BLOCK)
        def _(c):
            at = pl.ds(pl.multiple_of(c * BLOCK, BLOCK), BLOCK)
            mid = mid_ref[at, :]
            out_ref[at, :] = ((mid + mlp_acc[at, :]) * valid_ref[at, :]).astype(bf16)
            n, r = norm_stats(mid)
            gmid = g_ref[at, :].astype(f32) + norm_back(n, r, gnt_acc[at, :] * gain_ref[...])
            gmid_ref[at, :] = gmid
            do_ref[:, :, at] = dot_nt(wo, gmid.astype(bf16)).astype(bf16).reshape(do_ref.shape[0], 128, BLOCK)


def mlp(normed, g, b, mid, valid, gain, a, chunk=512):
    rows, width = normed.shape
    shards = b.shape[0]
    return pl.pallas_call(
        functools.partial(mlp_kernel, chunk=chunk),
        grid=(shards,),
        in_specs=[
            whole(normed), whole(g),
            pl.BlockSpec((1,) + b.shape[1:], lambda i: (i, 0, 0, 0)),
            whole(mid), whole(valid), whole(gain),
            pl.BlockSpec((shards, 4, 32, width), lambda i: (0, 0, 3, 0)),
        ],
        out_specs=[
            pl.BlockSpec((rows, width), lambda i: (0, 0)),
            pl.BlockSpec((rows, width), lambda i: (0, 0)),
            pl.BlockSpec((shards, 128, rows), lambda i: (0, 0, 0)),
        ],
        out_shape=[
            jax.ShapeDtypeStruct((rows, width), bf16),
            jax.ShapeDtypeStruct((rows, width), f32),
            jax.ShapeDtypeStruct((shards, 128, rows), bf16),
        ],
        scratch_shapes=[pltpu.VMEM((rows, width), f32)] * 2,
        compiler_params=params(),
    )(normed, g, b, mid, valid, gain, a)


def attn_bwd_kernel(qkv_ref, o_ref, do_ref, lse_ref, kaug_ref, qaug_ref, bias_ref, et_ref, lrs_ref, dqkv_ref, gl_ref, gb_ref, dk_acc, dv_acc):
    rows = qkv_ref.shape[2]
    step = pl.program_id(0)
    for h in range(2):
        c = h * 192
        q, k, v = (qkv_ref[0, c + 64 * t : c + 64 * t + 64] for t in range(3))
        qa = jnp.concatenate([q, qaug_ref[...]], axis=0)
        ka = jnp.concatenate([k, kaug_ref[...]], axis=0)
        for ib in range(rows // BLOCK):
            here = slice(ib * BLOCK, (ib + 1) * BLOCK)
            upto = (ib + 1) * BLOCK
            do = do_ref[0, h * 64 : (h + 1) * 64, here]
            o = o_ref[0, h * 64 : (h + 1) * 64, here]
            inner = jnp.sum(do.astype(f32) * o.astype(f32), axis=0, keepdims=True)
            s = dot_tn(ka[:, :upto], qa[:, here])
            diag = s[ib * BLOCK :] + bias_ref[ib]
            s = jnp.concatenate([s[: ib * BLOCK], diag], axis=0) if ib else diag
            p = jnp.exp(s - lse_ref[0, h : h + 1, here])
            dp = dot_tn(v[:, :upto], do)
            ds = (p * (dp - inner)).astype(bf16)
            pb = p.astype(bf16)
            dq = (dot_nn(k[:, :upto], ds) * 0.125).astype(bf16)
            dqkv_ref[0, c : c + 32, here] = dq[:32]
            dqkv_ref[0, c + 96 : c + 128, here] = dq[32:]
            dk = dot_nt(q[:, here], ds)
            dv = dot_nt(do, pb)
            if ib:
                dk_acc[:, : ib * BLOCK] += dk[:, : ib * BLOCK]
                dv_acc[:, : ib * BLOCK] += dv[:, : ib * BLOCK]
            dk_acc[:, here] = dk[:, ib * BLOCK :]
            dv_acc[:, here] = dv[:, ib * BLOCK :]
        for t, acc in ((32, dk_acc), (64, dv_acc)):
            low = acc[...].astype(bf16)
            dqkv_ref[0, c + t : c + t + 32] = low[:32]
            dqkv_ref[0, c + 96 + t : c + 128 + t] = low[32:]
    d = dqkv_ref[0]
    gl = dot_nn(et_ref[0], d)
    gl = gl[:8] + gl[8:]

    @pl.when(step == 0)
    def _():
        gl_ref[...] = gl

    @pl.when(step > 0)
    def _():
        gl_ref[...] += gl

    gb = dot_nt(lrs_ref[...], d)
    gb_ref[0] = gb[:8] + gb[8:]


def attn_bwd(qkv, o, do, lse, kaug, qaug, bias, et, lrs):
    shards, _, rows = qkv.shape
    return pl.pallas_call(
        attn_bwd_kernel,
        grid=(shards,),
        in_specs=[
            pl.BlockSpec((1, 384, rows), lambda i: (i, 0, 0)),
            pl.BlockSpec((1, 128, rows), lambda i: (i, 0, 0)),
            pl.BlockSpec((1, 128, rows), lambda i: (i, 0, 0)),
            pl.BlockSpec((1, 2, rows), lambda i: (i, 0, 0)),
            whole(kaug), whole(qaug), whole(bias),
            pl.BlockSpec((1, 16, 384), lambda i: (i, 0, 0)),
            whole(lrs),
        ],
        out_specs=[
            pl.BlockSpec((1, 384, rows), lambda i: (i, 0, 0)),
            pl.BlockSpec((8, rows), lambda i: (0, 0)),
            pl.BlockSpec((1, 8, 384), lambda i: (i, 0, 0)),
        ],
        out_shape=[
            jax.ShapeDtypeStruct((shards, 384, rows), bf16),
            jax.ShapeDtypeStruct((8, rows), f32),
            jax.ShapeDtypeStruct((shards, 8, 384), f32),
        ],
        scratch_shapes=[pltpu.VMEM((64, rows), f32)] * 2,
        compiler_params=params(),
    )(qkv, o, do, lse, kaug, qaug, bias, et, lrs)


def grad_a_kernel(gl_ref, n_ref, out_ref):
    hi, lo = split_hi_lo(gl_ref[...])
    out_ref[...] = dot_nn(hi, n_ref[...]) + dot_nn(lo, n_ref[...])


def grad_a_rows(gl, normed):
    return pl.pallas_call(
        grad_a_kernel,
        out_shape=jax.ShapeDtypeStruct((8, normed.shape[1]), f32),
        compiler_params=params(),
    )(gl, normed)


def input_grad_kernel(d_ref, w_ref, gl_ref, dn_ref, x_ref, gmid_ref, gain_ref, out_ref):
    width = x_ref.shape[1]
    d = d_ref[...].reshape(-1, BLOCK)
    w = w_ref[...].reshape(-1, width)
    hi, lo = split_hi_lo(gl_ref[...])
    dhi, dlo = split_hi_lo(dn_ref[...])
    g = dot_tn(d, w)
    g += dot_tn(jnp.concatenate([hi, lo, hi], axis=0), jnp.concatenate([dhi, dhi, dlo], axis=0))
    n, r = norm_stats(x_ref[...].astype(f32))
    out_ref[...] = (gmid_ref[...] + norm_back(n, r, g * gain_ref[...])).astype(bf16)


def input_grad_rows(d, w, gl, down_t, x, gmid, gain):
    rows, width = x.shape
    shards = d.shape[0]
    blk = pl.BlockSpec((BLOCK, width), lambda i: (i, 0))
    return pl.pallas_call(
        input_grad_kernel,
        grid=(rows // BLOCK,),
        in_specs=[
            pl.BlockSpec((shards, 384, BLOCK), lambda i: (0, 0, i)),
            pl.BlockSpec((shards, 4, 96, width), lambda i: (0, 0, 0, 0)),
            pl.BlockSpec((8, BLOCK), lambda i: (0, i)),
            whole(down_t),
            blk, blk,
            whole(gain),
        ],
        out_specs=blk,
        out_shape=jax.ShapeDtypeStruct((rows, width), bf16),
        compiler_params=params(),
    )(d, w, gl, down_t, x, gmid, gain)


def bucket_table():
    return [
        (8 * BASE_LEN, ITEMS, 0),
        (4 * BASE_LEN, ITEMS, ITEMS),
        (2 * BASE_LEN, ITEMS, 2 * ITEMS),
        (BASE_LEN, 2 * ITEMS, 3 * ITEMS),
    ]


def token_valid(counts, lengths):
    pieces = []
    for bucket, (length, number, offset) in enumerate(bucket_table()):
        slot_ids = jnp.arange(number, dtype=jnp.int32)
        living = slot_ids < counts[bucket]
        places = jnp.arange(length, dtype=jnp.int32)
        inside = places[None, :] < lengths[offset : offset + number][:, None]
        pieces.append(jnp.logical_and(living[:, None], inside).reshape(-1))
    return jnp.concatenate(pieces).astype(jnp.float32)


def slot_begins():
    begins = []
    at = 0
    for length, number, _ in bucket_table():
        for _ in range(number):
            begins.append(np.full((length,), at, np.int32))
            at += length
    return np.concatenate(begins)


def attention_masks(valid, begin):
    rows = valid.shape[0]
    blocks = rows // BLOCK
    at = jnp.arange(rows, dtype=jnp.int32)
    place = at.reshape(blocks, BLOCK)
    key_place, query_place = place[:, :, None], place[:, None, :]
    allowed = (
        (key_place <= query_place)
        & (key_place >= begin.reshape(blocks, 1, BLOCK))
        & ((valid.reshape(blocks, BLOCK, 1) > 0.0) | (key_place == query_place))
    )
    bias = jnp.where(allowed, 0.0, masked_score).astype(f32)
    block_id = jnp.arange(16, dtype=jnp.int32)[:, None]
    first = jnp.pad(begin[::BLOCK], (0, 16 - blocks))[:, None]
    own = at[None, :] // BLOCK == block_id
    open_pair = own | ((at[None, :] >= first) & (valid[None, :] > 0.0))
    kaug = jnp.where(open_pair | (block_id >= blocks), 0.0, masked_score).astype(bf16)
    qaug = jnp.where(own, 1.0, 0.0).astype(bf16)
    return bias, kaug, qaug


def exact_hi_lo(v):
    hi = lax.reduce_precision(v, 8, 7)
    return hi.astype(bf16), (v - hi).astype(bf16)


def xor_sum(v, axis, size):
    step = 1
    while step < size:
        v = v + lax.ppermute(v, axis, [(i, i ^ step) for i in range(size)])
        step *= 2
    return v


def whole_item_shards(
    tokens,
    cotangent,
    first_norm_gain,
    query_key_value_weight,
    output_matrix,
    second_norm_gain,
    up_matrix,
    down_matrix,
    query_down_factor,
    query_adapter_up,
    value_down_factor,
    value_adapter_up,
    counts,
    lengths,
):
    rows, width = tokens.shape
    heads_here = query_key_value_weight.shape[1]
    dp_size = lax.axis_size("dp")
    mp_size = lax.axis_size("mp")
    model_index = lax.axis_index("mp")
    group_index = lax.axis_index("dp")
    shards = mp_size
    qkv_t = jnp.transpose(query_key_value_weight.reshape(width, 2, 3, 2, 32), (1, 3, 2, 4, 0)).reshape(4, 96, width)
    a_own = jnp.concatenate([qkv_t, output_matrix.reshape(4, 32, width)], axis=1)
    b_own = jnp.concatenate([up_matrix.reshape(4, 128, width), down_matrix.reshape(4, 128, width)], axis=1)
    a_piece = lax.dynamic_slice_in_dim(a_own, group_index, 1, 0)
    b_piece = lax.dynamic_slice_in_dim(b_own, group_index, 1, 0)
    a_all = lax.all_gather(a_piece, ("mp", "dp"), axis=0, tiled=True).reshape(shards, 4, 128, width)
    b_all = lax.all_gather(b_piece, ("mp", "dp"), axis=0, tiled=True).reshape(shards, 4, 256, width)

    valid_all = token_valid(counts[0], lengths[0])
    valid = lax.dynamic_slice_in_dim(valid_all, model_index * rows, rows)
    begin = lax.dynamic_slice_in_dim(jnp.asarray(slot_begins()), model_index * rows, rows) - model_index * rows
    bias, kaug, qaug = attention_masks(valid, begin)
    valid_col = valid[:, None]

    x = tokens.astype(f32)
    center = x - jnp.mean(x, axis=-1, keepdims=True)
    spread = jnp.mean(center * center, axis=-1, keepdims=True)
    normed = (center * lax.rsqrt(spread + norm_eps) * first_norm_gain).astype(bf16)
    grad_out_low = (cotangent.astype(f32) * valid_col).astype(bf16)

    down_t = jnp.concatenate([query_down_factor, value_down_factor], axis=1).T
    dhi, dlo = exact_hi_lo(down_t)
    lowrank = lax.dot_general(
        jnp.concatenate([dhi, dlo], axis=0), normed, (((1,), (1,)), ((), ())), preferred_element_type=f32
    )
    lowrank = lowrank[:8] + lowrank[8:]
    lhi, llo = exact_hi_lo(lowrank)
    lr = jnp.concatenate([lhi, llo, lhi, jnp.zeros_like(lhi)], axis=0)
    lrs = jnp.concatenate([lhi, llo], axis=0)

    qu = adapter_scale * query_adapter_up.reshape(4, shards, 4, 1, 32)
    vu = adapter_scale * value_adapter_up.reshape(4, shards, 4, 1, 32)
    zero = jnp.zeros_like(qu)
    factor = jnp.concatenate(
        [jnp.concatenate([qu, zero, zero], axis=3), jnp.concatenate([zero, zero, vu], axis=3)], axis=0
    ).reshape(8, shards, 384)
    fhi, flo = exact_hi_lo(factor)
    e = jnp.transpose(jnp.concatenate([fhi, fhi, flo, jnp.zeros_like(fhi)], axis=0), (1, 2, 0))
    et = jnp.transpose(jnp.concatenate([fhi, flo], axis=0), (1, 0, 2))

    gain_one = first_norm_gain[None, :]
    gain_two = second_norm_gain[None, :]
    qkv, attended, lse = attn_fwd(normed, a_all, e, lr, kaug, qaug, bias)
    mid, normed_two = out_proj(attended, a_all, tokens, gain_two)
    output, grad_mid, grad_attended = mlp(normed_two, grad_out_low, b_all, mid, valid_col, gain_two, a_all)
    d, gl, gb = attn_bwd(qkv, attended, grad_attended, lse, kaug, qaug, bias, et, lrs)
    ga = grad_a_rows(gl, normed)
    gb = gb.reshape(shards, 2, 4, 4, 3, 32)
    gbq = jnp.transpose(gb[:, 0, :, :, 0], (1, 0, 2, 3)).reshape(4, width)
    gbv = jnp.transpose(gb[:, 1, :, :, 2], (1, 0, 2, 3)).reshape(4, width)
    packed = jnp.concatenate([ga, adapter_scale * gbq, adapter_scale * gbv], axis=0)
    packed = xor_sum(xor_sum(packed, "mp", mp_size), "dp", dp_size)
    input_grad = input_grad_rows(d, a_all, gl, down_t, tokens, grad_mid, gain_one)
    return (
        output,
        input_grad,
        packed[0:4].T,
        packed[8:12],
        packed[4:8].T,
        packed[12:16],
    )


def layer_norm(values, norm_gain):
    center = values - jnp.mean(values, axis=-1, keepdims=True)
    spread = jnp.mean(center * center, axis=-1, keepdims=True)
    return center * lax.rsqrt(spread + norm_eps) * norm_gain


def gelu_tanh(values):
    return jax.nn.gelu(values, approximate=True)


def contract_last(left, right):
    return lax.dot_general(
        left, right, (((1,), (1,)), ((), ())), preferred_element_type=jnp.float32
    )


def take_region(array, row_start, length, number):
    region = lax.slice_in_dim(array, row_start, row_start + length * number)
    return region.reshape((number, length) + array.shape[1:])


def allowed_pairs(valid_rows, length):
    places = jnp.arange(length, dtype=jnp.int32)
    causal = places[:, None] >= places[None, :]
    diagonal = places[:, None] == places[None, :]
    return jnp.logical_and(
        causal[None], jnp.logical_or(valid_rows[:, None, :] > 0.0, diagonal[None])
    )


def masked_scores(query_blk, key_blk, allowed, scale):
    scores = (
        jnp.einsum("nqhd,nkhd->nhqk", query_blk, key_blk, preferred_element_type=jnp.float32)
        * scale
    )
    return jnp.where(allowed[:, None], scores, masked_score)


def region_forward(query_blk, key_blk, value_blk, allowed, scale):
    scores = masked_scores(query_blk, key_blk, allowed, scale)
    row_max = jnp.max(scores, axis=-1, keepdims=True)
    raised = jnp.exp(scores - row_max)
    running = jnp.sum(raised, axis=-1, keepdims=True)
    probs_low = (raised / running).astype(jnp.bfloat16)
    attended = jnp.einsum(
        "nhqk,nkhd->nqhd", probs_low, value_blk, preferred_element_type=jnp.float32
    )
    return (attended, row_max + jnp.log(running))


def region_backward(query_blk, key_blk, value_blk, grad_blk, log_total, allowed, scale):
    scores = masked_scores(query_blk, key_blk, allowed, scale)
    probs = jnp.exp(scores - log_total)
    probs_low = probs.astype(jnp.bfloat16)
    grad_probs = jnp.einsum(
        "nqhd,nkhd->nhqk", grad_blk, value_blk, preferred_element_type=jnp.float32
    )
    inner = jnp.sum(grad_probs * probs, axis=-1, keepdims=True)
    grad_scores = (probs * (grad_probs - inner)).astype(jnp.bfloat16)
    grad_query = (
        jnp.einsum("nhqk,nkhd->nqhd", grad_scores, key_blk, preferred_element_type=jnp.float32)
        * scale
    )
    grad_key = (
        jnp.einsum("nhqk,nqhd->nkhd", grad_scores, query_blk, preferred_element_type=jnp.float32)
        * scale
    )
    grad_value = jnp.einsum(
        "nhqk,nqhd->nkhd", probs_low, grad_blk, preferred_element_type=jnp.float32
    )
    return (grad_query, grad_key, grad_value)


def split_item_shards(
    tokens,
    cotangent,
    first_norm_gain,
    query_key_value_weight,
    output_matrix,
    second_norm_gain,
    up_matrix,
    down_matrix,
    query_down_factor,
    query_adapter_up,
    value_down_factor,
    value_adapter_up,
    counts,
    lengths,
):
    local_rows = tokens.shape[0]
    model_width = tokens.shape[1]
    model_index = lax.axis_index("mp")
    heads_here = query_key_value_weight.shape[1]
    head_size = query_key_value_weight.shape[2] // 3
    head_columns = heads_here * head_size
    adapter_inner_rank = query_down_factor.shape[1]
    scale = 1.0 / math.sqrt(head_size)
    valid_all = token_valid(counts[0], lengths[0])
    rows_of_group = valid_all.shape[0]
    valid_here = lax.dynamic_slice_in_dim(valid_all, model_index * local_rows, local_rows)[:, None]
    adapter_down = jnp.concatenate([query_down_factor, value_down_factor], axis=1)
    inputs = tokens.astype(jnp.float32)
    first_normed = layer_norm(inputs, first_norm_gain).astype(jnp.bfloat16)
    rows_one_all = lax.all_gather(first_normed, "mp", axis=0, tiled=True)
    flat_qkv = query_key_value_weight.reshape(model_width, heads_here * 3 * head_size)
    projected_rows = jnp.dot(rows_one_all, flat_qkv, preferred_element_type=jnp.float32).reshape(
        rows_of_group, heads_here, 3, head_size
    )
    lowrank = jnp.dot(
        rows_one_all, adapter_down, precision=top_precision, preferred_element_type=jnp.float32
    )
    column_begin = model_index * head_columns
    query_up_factor = lax.dynamic_slice_in_dim(query_adapter_up, column_begin, head_columns, 1)
    value_up_factor = lax.dynamic_slice_in_dim(value_adapter_up, column_begin, head_columns, 1)
    query_vectors = projected_rows[:, :, 0] + adapter_scale * jnp.dot(
        lowrank[:, :adapter_inner_rank], query_up_factor, precision=top_precision
    ).reshape(rows_of_group, heads_here, head_size)
    rows_of_values = projected_rows[:, :, 2] + adapter_scale * jnp.dot(
        lowrank[:, adapter_inner_rank:], value_up_factor, precision=top_precision
    ).reshape(rows_of_group, heads_here, head_size)
    query_low = query_vectors.astype(jnp.bfloat16)
    key_low = projected_rows[:, :, 1].astype(jnp.bfloat16)
    value_low = rows_of_values.astype(jnp.bfloat16)
    attended_parts = []
    log_totals = []
    row_start = 0
    for length, number, offset in bucket_table():
        allowed = allowed_pairs(take_region(valid_all, row_start, length, number), length)
        attended, log_total = region_forward(
            take_region(query_low, row_start, length, number),
            take_region(key_low, row_start, length, number),
            take_region(value_low, row_start, length, number),
            allowed,
            scale,
        )
        attended_parts.append(attended.reshape(length * number, head_columns))
        log_totals.append(log_total)
        row_start = row_start + length * number
    attended_low = jnp.concatenate(attended_parts, axis=0).astype(jnp.bfloat16)
    out_flat = output_matrix.reshape(head_columns, model_width)
    attn_sum = lax.psum_scatter(
        jnp.dot(attended_low, out_flat, preferred_element_type=jnp.float32).astype(jnp.bfloat16),
        "mp",
        scatter_dimension=0,
        tiled=True,
    ).astype(jnp.float32)
    mid = inputs + attn_sum
    normed_two = layer_norm(mid, second_norm_gain).astype(jnp.bfloat16)
    grad_out = cotangent.astype(jnp.float32) * valid_here
    grad_out_low = grad_out.astype(jnp.bfloat16)
    rows_two_all = lax.all_gather(normed_two, "mp", axis=0, tiled=True)
    hidden_pre = contract_last(rows_two_all, up_matrix)
    hidden_low = gelu_tanh(hidden_pre).astype(jnp.bfloat16)
    mlp_sum = lax.psum_scatter(
        jnp.dot(hidden_low, down_matrix, preferred_element_type=jnp.float32).astype(jnp.bfloat16),
        "mp",
        scatter_dimension=0,
        tiled=True,
    ).astype(jnp.float32)
    grad_rows_two_all = lax.all_gather(grad_out_low, "mp", axis=0, tiled=True)
    grad_hidden = contract_last(grad_rows_two_all, down_matrix)
    gelu_unused, gelu_back = jax.vjp(gelu_tanh, hidden_pre)
    grad_pre_low = gelu_back(grad_hidden)[0].astype(jnp.bfloat16)
    grad_normed_two = lax.psum_scatter(
        jnp.dot(grad_pre_low, up_matrix, preferred_element_type=jnp.float32).astype(jnp.bfloat16),
        "mp",
        scatter_dimension=0,
        tiled=True,
    ).astype(jnp.float32)
    output = ((mid + mlp_sum) * valid_here).astype(jnp.bfloat16)
    norm_unused, norm_two_back = jax.vjp(lambda values: layer_norm(values, second_norm_gain), mid)
    grad_mid = grad_out + norm_two_back(grad_normed_two)[0]
    grad_mid_low = grad_mid.astype(jnp.bfloat16)
    grad_rows_one_all = lax.all_gather(grad_mid_low, "mp", axis=0, tiled=True)
    grad_attended = (
        contract_last(grad_rows_one_all, out_flat)
        .astype(jnp.bfloat16)
        .reshape(rows_of_group, heads_here, head_size)
    )
    grad_query_parts = []
    grad_key_parts = []
    grad_value_parts = []
    row_start = 0
    for (length, number, offset), log_total in zip(bucket_table(), log_totals):
        allowed = allowed_pairs(take_region(valid_all, row_start, length, number), length)
        grad_query, grad_key, grad_value = region_backward(
            take_region(query_low, row_start, length, number),
            take_region(key_low, row_start, length, number),
            take_region(value_low, row_start, length, number),
            take_region(grad_attended, row_start, length, number),
            log_total,
            allowed,
            scale,
        )
        grad_query_parts.append(grad_query.reshape(length * number, heads_here, head_size))
        grad_key_parts.append(grad_key.reshape(length * number, heads_here, head_size))
        grad_value_parts.append(grad_value.reshape(length * number, heads_here, head_size))
        row_start = row_start + length * number
    grad_query_low = jnp.concatenate(grad_query_parts, axis=0).astype(jnp.bfloat16)
    grad_key_low = jnp.concatenate(grad_key_parts, axis=0).astype(jnp.bfloat16)
    grad_value_low = jnp.concatenate(grad_value_parts, axis=0).astype(jnp.bfloat16)
    grad_query_flat = grad_query_low.reshape(rows_of_group, head_columns)
    grad_value_flat = grad_value_low.reshape(rows_of_group, head_columns)
    query_reduced_gradient = adapter_scale * jnp.dot(
        grad_query_flat,
        query_up_factor.T,
        precision=top_precision,
        preferred_element_type=jnp.float32,
    )
    value_reduced_gradient = adapter_scale * jnp.dot(
        grad_value_flat,
        value_up_factor.T,
        precision=top_precision,
        preferred_element_type=jnp.float32,
    )
    grad_lowrank = jnp.concatenate([query_reduced_gradient, value_reduced_gradient], axis=1)
    grad_qkv_low = jnp.stack([grad_query_low, grad_key_low, grad_value_low], axis=2).reshape(
        rows_of_group, heads_here * 3 * head_size
    )
    partial_rows = contract_last(grad_qkv_low, flat_qkv)
    grad_normed_one = lax.psum_scatter(
        (
            partial_rows
            + jnp.dot(
                grad_lowrank,
                adapter_down.T,
                precision=top_precision,
                preferred_element_type=jnp.float32,
            )
        ).astype(jnp.bfloat16),
        "mp",
        scatter_dimension=0,
        tiled=True,
    ).astype(jnp.float32)
    grad_a_part = lax.dot_general(
        rows_one_all,
        grad_lowrank,
        (((0,), (0,)), ((), ())),
        precision=top_precision,
        preferred_element_type=jnp.float32,
    )
    query_up_gradient_share = adapter_scale * lax.dot_general(
        lowrank[:, :adapter_inner_rank],
        grad_query_flat,
        (((0,), (0,)), ((), ())),
        precision=top_precision,
        preferred_element_type=jnp.float32,
    )
    value_up_gradient_share = adapter_scale * lax.dot_general(
        lowrank[:, adapter_inner_rank:],
        grad_value_flat,
        (((0,), (0,)), ((), ())),
        precision=top_precision,
        preferred_element_type=jnp.float32,
    )
    zero_cols = jnp.zeros((adapter_inner_rank, model_width), jnp.float32)
    grad_bq_full = lax.dynamic_update_slice_in_dim(
        zero_cols, query_up_gradient_share, column_begin, 1
    )
    grad_bv_full = lax.dynamic_update_slice_in_dim(
        zero_cols, value_up_gradient_share, column_begin, 1
    )
    grad_a_all, grad_bq_all, grad_bv_all = lax.psum(
        (grad_a_part, grad_bq_full, grad_bv_full), ("dp", "mp")
    )
    norm_unused, norm_one_back = jax.vjp(lambda values: layer_norm(values, first_norm_gain), inputs)
    input_grad = (grad_mid + norm_one_back(grad_normed_one)[0]).astype(jnp.bfloat16)
    return (
        output,
        input_grad,
        grad_a_all[:, :adapter_inner_rank],
        grad_bq_all,
        grad_a_all[:, adapter_inner_rank:],
        grad_bv_all,
    )


def solution(mesh):
    in_specs = (
        P(("dp", "mp"), None),
        P(("dp", "mp"), None),
        P(),
        P(None, "mp", None),
        P("mp", None, None),
        P(),
        P("mp", None),
        P("mp", None),
        P(),
        P(),
        P(),
        P(),
        P("dp", None),
        P("dp", None),
    )
    out_specs = (P(("dp", "mp"), None), P(("dp", "mp"), None), P(), P(), P(), P())
    whole_items = slot_begins().shape[0] // mesh.shape["mp"] == 8 * BASE_LEN and mesh.shape["dp"] == 4
    return jax.shard_map(
        whole_item_shards if whole_items else split_item_shards,
        mesh=mesh,
        in_specs=in_specs,
        out_specs=out_specs,
        check_vma=False,
    )
```

```python
import functools
import math

import jax
import jax.numpy as jnp
import numpy as np
from jax import lax
from jax.experimental import pallas as pl
from jax.experimental.pallas import tpu as pltpu
from jax.sharding import PartitionSpec as P

BASE_LEN = 128
ITEMS = 4
BLOCK = 256
VMEM_LIMIT = 56 * 1024 * 1024

norm_eps = 1e-05
adapter_scale = 8.0
top_precision = lax.Precision.HIGHEST
masked_score = -1e30
f32 = jnp.float32
bf16 = jnp.bfloat16


def dot_nn(a, b):
    return lax.dot_general(a, b, (((1,), (0,)), ((), ())), preferred_element_type=f32)


def dot_nt(a, b):
    return lax.dot_general(a, b, (((1,), (1,)), ((), ())), preferred_element_type=f32)


def dot_tn(a, b):
    return lax.dot_general(a, b, (((0,), (0,)), ((), ())), preferred_element_type=f32)


def split_hi_lo(v):
    hi = v.astype(bf16)
    return hi, (v - hi.astype(f32)).astype(bf16)


def whole(a):
    return pl.BlockSpec(a.shape, lambda *i: (0,) * a.ndim)


def params():
    return pltpu.CompilerParams(vmem_limit_bytes=VMEM_LIMIT)


def cost(us):
    return pl.CostEstimate(flops=int(us * 1e9), bytes_accessed=int(us * 2e6), transcendentals=0)


def pipeline(number, *stages):
    held = {}
    for t in range(number + len(stages) - 1):
        for k, stage in enumerate(stages):
            unit = t - k
            if 0 <= unit < number:
                held[unit] = stage(unit, *held.pop(unit, ()))


def score_block(ka, qa, bias_ref, ib):
    s = dot_tn(ka[:, : (ib + 1) * BLOCK], qa[:, ib * BLOCK : (ib + 1) * BLOCK])
    diag = s[ib * BLOCK :] + bias_ref[ib]
    return jnp.concatenate([s[: ib * BLOCK], diag], axis=0) if ib else diag


def attn_fwd_kernel(ids_ref, n_ref, w0_ref, w1_ref, w2_ref, w3_ref, e_ref, lr_ref, kaug_ref, qaug_ref, bias_ref, *refs):
    qkv_ref, o_ref, lse_ref, w_ref, wo_ref, tick_ref = refs[-6:]
    tick_ref[...] = jnp.zeros_like(tick_ref)
    rows, width = n_ref.shape
    pieces = [ref[...].reshape(128, width) for ref in (w0_ref, w1_ref, w2_ref, w3_ref)]
    w = jnp.concatenate([p[:96] for p in pieces], axis=0)
    w_ref[0] = w
    wo_ref[0] = jnp.concatenate([p[96:] for p in pieces], axis=0)
    e = jnp.concatenate([e_ref[0, ids_ref[r]] for r in range(4)], axis=0)
    low = (dot_nt(w, n_ref[...]) + dot_nn(e, lr_ref[...])).astype(bf16)
    heads = []
    for h in range(2):
        a, b = h * 192, h * 192 + 96
        q = jnp.concatenate([low[a : a + 32], low[b : b + 32]], axis=0) * bf16(0.125)
        k = jnp.concatenate([low[a + 32 : a + 64], low[b + 32 : b + 64]], axis=0)
        v = jnp.concatenate([low[a + 64 : a + 96], low[b + 64 : b + 96]], axis=0)
        for t, part in enumerate((q, k, v)):
            qkv_ref[0, h * 192 + t * 64 : h * 192 + t * 64 + 64] = part
        heads.append((jnp.concatenate([q, qaug_ref[...]], axis=0), jnp.concatenate([k, kaug_ref[...]], axis=0), v))
    units = [(h, ib) for ib in range(rows // BLOCK) for h in range(2)]

    def scores(t):
        h, ib = units[t]
        return (score_block(heads[h][1], heads[h][0], bias_ref, ib),)

    def softmax(t, s):
        h, ib = units[t]
        top = jnp.max(s, axis=0, keepdims=True)
        p = jnp.exp(s - top)
        total = jnp.sum(p, axis=0, keepdims=True)
        lse_ref[0, h : h + 1, ib * BLOCK : (ib + 1) * BLOCK] = top + jnp.log(total)
        return p.astype(bf16), 1.0 / total

    def attend(t, p, share):
        h, ib = units[t]
        o = dot_nn(heads[h][2][:, : (ib + 1) * BLOCK], p) * share
        o_ref[0, h * 64 : (h + 1) * 64, ib * BLOCK : (ib + 1) * BLOCK] = o.astype(bf16)

    pipeline(len(units), scores, softmax, attend)


def attn_fwd(ids, normed, pieces, e, lr, kaug, qaug, bias, first, number, shards, kept=None):
    rows, width = normed.shape
    one = len(pieces) == 1

    def piece(r):
        if one:
            return pl.BlockSpec((1, 1, 128, width), lambda i, ids: (i, ids[r], 0, 0))
        return pl.BlockSpec((1, 128, width), lambda i, ids: (i, 0, 0))

    def fixed(a):
        return pl.BlockSpec(a.shape, lambda i, ids: (0,) * a.ndim)

    def placed(*shape):
        return pl.BlockSpec((1,) + shape, lambda i, ids: (first + i,) + (0,) * len(shape))

    shapes = [((384, rows), bf16), ((128, rows), bf16), ((2, rows), f32), ((384, width), bf16), ((128, width), bf16)]
    tick = jax.ShapeDtypeStruct((8, 128), f32)
    kept = [] if kept is None else list(kept)
    *kept, tick = pl.pallas_call(
        attn_fwd_kernel,
        grid_spec=pltpu.PrefetchScalarGridSpec(
            num_scalar_prefetch=1,
            grid=(number,),
            in_specs=[fixed(normed)]
            + [piece(r) for r in range(4)]
            + [
                pl.BlockSpec((1,) + e.shape[1:], lambda i, ids: (ids[4 + first + i], 0, 0, 0)),
                fixed(lr), fixed(kaug), fixed(qaug), fixed(bias),
            ]
            + [pl.BlockSpec(memory_space=pl.ANY) for _ in kept],
            out_specs=[placed(*shape) for shape, _ in shapes] + [fixed(tick)],
        ),
        out_shape=[jax.ShapeDtypeStruct((shards,) + shape, kind) for shape, kind in shapes] + [tick],
        input_output_aliases={11 + t: t for t in range(len(kept))},
        compiler_params=params(),
        cost_estimate=cost(2 + 4 * number),
    )(ids, normed, *(pieces * 4 if one else pieces), e, lr, kaug, qaug, bias, *kept)
    return kept, tick


def norm_stats(v):
    center = v - jnp.mean(v, axis=-1, keepdims=True)
    r = lax.rsqrt(jnp.mean(center * center, axis=-1, keepdims=True) + norm_eps)
    return center * r, r


def norm_back(n, r, f):
    return r * (f - jnp.mean(f, axis=-1, keepdims=True) - n * jnp.mean(f * n, axis=-1, keepdims=True))


def out_proj_kernel(o_ref, w_ref, x_ref, gain_ref, mid_ref, n_ref):
    width = x_ref.shape[1]
    o = o_ref[...].reshape(width, BLOCK)
    w = w_ref[...].reshape(width, width)
    mid = x_ref[...].astype(f32) + dot_tn(o, w)
    n, r = norm_stats(mid)
    mid_ref[...] = mid
    n_ref[...] = (n * gain_ref[...]).astype(bf16)


def out_proj(o, w, x, gain):
    rows, width = x.shape
    shards = o.shape[0]
    blk = pl.BlockSpec((BLOCK, width), lambda i: (i, 0))
    return pl.pallas_call(
        out_proj_kernel,
        grid=(rows // BLOCK,),
        in_specs=[pl.BlockSpec((shards, 128, BLOCK), lambda i: (0, 0, i)), whole(w), blk, whole(gain)],
        out_specs=[blk, blk],
        out_shape=[jax.ShapeDtypeStruct((rows, width), f32), jax.ShapeDtypeStruct((rows, width), bf16)],
        compiler_params=params(),
        cost_estimate=cost(7),
    )(o, w, x, gain)


GELU_C = math.sqrt(2.0 / math.pi)


def mlp_kernel(ids_ref, n_ref, g_ref, *refs, sources, resumed, last):
    pieces, refs = refs[:sources], refs[sources:]
    if resumed:
        mlp_in, gnt_in, refs = refs[0], refs[1], refs[2:]
    if last:
        mid_ref, valid_ref, gain_ref, wo_ref, out_ref, gmid_ref, do_ref, mlp_acc, gnt_acc, sems = refs
    else:
        mlp_acc, gnt_acc, sems = refs
    step = pl.program_id(0)
    rows, width = n_ref.shape

    @pl.when(step == 0)
    def _():
        if resumed:
            copies = [
                pltpu.make_async_copy(src, dst, sems.at[t])
                for t, (src, dst) in enumerate(((mlp_in, mlp_acc), (gnt_in, gnt_acc)))
            ]
            for c in copies:
                c.start()
            for c in copies:
                c.wait()
        else:
            mlp_acc[...] = jnp.zeros_like(mlp_acc)
            gnt_acc[...] = jnp.zeros_like(gnt_acc)

    held = [ref[...].reshape(-1, 128, width) for ref in pieces]
    up = jnp.concatenate([p[:, :64].reshape(-1, width) for p in held], axis=0)
    down = jnp.concatenate([p[:, 64:].reshape(-1, width) for p in held], axis=0)
    u = dot_nt(n_ref[...], up)
    gh = dot_nt(g_ref[...], down)
    uu = u * u
    th = jnp.tanh(u * (GELU_C + (GELU_C * 0.044715) * uu))
    half = 0.5 + 0.5 * th
    hidden = u * half
    slope = half + (0.5 * u) * (1.0 - th * th) * (GELU_C + (3.0 * 0.044715 * GELU_C) * uu)
    mlp_acc[...] += dot_nn(hidden.astype(bf16), down)
    gnt_acc[...] += dot_nn((gh * slope).astype(bf16), up)

    if last:

        @pl.when(step == pl.num_programs(0) - 1)
        def _():
            wo = wo_ref[...].reshape(width, width)

            @pl.loop(0, rows // BLOCK)
            def _(c):
                at = pl.ds(pl.multiple_of(c * BLOCK, BLOCK), BLOCK)
                mid = mid_ref[at, :]
                out_ref[at, :] = ((mid + mlp_acc[at, :]) * valid_ref[at, :]).astype(bf16)
                n, r = norm_stats(mid)
                gmid = g_ref[at, :].astype(f32) + norm_back(n, r, gnt_acc[at, :] * gain_ref[...])
                gmid_ref[at, :] = gmid
                do_ref[:, :, at] = dot_nt(wo, gmid.astype(bf16)).astype(bf16).reshape(do_ref.shape[0], 128, BLOCK)


def mlp(ids, normed, g, pieces, steps, kept=None, final=None, gathered=False):
    rows, width = normed.shape
    acc = jax.ShapeDtypeStruct((rows, width), f32)
    sems = pltpu.SemaphoreType.DMA((2,))
    kept = [] if kept is None else list(kept)

    def fixed(a):
        return pl.BlockSpec(a.shape, lambda i, ids: (0,) * len(a.shape))

    def taken(t, a):
        if gathered:
            return pl.BlockSpec((1,) + a.shape[1:], lambda i, ids: (ids[6 + len(pieces) * i + t],) + (0,) * (a.ndim - 1))
        return pl.BlockSpec((a.shape[0] // steps,) + a.shape[1:], lambda i, ids: (i,) + (0,) * (a.ndim - 1))

    if final is None:
        extra, out_shape, scratch = [], [acc, acc], [sems]
    else:
        extra = list(final)
        shards = extra[3].shape[0]
        out_shape = [
            jax.ShapeDtypeStruct((rows, width), bf16),
            acc,
            jax.ShapeDtypeStruct((shards, 128, rows), bf16),
        ]
        scratch = [pltpu.VMEM((rows, width), f32)] * 2 + [sems]
    return pl.pallas_call(
        functools.partial(mlp_kernel, sources=len(pieces), resumed=bool(kept), last=final is not None),
        grid_spec=pltpu.PrefetchScalarGridSpec(
            num_scalar_prefetch=1,
            grid=(steps,),
            in_specs=[fixed(normed), fixed(g)]
            + [taken(t, a) for t, a in enumerate(pieces)]
            + [pl.BlockSpec(memory_space=pl.ANY) for _ in kept]
            + [fixed(a) for a in extra],
            out_specs=[fixed(a) for a in out_shape],
            scratch_shapes=scratch,
        ),
        out_shape=out_shape,
        compiler_params=params(),
        cost_estimate=cost(4 + 5 * steps),
    )(ids, normed, g, *pieces, *kept, *extra)


def attn_bwd_kernel(ids_ref, qkv_ref, o_ref, do_ref, lse_ref, kaug_ref, qaug_ref, bias_ref, et_ref, lrs_ref, n_ref, d_ref, gl_ref, sum_ref, dk_acc, dv_acc, gb_acc):
    rows = qkv_ref.shape[2]
    step = pl.program_id(0)
    heads = []
    for h in range(2):
        q, k, v = (qkv_ref[0, h * 192 + 64 * t : h * 192 + 64 * t + 64] for t in range(3))
        heads.append((q, k, v, jnp.concatenate([q, qaug_ref[...]], axis=0), jnp.concatenate([k, kaug_ref[...]], axis=0)))
    units = [(h, ib) for h in range(2) for ib in range(rows // BLOCK)]

    def products(t):
        h, ib = units[t]
        q, k, v, qa, ka = heads[h]
        here = slice(ib * BLOCK, (ib + 1) * BLOCK)
        do, o = (ref[0, h * 64 : (h + 1) * 64, here] for ref in (do_ref, o_ref))
        inner = jnp.sum(do.astype(f32) * o.astype(f32), axis=0, keepdims=True)
        return do, inner, score_block(ka, qa, bias_ref, ib), dot_tn(v[:, : (ib + 1) * BLOCK], do)

    def scores(t, do, inner, s, dp):
        h, ib = units[t]
        p = jnp.exp(s - lse_ref[0, h : h + 1, ib * BLOCK : (ib + 1) * BLOCK])
        return do, (p * (dp - inner)).astype(bf16), p.astype(bf16)

    def grads(t, do, ds, p):
        h, ib = units[t]
        c = h * 192
        q, k = heads[h][:2]
        before, here = slice(0, ib * BLOCK), slice(ib * BLOCK, (ib + 1) * BLOCK)
        dq = (dot_nn(k[:, : (ib + 1) * BLOCK], ds) * 0.125).astype(bf16)
        d_ref[0, c : c + 32, here] = dq[:32]
        d_ref[0, c + 96 : c + 128, here] = dq[32:]
        for acc, part in ((dk_acc, dot_nt(q[:, here], ds)), (dv_acc, dot_nt(do, p))):
            if ib:
                acc[h, :, before] += part[:, before]
            acc[h, :, here] = part[:, here]

    pipeline(len(units), products, scores, grads)
    for h in range(2):
        c = h * 192
        for t, acc in ((32, dk_acc), (64, dv_acc)):
            low = acc[h].astype(bf16)
            d_ref[0, c + t : c + t + 32] = low[:32]
            d_ref[0, c + 96 + t : c + 128 + t] = low[32:]
    gl = jnp.zeros((16, rows), f32)
    shard = ids_ref[4 + step]
    for r in range(4):
        d = d_ref[0, r * 96 : r * 96 + 96]
        gl += dot_nn(et_ref[0, ids_ref[r]], d)
        gb = dot_nt(lrs_ref[...], d)
        gb = adapter_scale * (gb[:8] + gb[8:])
        is_query = lax.broadcasted_iota(jnp.int32, (8, 32), 0) < 4
        gb_acc[shard * 4 + ids_ref[r]] = jnp.where(is_query, gb[:, :32], gb[:, 64:96])
    gl = gl[:8] + gl[8:]

    @pl.when(step == 0)
    def _():
        gl_ref[...] = gl

    @pl.when(step > 0)
    def _():
        gl_ref[...] += gl

    @pl.when(step == pl.num_programs(0) - 1)
    def _():
        hi, lo = split_hi_lo(gl_ref[...])
        sum_ref[:8] = dot_nn(hi, n_ref[...]) + dot_nn(lo, n_ref[...])
        sum_ref[8:] = jnp.concatenate([gb_acc[t] for t in range(gb_acc.shape[0])], axis=1)


def attn_bwd(ids, qkv, o, do, lse, kaug, qaug, bias, et, lrs, normed):
    shards, _, rows = qkv.shape
    width = normed.shape[1]

    def fixed(*shape):
        return pl.BlockSpec(shape, lambda i, ids: (0,) * len(shape))

    def rel(*shape):
        return pl.BlockSpec((1,) + shape, lambda i, ids: (i,) + (0,) * len(shape))

    return pl.pallas_call(
        attn_bwd_kernel,
        grid_spec=pltpu.PrefetchScalarGridSpec(
            num_scalar_prefetch=1,
            grid=(shards,),
            in_specs=[
                rel(384, rows), rel(128, rows), rel(128, rows), rel(2, rows),
                fixed(*kaug.shape), fixed(*qaug.shape), fixed(*bias.shape),
                pl.BlockSpec((1,) + et.shape[1:], lambda i, ids: (ids[4 + i], 0, 0, 0)),
                fixed(*lrs.shape), fixed(*normed.shape),
            ],
            out_specs=[rel(384, rows), fixed(8, rows), fixed(16, width)],
            scratch_shapes=[pltpu.VMEM((2, 64, rows), f32)] * 2 + [pltpu.VMEM((4 * shards, 8, 32), f32)],
        ),
        out_shape=[
            jax.ShapeDtypeStruct((shards, 384, rows), bf16),
            jax.ShapeDtypeStruct((8, rows), f32),
            jax.ShapeDtypeStruct((16, width), f32),
        ],
        compiler_params=params(),
        cost_estimate=cost(35),
    )(ids, qkv, o, do, lse, kaug, qaug, bias, et, lrs, normed)


def input_grad_kernel(d_ref, w_ref, gl_ref, dn_ref, x_ref, gmid_ref, gain_ref, event_ref, out_ref):
    width = x_ref.shape[1]
    d = d_ref[...].reshape(-1, BLOCK)
    w = w_ref[...].reshape(-1, width)
    hi, lo = split_hi_lo(gl_ref[...])
    dhi, dlo = split_hi_lo(dn_ref[...])
    g = dot_tn(d, w)
    g += dot_tn(jnp.concatenate([hi, lo, hi], axis=0), jnp.concatenate([dhi, dhi, dlo], axis=0))
    n, r = norm_stats(x_ref[...].astype(f32))
    out_ref[...] = (gmid_ref[...] + norm_back(n, r, g * gain_ref[...])).astype(bf16)


def input_grad_rows(d, w, gl, down_t, x, gmid, gain, event):
    rows, width = x.shape
    shards = d.shape[0]
    blk = pl.BlockSpec((BLOCK, width), lambda i: (i, 0))
    return pl.pallas_call(
        input_grad_kernel,
        grid=(rows // BLOCK,),
        in_specs=[
            pl.BlockSpec((shards, 384, BLOCK), lambda i: (0, 0, i)),
            whole(w),
            pl.BlockSpec((8, BLOCK), lambda i: (0, i)),
            whole(down_t),
            blk, blk,
            whole(gain),
            pl.BlockSpec(memory_space=pl.ANY),
        ],
        out_specs=blk,
        out_shape=jax.ShapeDtypeStruct((rows, width), bf16),
        compiler_params=params(),
        cost_estimate=cost(13),
    )(d, w, gl, down_t, x, gmid, gain, event)


def bucket_table():
    return [
        (8 * BASE_LEN, ITEMS, 0),
        (4 * BASE_LEN, ITEMS, ITEMS),
        (2 * BASE_LEN, ITEMS, 2 * ITEMS),
        (BASE_LEN, 2 * ITEMS, 3 * ITEMS),
    ]


def token_valid(counts, lengths):
    pieces = []
    for bucket, (length, number, offset) in enumerate(bucket_table()):
        slot_ids = jnp.arange(number, dtype=jnp.int32)
        living = slot_ids < counts[bucket]
        places = jnp.arange(length, dtype=jnp.int32)
        inside = places[None, :] < lengths[offset : offset + number][:, None]
        pieces.append(jnp.logical_and(living[:, None], inside).reshape(-1))
    return jnp.concatenate(pieces).astype(jnp.float32)


def slot_begins():
    begins = []
    at = 0
    for length, number, _ in bucket_table():
        for _ in range(number):
            begins.append(np.full((length,), at, np.int32))
            at += length
    return np.concatenate(begins)


def attention_masks(valid, begin):
    rows = valid.shape[0]
    blocks = rows // BLOCK
    at = jnp.arange(rows, dtype=jnp.int32)
    place = at.reshape(blocks, BLOCK)
    key_place, query_place = place[:, :, None], place[:, None, :]
    allowed = (
        (key_place <= query_place)
        & (key_place >= begin.reshape(blocks, 1, BLOCK))
        & ((valid.reshape(blocks, BLOCK, 1) > 0.0) | (key_place == query_place))
    )
    bias = jnp.where(allowed, 0.0, masked_score).astype(f32)
    block_id = jnp.arange(16, dtype=jnp.int32)[:, None]
    first = jnp.pad(begin[::BLOCK], (0, 16 - blocks))[:, None]
    own = at[None, :] // BLOCK == block_id
    open_pair = own | ((at[None, :] >= first) & (valid[None, :] > 0.0))
    kaug = jnp.where(open_pair | (block_id >= blocks), 0.0, masked_score).astype(bf16)
    qaug = jnp.where(own, 1.0, 0.0).astype(bf16)
    return bias, kaug, qaug


def exact_hi_lo(v):
    hi = lax.reduce_precision(v, 8, 7)
    return hi.astype(bf16), (v - hi).astype(bf16)


def flip_send(v, axis, bits):
    return lax.ppermute(v, axis, [(i, i ^ bits) for i in range(lax.axis_size(axis))])


def flip_sum(v, axis, flips):
    return sum([flip_send(v, axis, k) for k in flips], v)


def whole_item_shards(
    tokens,
    cotangent,
    first_norm_gain,
    query_key_value_weight,
    output_matrix,
    second_norm_gain,
    up_matrix,
    down_matrix,
    query_down_factor,
    query_adapter_up,
    value_down_factor,
    value_adapter_up,
    counts,
    lengths,
):
    rows, width = tokens.shape
    heads_here = query_key_value_weight.shape[1]
    dp_size = lax.axis_size("dp")
    mp_size = lax.axis_size("mp")
    model_index = lax.axis_index("mp")
    group_index = lax.axis_index("dp")
    shards = mp_size
    qkv_own = jnp.transpose(query_key_value_weight.reshape(width, 2, 3, 2, 32), (1, 3, 2, 4, 0))
    a_own = jnp.concatenate([qkv_own.reshape(4, 96, width), output_matrix.reshape(4, 32, width)], axis=1)
    b_own = jnp.concatenate([up_matrix.reshape(4, 2, 64, width), down_matrix.reshape(4, 2, 64, width)], axis=2)

    def after(v, *events):
        return lax.optimization_barrier((v,) + events)[0]

    def quarter(own):
        return lax.dynamic_slice_in_dim(own, group_index, 1, 0)

    def across(v, flips):
        return jnp.concatenate([flip_send(v, "mp", k) for k in flips], axis=0)

    def plane(v):
        return [v] + [flip_send(v, "dp", k) for k in range(1, dp_size)]

    def other_core(arrays):
        return [flip_send(a, "mp", 1) for a in arrays]

    b_gathered = lax.all_gather(quarter(b_own), ("mp", "dp"), axis=0, tiled=True).reshape(shards, 8, 128, width)
    (a_core,) = other_core([a_own])
    a_far = across(quarter(a_own), (4, 6))
    a_near = flip_send(a_own, "mp", 2)
    (b_core,) = other_core([after(b_own, a_core)])
    (a_near_core,) = other_core([a_near])
    ids = jnp.concatenate(
        [
            group_index ^ jnp.arange(4, dtype=jnp.int32),
            model_index ^ jnp.array([0, 1, 2, 3, 4, 6, 5, 7], dtype=jnp.int32),
        ]
    )

    valid_all = token_valid(counts[0], lengths[0])
    valid = lax.dynamic_slice_in_dim(valid_all, model_index * rows, rows)
    begin = lax.dynamic_slice_in_dim(jnp.asarray(slot_begins()), model_index * rows, rows) - model_index * rows
    bias, kaug, qaug = attention_masks(valid, begin)
    valid_col = valid[:, None]

    x = tokens.astype(f32)
    center = x - jnp.mean(x, axis=-1, keepdims=True)
    spread = jnp.mean(center * center, axis=-1, keepdims=True)
    normed = (center * lax.rsqrt(spread + norm_eps) * first_norm_gain).astype(bf16)
    grad_out_low = (cotangent.astype(f32) * valid_col).astype(bf16)

    down_t = jnp.concatenate([query_down_factor, value_down_factor], axis=1).T
    dhi, dlo = exact_hi_lo(down_t)
    lowrank = lax.dot_general(
        jnp.concatenate([dhi, dlo], axis=0), normed, (((1,), (1,)), ((), ())), preferred_element_type=f32
    )
    lowrank = lowrank[:8] + lowrank[8:]
    lhi, llo = exact_hi_lo(lowrank)
    lr = jnp.concatenate([lhi, llo, lhi, jnp.zeros_like(lhi)], axis=0)
    lrs = jnp.concatenate([lhi, llo], axis=0)

    qu = adapter_scale * query_adapter_up.reshape(4, shards, 4, 1, 32)
    vu = adapter_scale * value_adapter_up.reshape(4, shards, 4, 1, 32)
    zero = jnp.zeros_like(qu)
    factor = jnp.concatenate(
        [jnp.concatenate([qu, zero, zero], axis=3), jnp.concatenate([zero, zero, vu], axis=3)], axis=0
    ).reshape(8, shards, 4, 96)
    fhi, flo = exact_hi_lo(factor)
    e = jnp.transpose(jnp.concatenate([fhi, fhi, flo, jnp.zeros_like(fhi)], axis=0), (1, 2, 3, 0))
    et = jnp.transpose(jnp.concatenate([fhi, flo], axis=0), (1, 2, 0, 3))

    gain_one = first_norm_gain[None, :]
    gain_two = second_norm_gain[None, :]
    fixed = (e, lr, kaug, qaug, bias)
    kept, _ = attn_fwd(ids, normed, [a_own[None]], *fixed, 0, 1, shards)
    kept, tick = attn_fwd(ids, normed, [a_core[None]], *fixed, 1, 1, shards, kept)
    a_same = plane(after(a_far, tick))
    kept, _ = attn_fwd(ids, normed, [a_near[None]], *fixed, 2, 1, shards, kept)
    kept, tick = attn_fwd(ids, normed, [a_near_core[None]], *fixed, 3, 1, shards, kept)
    a_other = other_core([after(a, tick) for a in a_same])
    kept, _ = attn_fwd(ids, normed, a_same, *fixed, 4, 2, shards, kept)
    kept, _ = attn_fwd(ids, normed, a_other, *fixed, 6, 2, shards, kept)
    qkv, attended, lse, w_all, wo_all = kept
    mid, normed_two = out_proj(attended, wo_all, tokens, gain_two)
    sums = mlp(ids, normed_two, grad_out_low, [b_own.reshape(8, 128, width), b_core.reshape(8, 128, width)], 2)
    output, grad_mid, grad_attended = mlp(
        ids, normed_two, grad_out_low, [b_gathered], 6, sums, (mid, valid_col, gain_two, wo_all), gathered=True
    )
    d, gl, packed = attn_bwd(ids, qkv, attended, grad_attended, lse, kaug, qaug, bias, et, lrs, normed)
    packed = flip_sum(packed, "mp", (1,))
    packed = flip_sum(packed, "mp", (2, 4, 6))
    event = packed
    packed = flip_sum(packed, "dp", tuple(range(1, dp_size)))
    input_grad = input_grad_rows(d, w_all, gl, down_t, tokens, grad_mid, gain_one, event)
    return (
        output,
        input_grad,
        packed[0:4].T,
        packed[8:12],
        packed[4:8].T,
        packed[12:16],
    )


def layer_norm(values, norm_gain):
    center = values - jnp.mean(values, axis=-1, keepdims=True)
    spread = jnp.mean(center * center, axis=-1, keepdims=True)
    return center * lax.rsqrt(spread + norm_eps) * norm_gain


def gelu_tanh(values):
    return jax.nn.gelu(values, approximate=True)


def contract_last(left, right):
    return lax.dot_general(
        left, right, (((1,), (1,)), ((), ())), preferred_element_type=jnp.float32
    )


def take_region(array, row_start, length, number):
    region = lax.slice_in_dim(array, row_start, row_start + length * number)
    return region.reshape((number, length) + array.shape[1:])


def allowed_pairs(valid_rows, length):
    places = jnp.arange(length, dtype=jnp.int32)
    causal = places[:, None] >= places[None, :]
    diagonal = places[:, None] == places[None, :]
    return jnp.logical_and(
        causal[None], jnp.logical_or(valid_rows[:, None, :] > 0.0, diagonal[None])
    )


def masked_scores(query_blk, key_blk, allowed, scale):
    scores = (
        jnp.einsum("nqhd,nkhd->nhqk", query_blk, key_blk, preferred_element_type=jnp.float32)
        * scale
    )
    return jnp.where(allowed[:, None], scores, masked_score)


def region_forward(query_blk, key_blk, value_blk, allowed, scale):
    scores = masked_scores(query_blk, key_blk, allowed, scale)
    row_max = jnp.max(scores, axis=-1, keepdims=True)
    raised = jnp.exp(scores - row_max)
    running = jnp.sum(raised, axis=-1, keepdims=True)
    probs_low = (raised / running).astype(jnp.bfloat16)
    attended = jnp.einsum(
        "nhqk,nkhd->nqhd", probs_low, value_blk, preferred_element_type=jnp.float32
    )
    return (attended, row_max + jnp.log(running))


def region_backward(query_blk, key_blk, value_blk, grad_blk, log_total, allowed, scale):
    scores = masked_scores(query_blk, key_blk, allowed, scale)
    probs = jnp.exp(scores - log_total)
    probs_low = probs.astype(jnp.bfloat16)
    grad_probs = jnp.einsum(
        "nqhd,nkhd->nhqk", grad_blk, value_blk, preferred_element_type=jnp.float32
    )
    inner = jnp.sum(grad_probs * probs, axis=-1, keepdims=True)
    grad_scores = (probs * (grad_probs - inner)).astype(jnp.bfloat16)
    grad_query = (
        jnp.einsum("nhqk,nkhd->nqhd", grad_scores, key_blk, preferred_element_type=jnp.float32)
        * scale
    )
    grad_key = (
        jnp.einsum("nhqk,nqhd->nkhd", grad_scores, query_blk, preferred_element_type=jnp.float32)
        * scale
    )
    grad_value = jnp.einsum(
        "nhqk,nqhd->nkhd", probs_low, grad_blk, preferred_element_type=jnp.float32
    )
    return (grad_query, grad_key, grad_value)


def split_item_shards(
    tokens,
    cotangent,
    first_norm_gain,
    query_key_value_weight,
    output_matrix,
    second_norm_gain,
    up_matrix,
    down_matrix,
    query_down_factor,
    query_adapter_up,
    value_down_factor,
    value_adapter_up,
    counts,
    lengths,
):
    local_rows = tokens.shape[0]
    model_width = tokens.shape[1]
    model_index = lax.axis_index("mp")
    heads_here = query_key_value_weight.shape[1]
    head_size = query_key_value_weight.shape[2] // 3
    head_columns = heads_here * head_size
    adapter_inner_rank = query_down_factor.shape[1]
    scale = 1.0 / math.sqrt(head_size)
    valid_all = token_valid(counts[0], lengths[0])
    rows_of_group = valid_all.shape[0]
    valid_here = lax.dynamic_slice_in_dim(valid_all, model_index * local_rows, local_rows)[:, None]
    adapter_down = jnp.concatenate([query_down_factor, value_down_factor], axis=1)
    inputs = tokens.astype(jnp.float32)
    first_normed = layer_norm(inputs, first_norm_gain).astype(jnp.bfloat16)
    rows_one_all = lax.all_gather(first_normed, "mp", axis=0, tiled=True)
    flat_qkv = query_key_value_weight.reshape(model_width, heads_here * 3 * head_size)
    projected_rows = jnp.dot(rows_one_all, flat_qkv, preferred_element_type=jnp.float32).reshape(
        rows_of_group, heads_here, 3, head_size
    )
    lowrank = jnp.dot(
        rows_one_all, adapter_down, precision=top_precision, preferred_element_type=jnp.float32
    )
    column_begin = model_index * head_columns
    query_up_factor = lax.dynamic_slice_in_dim(query_adapter_up, column_begin, head_columns, 1)
    value_up_factor = lax.dynamic_slice_in_dim(value_adapter_up, column_begin, head_columns, 1)
    query_vectors = projected_rows[:, :, 0] + adapter_scale * jnp.dot(
        lowrank[:, :adapter_inner_rank], query_up_factor, precision=top_precision
    ).reshape(rows_of_group, heads_here, head_size)
    rows_of_values = projected_rows[:, :, 2] + adapter_scale * jnp.dot(
        lowrank[:, adapter_inner_rank:], value_up_factor, precision=top_precision
    ).reshape(rows_of_group, heads_here, head_size)
    query_low = query_vectors.astype(jnp.bfloat16)
    key_low = projected_rows[:, :, 1].astype(jnp.bfloat16)
    value_low = rows_of_values.astype(jnp.bfloat16)
    attended_parts = []
    log_totals = []
    row_start = 0
    for length, number, offset in bucket_table():
        allowed = allowed_pairs(take_region(valid_all, row_start, length, number), length)
        attended, log_total = region_forward(
            take_region(query_low, row_start, length, number),
            take_region(key_low, row_start, length, number),
            take_region(value_low, row_start, length, number),
            allowed,
            scale,
        )
        attended_parts.append(attended.reshape(length * number, head_columns))
        log_totals.append(log_total)
        row_start = row_start + length * number
    attended_low = jnp.concatenate(attended_parts, axis=0).astype(jnp.bfloat16)
    out_flat = output_matrix.reshape(head_columns, model_width)
    attn_sum = lax.psum_scatter(
        jnp.dot(attended_low, out_flat, preferred_element_type=jnp.float32).astype(jnp.bfloat16),
        "mp",
        scatter_dimension=0,
        tiled=True,
    ).astype(jnp.float32)
    mid = inputs + attn_sum
    normed_two = layer_norm(mid, second_norm_gain).astype(jnp.bfloat16)
    grad_out = cotangent.astype(jnp.float32) * valid_here
    grad_out_low = grad_out.astype(jnp.bfloat16)
    rows_two_all = lax.all_gather(normed_two, "mp", axis=0, tiled=True)
    hidden_pre = contract_last(rows_two_all, up_matrix)
    hidden_low = gelu_tanh(hidden_pre).astype(jnp.bfloat16)
    mlp_sum = lax.psum_scatter(
        jnp.dot(hidden_low, down_matrix, preferred_element_type=jnp.float32).astype(jnp.bfloat16),
        "mp",
        scatter_dimension=0,
        tiled=True,
    ).astype(jnp.float32)
    grad_rows_two_all = lax.all_gather(grad_out_low, "mp", axis=0, tiled=True)
    grad_hidden = contract_last(grad_rows_two_all, down_matrix)
    gelu_unused, gelu_back = jax.vjp(gelu_tanh, hidden_pre)
    grad_pre_low = gelu_back(grad_hidden)[0].astype(jnp.bfloat16)
    grad_normed_two = lax.psum_scatter(
        jnp.dot(grad_pre_low, up_matrix, preferred_element_type=jnp.float32).astype(jnp.bfloat16),
        "mp",
        scatter_dimension=0,
        tiled=True,
    ).astype(jnp.float32)
    output = ((mid + mlp_sum) * valid_here).astype(jnp.bfloat16)
    norm_unused, norm_two_back = jax.vjp(lambda values: layer_norm(values, second_norm_gain), mid)
    grad_mid = grad_out + norm_two_back(grad_normed_two)[0]
    grad_mid_low = grad_mid.astype(jnp.bfloat16)
    grad_rows_one_all = lax.all_gather(grad_mid_low, "mp", axis=0, tiled=True)
    grad_attended = (
        contract_last(grad_rows_one_all, out_flat)
        .astype(jnp.bfloat16)
        .reshape(rows_of_group, heads_here, head_size)
    )
    grad_query_parts = []
    grad_key_parts = []
    grad_value_parts = []
    row_start = 0
    for (length, number, offset), log_total in zip(bucket_table(), log_totals):
        allowed = allowed_pairs(take_region(valid_all, row_start, length, number), length)
        grad_query, grad_key, grad_value = region_backward(
            take_region(query_low, row_start, length, number),
            take_region(key_low, row_start, length, number),
            take_region(value_low, row_start, length, number),
            take_region(grad_attended, row_start, length, number),
            log_total,
            allowed,
            scale,
        )
        grad_query_parts.append(grad_query.reshape(length * number, heads_here, head_size))
        grad_key_parts.append(grad_key.reshape(length * number, heads_here, head_size))
        grad_value_parts.append(grad_value.reshape(length * number, heads_here, head_size))
        row_start = row_start + length * number
    grad_query_low = jnp.concatenate(grad_query_parts, axis=0).astype(jnp.bfloat16)
    grad_key_low = jnp.concatenate(grad_key_parts, axis=0).astype(jnp.bfloat16)
    grad_value_low = jnp.concatenate(grad_value_parts, axis=0).astype(jnp.bfloat16)
    grad_query_flat = grad_query_low.reshape(rows_of_group, head_columns)
    grad_value_flat = grad_value_low.reshape(rows_of_group, head_columns)
    query_reduced_gradient = adapter_scale * jnp.dot(
        grad_query_flat,
        query_up_factor.T,
        precision=top_precision,
        preferred_element_type=jnp.float32,
    )
    value_reduced_gradient = adapter_scale * jnp.dot(
        grad_value_flat,
        value_up_factor.T,
        precision=top_precision,
        preferred_element_type=jnp.float32,
    )
    grad_lowrank = jnp.concatenate([query_reduced_gradient, value_reduced_gradient], axis=1)
    grad_qkv_low = jnp.stack([grad_query_low, grad_key_low, grad_value_low], axis=2).reshape(
        rows_of_group, heads_here * 3 * head_size
    )
    partial_rows = contract_last(grad_qkv_low, flat_qkv)
    grad_normed_one = lax.psum_scatter(
        (
            partial_rows
            + jnp.dot(
                grad_lowrank,
                adapter_down.T,
                precision=top_precision,
                preferred_element_type=jnp.float32,
            )
        ).astype(jnp.bfloat16),
        "mp",
        scatter_dimension=0,
        tiled=True,
    ).astype(jnp.float32)
    grad_a_part = lax.dot_general(
        rows_one_all,
        grad_lowrank,
        (((0,), (0,)), ((), ())),
        precision=top_precision,
        preferred_element_type=jnp.float32,
    )
    query_up_gradient_share = adapter_scale * lax.dot_general(
        lowrank[:, :adapter_inner_rank],
        grad_query_flat,
        (((0,), (0,)), ((), ())),
        precision=top_precision,
        preferred_element_type=jnp.float32,
    )
    value_up_gradient_share = adapter_scale * lax.dot_general(
        lowrank[:, adapter_inner_rank:],
        grad_value_flat,
        (((0,), (0,)), ((), ())),
        precision=top_precision,
        preferred_element_type=jnp.float32,
    )
    zero_cols = jnp.zeros((adapter_inner_rank, model_width), jnp.float32)
    grad_bq_full = lax.dynamic_update_slice_in_dim(
        zero_cols, query_up_gradient_share, column_begin, 1
    )
    grad_bv_full = lax.dynamic_update_slice_in_dim(
        zero_cols, value_up_gradient_share, column_begin, 1
    )
    grad_a_all, grad_bq_all, grad_bv_all = lax.psum(
        (grad_a_part, grad_bq_full, grad_bv_full), ("dp", "mp")
    )
    norm_unused, norm_one_back = jax.vjp(lambda values: layer_norm(values, first_norm_gain), inputs)
    input_grad = (grad_mid + norm_one_back(grad_normed_one)[0]).astype(jnp.bfloat16)
    return (
        output,
        input_grad,
        grad_a_all[:, :adapter_inner_rank],
        grad_bq_all,
        grad_a_all[:, adapter_inner_rank:],
        grad_bv_all,
    )


def solution(mesh):
    in_specs = (
        P(("dp", "mp"), None),
        P(("dp", "mp"), None),
        P(),
        P(None, "mp", None),
        P("mp", None, None),
        P(),
        P("mp", None),
        P("mp", None),
        P(),
        P(),
        P(),
        P(),
        P("dp", None),
        P("dp", None),
    )
    out_specs = (P(("dp", "mp"), None), P(("dp", "mp"), None), P(), P(), P(), P())
    whole_items = slot_begins().shape[0] // mesh.shape["mp"] == 8 * BASE_LEN and mesh.shape["dp"] == 4
    return jax.shard_map(
        whole_item_shards if whole_items else split_item_shards,
        mesh=mesh,
        in_specs=in_specs,
        out_specs=out_specs,
        check_vma=False,
    )
```

```python
import functools
import math

import jax
import jax.numpy as jnp
import numpy as np
from jax import lax
from jax.experimental import pallas as pl
from jax.experimental.pallas import tpu as pltpu
from jax.sharding import PartitionSpec as P

BASE_LEN = 128
ITEMS = 4
BLOCK = 256
VMEM_LIMIT = 62 * 1024 * 1024

norm_eps = 1e-05
adapter_scale = 8.0
top_precision = lax.Precision.HIGHEST
masked_score = -1e30
f32 = jnp.float32
bf16 = jnp.bfloat16


def bucket_table():
    return [
        (8 * BASE_LEN, ITEMS, 0),
        (4 * BASE_LEN, ITEMS, ITEMS),
        (2 * BASE_LEN, ITEMS, 2 * ITEMS),
        (BASE_LEN, 2 * ITEMS, 3 * ITEMS),
    ]


def dot_nn(a, b):
    return lax.dot_general(a, b, (((1,), (0,)), ((), ())), preferred_element_type=f32)


def dot_nt(a, b):
    return lax.dot_general(a, b, (((1,), (1,)), ((), ())), preferred_element_type=f32)


def dot_tn(a, b):
    return lax.dot_general(a, b, (((0,), (0,)), ((), ())), preferred_element_type=f32)


def split_hi_lo(v):
    hi = v.astype(bf16)
    return hi, (v - hi.astype(f32)).astype(bf16)


def whole(a):
    return pl.BlockSpec(a.shape, lambda *i: (0,) * a.ndim)


def params():
    return pltpu.CompilerParams(vmem_limit_bytes=VMEM_LIMIT)


def cost(us):
    return pl.CostEstimate(flops=int(us * 1e9), bytes_accessed=int(us * 2e6), transcendentals=0)


def slot_of(place):
    bucket = slot = inside = number = jnp.zeros_like(place)
    at = 0
    for t, (length, count, offset) in enumerate(bucket_table()):
        here = (place >= at) & (place < at + length * count)
        rel = place - at
        bucket = jnp.where(here, t, bucket)
        slot = jnp.where(here, rel // length, slot)
        inside = jnp.where(here, rel % length, inside)
        number = jnp.where(here, offset + rel // length, number)
        at += length * count
    return bucket, slot, inside, number


def prologue_kernel(at_ref, counts_ref, lengths_ref, x_ref, c_ref, gain_ref, dq_ref, dv_ref, qu_ref, vu_ref, n_ref, g_ref, lr_ref, lrs_ref, bias_ref, kaug_ref, qaug_ref, valid_ref, e_ref, et_ref):
    rows, width = x_ref.shape
    place = lax.broadcasted_iota(jnp.int32, (8, rows), 1)
    bucket, slot, inside, number = slot_of(at_ref[0] * rows + place)
    length = jnp.zeros_like(place)
    offset = 0
    for t, (_, count, offset) in enumerate(bucket_table()):
        for k in range(count):
            taken = jnp.where(k < counts_ref[0, t], lengths_ref[0, offset + k], 0)
            length = jnp.where(number == offset + k, taken, length)
    valid = jnp.where(inside < length, 1.0, 0.0).astype(f32)
    begin = place - inside
    valid_t = jnp.transpose(valid)[:, :1]
    valid_ref[...] = valid_t
    block = place // BLOCK
    row = lax.broadcasted_iota(jnp.int32, (8, rows), 0)
    first = jnp.zeros_like(place)
    for ib in range(rows // BLOCK):
        key = lax.broadcasted_iota(jnp.int32, (BLOCK, BLOCK), 0)
        query = lax.broadcasted_iota(jnp.int32, (BLOCK, BLOCK), 1)
        here = slice(ib * BLOCK, (ib + 1) * BLOCK)
        allowed = (
            (key <= query)
            & (key + ib * BLOCK >= begin[:1, here])
            & ((valid_t[here] > 0.0) | (key == query))
        )
        bias_ref[ib] = jnp.where(allowed, 0.0, masked_score).astype(f32)
        first = jnp.where(row == ib, begin[:, ib * BLOCK : ib * BLOCK + 1], first)
    own = block == row
    open_pair = own | ((place >= first) & (valid > 0.0)) | (row >= rows // BLOCK)
    zero = jnp.zeros((8, rows), f32)
    kaug_ref[...] = jnp.concatenate([jnp.where(open_pair, 0.0, masked_score), zero], axis=0).astype(bf16)
    qaug_ref[...] = jnp.concatenate([jnp.where(own, 1.0, 0.0), zero], axis=0).astype(bf16)

    @pl.loop(0, rows // BLOCK)
    def _(b):
        at = pl.ds(pl.multiple_of(b * BLOCK, BLOCK), BLOCK)
        n, _ = norm_stats(x_ref[at, :].astype(f32))
        n_ref[at, :] = (n * gain_ref[...]).astype(bf16)
        g_ref[at, :] = (c_ref[at, :].astype(f32) * valid_ref[at, :]).astype(bf16)

    hi, lo = split_hi_lo(jnp.concatenate([dq_ref[...], dv_ref[...]], axis=0))
    low = dot_nt(jnp.concatenate([hi, lo], axis=0), n_ref[...])
    hi, lo = split_hi_lo(low[:8] + low[8:])
    lr_ref[...] = jnp.concatenate([hi, lo, hi, jnp.zeros_like(hi)], axis=0)
    lrs_ref[...] = jnp.concatenate([hi, lo], axis=0)
    none = jnp.zeros((4, width), f32)
    for part, rows_of in ((0, [qu_ref[...], none]), (64, [none, vu_ref[...]])):
        hi, lo = split_hi_lo(adapter_scale * jnp.concatenate(rows_of, axis=0))
        full = jnp.concatenate([hi, hi, lo, jnp.zeros_like(hi)], axis=0).astype(f32)
        e_ref[:, part : part + 32, :] = jnp.transpose(full).astype(bf16).reshape(width // 32, 32, 32)
        pair = jnp.concatenate([hi, lo], axis=0).astype(f32)
        for p in range(width // 32):
            et_ref[p, :, part : part + 32] = pair[:, p * 32 : p * 32 + 32].astype(bf16)
    e_ref[:, 32:64, :] = jnp.zeros((width // 32, 32, 32), bf16)
    for p in range(width // 32):
        et_ref[p, :, 32:64] = jnp.zeros((16, 32), bf16)


def prologue(at, counts, lengths, x, c, gain, dq, dv, qu, vu):
    rows, width = x.shape
    smem = pl.BlockSpec(memory_space=pltpu.SMEM)
    return pl.pallas_call(
        prologue_kernel,
        in_specs=[smem, smem, smem] + [pl.BlockSpec(memory_space=pltpu.VMEM)] * 7,
        out_shape=[
            jax.ShapeDtypeStruct(shape, kind)
            for shape, kind in (
                ((rows, width), bf16),
                ((rows, width), bf16),
                ((32, rows), bf16),
                ((16, rows), bf16),
                ((rows // BLOCK, BLOCK, BLOCK), f32),
                ((16, rows), bf16),
                ((16, rows), bf16),
                ((rows, 1), f32),
                ((width // 32, 96, 32), bf16),
                ((width // 32, 16, 96), bf16),
            )
        ],
        compiler_params=params(),
        cost_estimate=cost(10),
    )(at, counts, lengths, x, c, gain, dq, dv, qu, vu)


def pipeline(number, *stages):
    held = {}
    for t in range(number + len(stages) - 1):
        for k, stage in enumerate(stages):
            unit = t - k
            if 0 <= unit < number:
                held[unit] = stage(unit, *held.pop(unit, ()))


def score_block(ka, qa, bias_ref, ib):
    s = dot_tn(ka[:, : (ib + 1) * BLOCK], qa[:, ib * BLOCK : (ib + 1) * BLOCK])
    diag = s[ib * BLOCK :] + bias_ref[ib]
    return jnp.concatenate([s[: ib * BLOCK], diag], axis=0) if ib else diag


def attn_fwd_kernel(ids_ref, n_ref, w0_ref, w1_ref, w2_ref, w3_ref, e_ref, lr_ref, kaug_ref, qaug_ref, bias_ref, *refs, first):
    qkv_ref, o_ref, lse_ref, w_ref, wo_ref, tick_ref = refs[-6:]
    tick_ref[...] = jnp.zeros_like(tick_ref)
    rows, width = n_ref.shape
    unit = first + pl.program_id(0)
    pieces = [ref[...].reshape(128, width) for ref in (w0_ref, w1_ref, w2_ref, w3_ref)]
    w = jnp.concatenate([p[:96] for p in pieces], axis=0)
    w_ref[0] = w
    wo_ref[0] = jnp.concatenate([p[96:] for p in pieces], axis=0)
    e = jnp.concatenate([e_ref[ids_ref[4 * unit + r]] for r in range(4)], axis=0)
    low = (dot_nt(w, n_ref[...]) + dot_nn(e, lr_ref[...])).astype(bf16)
    heads = []
    for h in range(2):
        a, b = h * 192, h * 192 + 96
        q = jnp.concatenate([low[a : a + 32], low[b : b + 32]], axis=0) * bf16(0.125)
        k = jnp.concatenate([low[a + 32 : a + 64], low[b + 32 : b + 64]], axis=0)
        v = jnp.concatenate([low[a + 64 : a + 96], low[b + 64 : b + 96]], axis=0)
        for t, part in enumerate((q, k, v)):
            qkv_ref[0, h * 192 + t * 64 : h * 192 + t * 64 + 64] = part
        heads.append((jnp.concatenate([q, qaug_ref[...]], axis=0), jnp.concatenate([k, kaug_ref[...]], axis=0), v))
    units = [(h, ib) for ib in range(rows // BLOCK) for h in range(2)]

    def scores(t):
        h, ib = units[t]
        return (score_block(heads[h][1], heads[h][0], bias_ref, ib),)

    def softmax(t, s):
        h, ib = units[t]
        top = jnp.max(s, axis=0, keepdims=True)
        p = jnp.exp(s - top)
        total = jnp.sum(p, axis=0, keepdims=True)
        lse_ref[0, h : h + 1, ib * BLOCK : (ib + 1) * BLOCK] = top + jnp.log(total)
        return p.astype(bf16), 1.0 / total

    def attend(t, p, share):
        h, ib = units[t]
        o = dot_nn(heads[h][2][:, : (ib + 1) * BLOCK], p) * share
        o_ref[0, h * 64 : (h + 1) * 64, ib * BLOCK : (ib + 1) * BLOCK] = o.astype(bf16)

    pipeline(len(units), scores, softmax, attend)


def attn_fwd(ids, normed, pieces, e, lr, kaug, qaug, bias, unit, number, units, kept=None, events=()):
    rows, width = normed.shape
    whole_shard = len(pieces) == 1

    def piece(r):
        if whole_shard:
            return pl.BlockSpec((1, 128, width), lambda i, ids: (ids[4 * unit + r] % 4, 0, 0))
        return pl.BlockSpec((1, 128, width), lambda i, ids: (i, 0, 0))

    def fixed(a):
        return pl.BlockSpec(a.shape, lambda i, ids: (0,) * len(a.shape))

    def placed(*shape):
        return pl.BlockSpec((1,) + shape, lambda i, ids: (unit + i,) + (0,) * len(shape))

    shapes = [((384, rows), bf16), ((128, rows), bf16), ((2, rows), f32), ((384, width), bf16), ((128, width), bf16)]
    tick = jax.ShapeDtypeStruct((8, 128), f32)
    kept = [] if kept is None else list(kept)
    *kept, tick = pl.pallas_call(
        functools.partial(attn_fwd_kernel, first=unit),
        grid_spec=pltpu.PrefetchScalarGridSpec(
            num_scalar_prefetch=1,
            grid=(number,),
            in_specs=[fixed(normed)]
            + [piece(r) for r in range(4)]
            + [fixed(e), fixed(lr), fixed(kaug), fixed(qaug), fixed(bias)]
            + [pl.BlockSpec(memory_space=pl.ANY) for _ in (*kept, *events)],
            out_specs=[placed(*shape) for shape, _ in shapes] + [fixed(tick)],
        ),
        out_shape=[jax.ShapeDtypeStruct((units,) + shape, kind) for shape, kind in shapes] + [tick],
        input_output_aliases={11 + t: t for t in range(len(kept))},
        compiler_params=params(),
        cost_estimate=cost(2 + 4 * number),
    )(ids, normed, *(pieces * 4 if whole_shard else pieces), e, lr, kaug, qaug, bias, *kept, *events)
    return kept, tick


def norm_stats(v):
    center = v - jnp.mean(v, axis=-1, keepdims=True)
    r = lax.rsqrt(jnp.mean(center * center, axis=-1, keepdims=True) + norm_eps)
    return center * r, r


def norm_back(n, r, f):
    return r * (f - jnp.mean(f, axis=-1, keepdims=True) - n * jnp.mean(f * n, axis=-1, keepdims=True))


def out_proj_kernel(o_ref, w_ref, x_ref, gain_ref, *refs):
    mid_ref, n_ref = refs[-2:]
    width = x_ref.shape[1]
    o = o_ref[...].reshape(width, BLOCK)
    w = w_ref[...].reshape(width, width)
    mid = x_ref[...].astype(f32) + dot_tn(o, w)
    n, r = norm_stats(mid)
    mid_ref[...] = mid
    n_ref[...] = (n * gain_ref[...]).astype(bf16)


def out_proj(o, w, x, gain, events=()):
    rows, width = x.shape
    shards = o.shape[0]
    blk = pl.BlockSpec((BLOCK, width), lambda i: (i, 0))
    return pl.pallas_call(
        out_proj_kernel,
        grid=(rows // BLOCK,),
        in_specs=[pl.BlockSpec((shards, 128, BLOCK), lambda i: (0, 0, i)), whole(w), blk, whole(gain)]
        + [pl.BlockSpec(memory_space=pl.ANY) for _ in events],
        out_specs=[blk, blk],
        out_shape=[jax.ShapeDtypeStruct((rows, width), f32), jax.ShapeDtypeStruct((rows, width), bf16)],
        compiler_params=params(),
        cost_estimate=cost(7),
    )(o, w, x, gain, *events)


GELU_C = math.sqrt(2.0 / math.pi)


def mlp_kernel(n_ref, g_ref, *refs, sources, resumed, events, last):
    pieces, refs = refs[:sources], refs[sources:]
    if resumed:
        mlp_in, gnt_in, refs = refs[0], refs[1], refs[2:]
    refs = refs[events:]
    fetched = []
    if last:
        mid_in, wo_in, valid_ref, gain_ref, out_ref, gmid_ref, do_ref, mlp_acc, gnt_acc, mid_ref, wo_ref = refs[:11]
        refs = refs[11:]
        fetched += [(mid_in, mid_ref), (wo_in, wo_ref)]
    else:
        mlp_acc, gnt_acc = refs[:2]
        refs = refs[2:]
    if resumed:
        mlp_was, gnt_was, sems = refs
        fetched += [(mlp_in, mlp_was), (gnt_in, gnt_was)]
    step = pl.program_id(0)
    width = n_ref.shape[1]
    copies = [pltpu.make_async_copy(src, dst, sems.at[t]) for t, (src, dst) in enumerate(fetched)]

    @pl.when(step == 0)
    def _():
        for c in copies:
            c.start()
        mlp_acc[...] = jnp.zeros_like(mlp_acc)
        gnt_acc[...] = jnp.zeros_like(gnt_acc)

    held = [ref[...].reshape(-1, 128, width) for ref in pieces]
    up = jnp.concatenate([p[:, :64].reshape(-1, width) for p in held], axis=0)
    down = jnp.concatenate([p[:, 64:].reshape(-1, width) for p in held], axis=0)
    u = dot_nt(n_ref[...], up)
    gh = dot_nt(g_ref[...], down)
    uu = u * u
    th = jnp.tanh(u * (GELU_C + (GELU_C * 0.044715) * uu))
    half = 0.5 + 0.5 * th
    hidden = u * half
    slope = half + (0.5 * u) * (1.0 - th * th) * (GELU_C + (3.0 * 0.044715 * GELU_C) * uu)
    mlp_acc[...] += dot_nn(hidden.astype(bf16), down)
    gnt_acc[...] += dot_nn((gh * slope).astype(bf16), up)

    if copies:

        @pl.when(step == pl.num_programs(0) - 1)
        def _():
            for c in copies:
                c.wait()
            if not last:
                mlp_acc[...] += mlp_was[...]
                gnt_acc[...] += gnt_was[...]
            else:
                finish_rows(
                    g_ref, valid_ref, gain_ref, out_ref, gmid_ref, do_ref, mlp_acc, gnt_acc, mid_ref, wo_ref, mlp_was, gnt_was
                )


def finish_rows(g_ref, valid_ref, gain_ref, out_ref, gmid_ref, do_ref, mlp_acc, gnt_acc, mid_ref, wo_ref, mlp_was, gnt_was):
    rows, width = g_ref.shape
    wo = wo_ref[...].reshape(width, width)

    def norm(c):
        at = slice(c * BLOCK, (c + 1) * BLOCK)
        mid = mid_ref[at, :]
        out_ref[at, :] = ((mid + (mlp_acc[at, :] + mlp_was[at, :])) * valid_ref[at, :]).astype(bf16)
        n, r = norm_stats(mid)
        grad = (gnt_acc[at, :] + gnt_was[at, :]) * gain_ref[...]
        gmid = g_ref[at, :].astype(f32) + norm_back(n, r, grad)
        gmid_ref[at, :] = gmid
        return (gmid.astype(bf16),)

    def attend(c, low):
        do_ref[:, :, c * BLOCK : (c + 1) * BLOCK] = dot_nt(wo, low).astype(bf16).reshape(do_ref.shape[0], 128, BLOCK)

    pipeline(rows // BLOCK, norm, attend)


def mlp(normed, g, pieces, steps, kept=None, final=None, events=()):
    rows, width = normed.shape
    acc = jax.ShapeDtypeStruct((rows, width), f32)
    kept = [] if kept is None else list(kept)
    total = pltpu.VMEM((rows, width), f32)

    def taken(a):
        return pl.BlockSpec((a.shape[0] // steps,) + a.shape[1:], lambda i: (i,) + (0,) * (a.ndim - 1))

    def once(a):
        return pl.BlockSpec(a.shape, lambda i: (0,) * len(a.shape), pipeline_mode=pl.Buffered(1))

    if final is None:
        extra, extra_specs, out_shape, scratch = [], [], [acc, acc], []
    else:
        mid, wo, valid, gain = extra = list(final)
        extra_specs = [pl.BlockSpec(memory_space=pl.ANY)] * 2 + [once(valid), once(gain)]
        out_shape = [
            jax.ShapeDtypeStruct((rows, width), bf16),
            acc,
            jax.ShapeDtypeStruct((wo.shape[0], 128, rows), bf16),
        ]
        scratch = [total, total, pltpu.VMEM(mid.shape, f32), pltpu.VMEM(wo.shape, bf16)]
    if kept:
        scratch += [total, total, pltpu.SemaphoreType.DMA((4,))]
    return pl.pallas_call(
        functools.partial(mlp_kernel, sources=len(pieces), resumed=bool(kept), events=len(events), last=final is not None),
        grid=(steps,),
        in_specs=[once(normed), once(g)]
        + [taken(a) for a in pieces]
        + [pl.BlockSpec(memory_space=pl.ANY) for _ in (*kept, *events)]
        + extra_specs,
        out_specs=[once(a) for a in out_shape],
        out_shape=out_shape,
        scratch_shapes=scratch,
        compiler_params=params(),
        cost_estimate=cost(4 + 5 * steps),
    )(normed, g, *pieces, *kept, *events, *extra)


def attn_bwd_kernel(ids_ref, qkv_ref, o_ref, do_ref, lse_ref, kaug_ref, qaug_ref, bias_ref, et_ref, lrs_ref, n_ref, d_ref, gl_ref, sum_ref, dk_acc, dv_acc, gb_acc):
    rows = qkv_ref.shape[2]
    step = pl.program_id(0)
    heads = []
    for h in range(2):
        q, k, v = (qkv_ref[0, h * 192 + 64 * t : h * 192 + 64 * t + 64] for t in range(3))
        heads.append((q, k, v, jnp.concatenate([q, qaug_ref[...]], axis=0), jnp.concatenate([k, kaug_ref[...]], axis=0)))
    units = [(h, ib) for h in range(2) for ib in range(rows // BLOCK)]

    def products(t):
        h, ib = units[t]
        q, k, v, qa, ka = heads[h]
        here = slice(ib * BLOCK, (ib + 1) * BLOCK)
        do, o = (ref[0, h * 64 : (h + 1) * 64, here] for ref in (do_ref, o_ref))
        inner = jnp.sum(do.astype(f32) * o.astype(f32), axis=0, keepdims=True)
        return do, inner, score_block(ka, qa, bias_ref, ib), dot_tn(v[:, : (ib + 1) * BLOCK], do)

    def scores(t, do, inner, s, dp):
        h, ib = units[t]
        p = jnp.exp(s - lse_ref[0, h : h + 1, ib * BLOCK : (ib + 1) * BLOCK])
        return do, (p * (dp - inner)).astype(bf16), p.astype(bf16)

    def grads(t, do, ds, p):
        h, ib = units[t]
        c = h * 192
        q, k = heads[h][:2]
        before, here = slice(0, ib * BLOCK), slice(ib * BLOCK, (ib + 1) * BLOCK)
        dq = (dot_nn(k[:, : (ib + 1) * BLOCK], ds) * 0.125).astype(bf16)
        d_ref[0, c : c + 32, here] = dq[:32]
        d_ref[0, c + 96 : c + 128, here] = dq[32:]
        for acc, part in ((dk_acc, dot_nt(q[:, here], ds)), (dv_acc, dot_nt(do, p))):
            if ib:
                acc[h, :, before] += part[:, before]
            acc[h, :, here] = part[:, here]

    pipeline(len(units), products, scores, grads)
    for h in range(2):
        c = h * 192
        for t, acc in ((32, dk_acc), (64, dv_acc)):
            low = acc[h].astype(bf16)
            d_ref[0, c + t : c + t + 32] = low[:32]
            d_ref[0, c + 96 + t : c + 128 + t] = low[32:]
    gl = jnp.zeros((16, rows), f32)
    for r in range(4):
        d = d_ref[0, r * 96 : r * 96 + 96]
        gl += dot_nn(et_ref[ids_ref[4 * step + r]], d)
        gb = dot_nt(lrs_ref[...], d)
        gb = adapter_scale * (gb[:8] + gb[8:])
        is_query = lax.broadcasted_iota(jnp.int32, (8, 32), 0) < 4
        gb_acc[ids_ref[4 * step + r]] = jnp.where(is_query, gb[:, :32], gb[:, 64:96])
    gl = gl[:8] + gl[8:]

    @pl.when(step == 0)
    def _():
        gl_ref[...] = gl

    @pl.when(step > 0)
    def _():
        gl_ref[...] += gl

    @pl.when(step == pl.num_programs(0) - 1)
    def _():
        hi, lo = split_hi_lo(gl_ref[...])
        sum_ref[:8] = dot_nn(hi, n_ref[...]) + dot_nn(lo, n_ref[...])
        sum_ref[8:] = jnp.concatenate([gb_acc[t] for t in range(gb_acc.shape[0])], axis=1)


def attn_bwd(ids, qkv, o, do, lse, kaug, qaug, bias, et, lrs, normed):
    shards, _, rows = qkv.shape
    width = normed.shape[1]

    def fixed(*shape):
        return pl.BlockSpec(shape, lambda i, ids: (0,) * len(shape))

    def rel(*shape):
        return pl.BlockSpec((1,) + shape, lambda i, ids: (i,) + (0,) * len(shape))

    return pl.pallas_call(
        attn_bwd_kernel,
        grid_spec=pltpu.PrefetchScalarGridSpec(
            num_scalar_prefetch=1,
            grid=(shards,),
            in_specs=[
                rel(384, rows), rel(128, rows), rel(128, rows), rel(2, rows),
                fixed(*kaug.shape), fixed(*qaug.shape), fixed(*bias.shape),
                fixed(*et.shape), fixed(*lrs.shape), fixed(*normed.shape),
            ],
            out_specs=[rel(384, rows), fixed(8, rows), fixed(16, width)],
            scratch_shapes=[pltpu.VMEM((2, 64, rows), f32)] * 2 + [pltpu.VMEM((4 * shards, 8, 32), f32)],
        ),
        out_shape=[
            jax.ShapeDtypeStruct((shards, 384, rows), bf16),
            jax.ShapeDtypeStruct((8, rows), f32),
            jax.ShapeDtypeStruct((16, width), f32),
        ],
        compiler_params=params(),
        cost_estimate=cost(35),
    )(ids, qkv, o, do, lse, kaug, qaug, bias, et, lrs, normed)


def input_grad_kernel(d_ref, w_ref, gl_ref, dn_ref, x_ref, gmid_ref, gain_ref, event_ref, out_ref):
    width = x_ref.shape[1]
    d = d_ref[...].reshape(-1, BLOCK)
    w = w_ref[...].reshape(-1, width)
    hi, lo = split_hi_lo(gl_ref[...])
    dhi, dlo = split_hi_lo(dn_ref[...])
    g = dot_tn(d, w)
    g += dot_tn(jnp.concatenate([hi, lo, hi], axis=0), jnp.concatenate([dhi, dhi, dlo], axis=0))
    n, r = norm_stats(x_ref[...].astype(f32))
    out_ref[...] = (gmid_ref[...] + norm_back(n, r, g * gain_ref[...])).astype(bf16)


def input_grad_rows(d, w, gl, down_t, x, gmid, gain, event):
    rows, width = x.shape
    shards = d.shape[0]
    blk = pl.BlockSpec((BLOCK, width), lambda i: (i, 0))
    return pl.pallas_call(
        input_grad_kernel,
        grid=(rows // BLOCK,),
        in_specs=[
            pl.BlockSpec((shards, 384, BLOCK), lambda i: (0, 0, i)),
            whole(w),
            pl.BlockSpec((8, BLOCK), lambda i: (0, i)),
            whole(down_t),
            blk, blk,
            whole(gain),
            pl.BlockSpec(memory_space=pl.ANY),
        ],
        out_specs=blk,
        out_shape=jax.ShapeDtypeStruct((rows, width), bf16),
        compiler_params=params(),
        cost_estimate=cost(13),
    )(d, w, gl, down_t, x, gmid, gain, event)


def token_valid(counts, lengths):
    pieces = []
    for bucket, (length, number, offset) in enumerate(bucket_table()):
        slot_ids = jnp.arange(number, dtype=jnp.int32)
        living = slot_ids < counts[bucket]
        places = jnp.arange(length, dtype=jnp.int32)
        inside = places[None, :] < lengths[offset : offset + number][:, None]
        pieces.append(jnp.logical_and(living[:, None], inside).reshape(-1))
    return jnp.concatenate(pieces).astype(jnp.float32)


def slot_begins():
    begins = []
    at = 0
    for length, number, _ in bucket_table():
        for _ in range(number):
            begins.append(np.full((length,), at, np.int32))
            at += length
    return np.concatenate(begins)


def unit_pieces():
    full = [(flip, slot) for flip in range(2) for slot in range(4)]
    cut = [(flip ^ k, slot) for slots in ((0, 1), (2, 3)) for flip in (4, 2, 6) for k in (0, 1) for slot in slots]
    return full + cut


def flip_send(v, axis, bits):
    return lax.ppermute(v, axis, [(i, i ^ bits) for i in range(lax.axis_size(axis))])


def flip_sum(v, axis, flips):
    return sum([flip_send(v, axis, k) for k in flips], v)


def whole_item_shards(
    tokens,
    cotangent,
    first_norm_gain,
    query_key_value_weight,
    output_matrix,
    second_norm_gain,
    up_matrix,
    down_matrix,
    query_down_factor,
    query_adapter_up,
    value_down_factor,
    value_adapter_up,
    counts,
    lengths,
):
    rows, width = tokens.shape
    heads_here = query_key_value_weight.shape[1]
    dp_size = lax.axis_size("dp")
    mp_size = lax.axis_size("mp")
    model_index = lax.axis_index("mp")
    group_index = lax.axis_index("dp")
    shards = mp_size
    qkv_own = jnp.transpose(query_key_value_weight.reshape(width, 2, 3, 2, 32), (1, 3, 2, 4, 0))
    a_own = jnp.concatenate([qkv_own.reshape(4, 96, width), output_matrix.reshape(4, 32, width)], axis=1)
    up_parts, down_parts = up_matrix.reshape(4, 2, 64, width), down_matrix.reshape(4, 2, 64, width)
    swapped = (group_index % 2) * 2 + group_index // 2
    quarter_own = jnp.where(model_index % 2 == 1, swapped, group_index)

    def b_quarter(half):
        at = (quarter_own, half, 0, 0)
        parts = [lax.dynamic_slice(a, at, (1, 1, 64, width)).reshape(1, 64, width) for a in (up_parts, down_parts)]
        return jnp.concatenate(parts, axis=1)

    def together(*arrays):
        return lax.optimization_barrier(arrays)

    def after(v, *events):
        return together(v, *events)[0]

    def stack(parts, *events):
        return jnp.concatenate(together(*parts, *events)[: len(parts)], axis=0)

    def core(v):
        return flip_send(v, "mp", 1)

    def in_plane(v, turn):
        flips = (1, 2) if turn == 0 else (2, 1)
        pairs = [(d * mp_size + i, (d ^ flips[i % 2]) * mp_size + i) for d in range(dp_size) for i in range(mp_size)]
        return lax.ppermute(v, ("dp", "mp"), pairs)

    flips, slots = (jnp.asarray(np.array(t, np.int32)) for t in zip(*unit_pieces()))
    shard_of = model_index ^ flips
    ids = shard_of * 4 + (jnp.where(shard_of % 2 == 1, swapped, group_index) ^ slots)

    gain_one = first_norm_gain[None, :]
    gain_two = second_norm_gain[None, :]
    down_q, down_v = query_down_factor.T, value_down_factor.T
    down_t = jnp.concatenate([down_q, down_v], axis=0)
    normed, grad_out_low, lr, lrs, bias, kaug, qaug, valid_col, e, et = prologue(
        model_index.reshape(1).astype(jnp.int32),
        counts,
        lengths,
        tokens,
        cotangent,
        gain_one,
        down_q,
        down_v,
        query_adapter_up,
        value_adapter_up,
    )
    def z_near(v):
        return flip_send(v, "mp", 2)

    def z_far(v):
        return flip_send(v, "mp", 4)

    def heads(pieces, unit, number, kept=None, events=()):
        return attn_fwd(ids, normed, pieces, e, lr, kaug, qaug, bias, unit, number, shards, kept, events)

    a_mine = lax.dynamic_slice_in_dim(a_own, quarter_own, 1, 0)
    a_f = z_far(a_mine)
    a_n = z_near(a_mine)
    a_core = core(a_own)
    kept, tick = heads([a_own], 0, 1)
    a_f, tick = together(a_f, tick)
    a_fn = z_near(a_f)
    kept, tick = heads([a_core], 1, 1, kept, (a_f,))
    a_n, a_fn, tick = together(a_n, a_fn, tick)
    b_mine, c_mine = b_quarter(0), b_quarter(1)
    a_s = stack([a_f, a_n, a_fn], tick)
    a_x = in_plane(a_s, 0)
    a_sc = core(a_s)
    b_f = z_far(after(b_mine, a_s))
    b_own = jnp.concatenate([after(up_parts, a_s), down_parts], axis=2)
    a_x, a_sc, b_f, b_own, c_mine, tick = together(a_x, a_sc, b_f, b_own, c_mine, tick)
    a_xc = core(a_x)
    a_y, a_d = in_plane(a_s, 1), in_plane(a_x, 1)
    b_n = z_near(stack([b_mine, b_f], tick))
    c_f = z_far(after(c_mine, a_x))
    kept, tick = heads([a_s, a_x, a_sc, a_xc], 2, 3, kept)
    a_y, a_d, b_n, c_f, tick = together(a_y, a_d, b_n, c_f, tick)
    a_yc, a_dc = core(a_y), core(a_d)
    b_s = stack([b_f, b_n], tick)
    b_x = in_plane(b_s, 0)
    c_n = z_near(stack([c_mine, c_f], tick))
    b_core = core(after(b_own, tick))
    kept, tick = heads([a_y, a_d, a_yc, a_dc], 5, 3, kept, (b_s,))
    b_x, c_n, b_core, tick = together(b_x, c_n, b_core, tick)
    qkv, attended, lse, w_all, wo_all = kept
    b_y, b_d = in_plane(after(b_s, tick), 1), in_plane(b_x, 1)
    b_xc = core(b_x)
    c_s = stack([c_f, c_n], tick)
    c_x = in_plane(c_s, 0)
    mid, normed_two = out_proj(attended, wo_all, tokens, gain_two, (c_s,))
    b_sc = core(after(b_s, normed_two))
    sums = mlp(normed_two, grad_out_low, [b_own.reshape(8, 128, width), b_core.reshape(8, 128, width)], 2)
    b_y, b_d, b_xc, b_sc, c_x, *sums = together(b_y, b_d, b_xc, b_sc, c_x, *sums)
    b_yc, b_dc = core(b_y), core(b_d)
    c_y, c_d = in_plane(after(c_s, sums[0]), 1), in_plane(c_x, 1)
    c_xc = core(c_x)
    sums = mlp(normed_two, grad_out_low, [b_s, b_x, b_y, b_d, b_sc, b_xc, b_yc, b_dc], 3, sums)
    c_y, c_d, c_xc, *sums = together(c_y, c_d, c_xc, *sums)
    c_sc, c_yc, c_dc = core(after(c_s, sums[0])), core(c_y), core(c_d)
    output, grad_mid, grad_attended = mlp(
        normed_two,
        grad_out_low,
        [c_s, c_x, c_y, c_d, c_sc, c_xc, c_yc, c_dc],
        3,
        sums,
        (mid, wo_all, valid_col, gain_two),
    )
    d, gl, packed = attn_bwd(ids, qkv, attended, grad_attended, lse, kaug, qaug, bias, et, lrs, normed)
    packed = flip_sum(packed, "mp", (1,))
    packed = flip_sum(packed, "mp", (2, 4, 6))
    event = packed
    packed = flip_sum(packed, "dp", tuple(range(1, dp_size)))
    input_grad = input_grad_rows(d, w_all, gl, down_t, tokens, grad_mid, gain_one, event)
    return (
        output,
        input_grad,
        packed[0:4].T,
        packed[8:12],
        packed[4:8].T,
        packed[12:16],
    )


def layer_norm(values, norm_gain):
    center = values - jnp.mean(values, axis=-1, keepdims=True)
    spread = jnp.mean(center * center, axis=-1, keepdims=True)
    return center * lax.rsqrt(spread + norm_eps) * norm_gain


def gelu_tanh(values):
    return jax.nn.gelu(values, approximate=True)


def contract_last(left, right):
    return lax.dot_general(
        left, right, (((1,), (1,)), ((), ())), preferred_element_type=jnp.float32
    )


def take_region(array, row_start, length, number):
    region = lax.slice_in_dim(array, row_start, row_start + length * number)
    return region.reshape((number, length) + array.shape[1:])


def allowed_pairs(valid_rows, length):
    places = jnp.arange(length, dtype=jnp.int32)
    causal = places[:, None] >= places[None, :]
    diagonal = places[:, None] == places[None, :]
    return jnp.logical_and(
        causal[None], jnp.logical_or(valid_rows[:, None, :] > 0.0, diagonal[None])
    )


def masked_scores(query_blk, key_blk, allowed, scale):
    scores = (
        jnp.einsum("nqhd,nkhd->nhqk", query_blk, key_blk, preferred_element_type=jnp.float32)
        * scale
    )
    return jnp.where(allowed[:, None], scores, masked_score)


def region_forward(query_blk, key_blk, value_blk, allowed, scale):
    scores = masked_scores(query_blk, key_blk, allowed, scale)
    row_max = jnp.max(scores, axis=-1, keepdims=True)
    raised = jnp.exp(scores - row_max)
    running = jnp.sum(raised, axis=-1, keepdims=True)
    probs_low = (raised / running).astype(jnp.bfloat16)
    attended = jnp.einsum(
        "nhqk,nkhd->nqhd", probs_low, value_blk, preferred_element_type=jnp.float32
    )
    return (attended, row_max + jnp.log(running))


def region_backward(query_blk, key_blk, value_blk, grad_blk, log_total, allowed, scale):
    scores = masked_scores(query_blk, key_blk, allowed, scale)
    probs = jnp.exp(scores - log_total)
    probs_low = probs.astype(jnp.bfloat16)
    grad_probs = jnp.einsum(
        "nqhd,nkhd->nhqk", grad_blk, value_blk, preferred_element_type=jnp.float32
    )
    inner = jnp.sum(grad_probs * probs, axis=-1, keepdims=True)
    grad_scores = (probs * (grad_probs - inner)).astype(jnp.bfloat16)
    grad_query = (
        jnp.einsum("nhqk,nkhd->nqhd", grad_scores, key_blk, preferred_element_type=jnp.float32)
        * scale
    )
    grad_key = (
        jnp.einsum("nhqk,nqhd->nkhd", grad_scores, query_blk, preferred_element_type=jnp.float32)
        * scale
    )
    grad_value = jnp.einsum(
        "nhqk,nqhd->nkhd", probs_low, grad_blk, preferred_element_type=jnp.float32
    )
    return (grad_query, grad_key, grad_value)


def split_item_shards(
    tokens,
    cotangent,
    first_norm_gain,
    query_key_value_weight,
    output_matrix,
    second_norm_gain,
    up_matrix,
    down_matrix,
    query_down_factor,
    query_adapter_up,
    value_down_factor,
    value_adapter_up,
    counts,
    lengths,
):
    local_rows = tokens.shape[0]
    model_width = tokens.shape[1]
    model_index = lax.axis_index("mp")
    heads_here = query_key_value_weight.shape[1]
    head_size = query_key_value_weight.shape[2] // 3
    head_columns = heads_here * head_size
    adapter_inner_rank = query_down_factor.shape[1]
    scale = 1.0 / math.sqrt(head_size)
    valid_all = token_valid(counts[0], lengths[0])
    rows_of_group = valid_all.shape[0]
    valid_here = lax.dynamic_slice_in_dim(valid_all, model_index * local_rows, local_rows)[:, None]
    adapter_down = jnp.concatenate([query_down_factor, value_down_factor], axis=1)
    inputs = tokens.astype(jnp.float32)
    first_normed = layer_norm(inputs, first_norm_gain).astype(jnp.bfloat16)
    rows_one_all = lax.all_gather(first_normed, "mp", axis=0, tiled=True)
    flat_qkv = query_key_value_weight.reshape(model_width, heads_here * 3 * head_size)
    projected_rows = jnp.dot(rows_one_all, flat_qkv, preferred_element_type=jnp.float32).reshape(
        rows_of_group, heads_here, 3, head_size
    )
    lowrank = jnp.dot(
        rows_one_all, adapter_down, precision=top_precision, preferred_element_type=jnp.float32
    )
    column_begin = model_index * head_columns
    query_up_factor = lax.dynamic_slice_in_dim(query_adapter_up, column_begin, head_columns, 1)
    value_up_factor = lax.dynamic_slice_in_dim(value_adapter_up, column_begin, head_columns, 1)
    query_vectors = projected_rows[:, :, 0] + adapter_scale * jnp.dot(
        lowrank[:, :adapter_inner_rank], query_up_factor, precision=top_precision
    ).reshape(rows_of_group, heads_here, head_size)
    rows_of_values = projected_rows[:, :, 2] + adapter_scale * jnp.dot(
        lowrank[:, adapter_inner_rank:], value_up_factor, precision=top_precision
    ).reshape(rows_of_group, heads_here, head_size)
    query_low = query_vectors.astype(jnp.bfloat16)
    key_low = projected_rows[:, :, 1].astype(jnp.bfloat16)
    value_low = rows_of_values.astype(jnp.bfloat16)
    attended_parts = []
    log_totals = []
    row_start = 0
    for length, number, offset in bucket_table():
        allowed = allowed_pairs(take_region(valid_all, row_start, length, number), length)
        attended, log_total = region_forward(
            take_region(query_low, row_start, length, number),
            take_region(key_low, row_start, length, number),
            take_region(value_low, row_start, length, number),
            allowed,
            scale,
        )
        attended_parts.append(attended.reshape(length * number, head_columns))
        log_totals.append(log_total)
        row_start = row_start + length * number
    attended_low = jnp.concatenate(attended_parts, axis=0).astype(jnp.bfloat16)
    out_flat = output_matrix.reshape(head_columns, model_width)
    attn_sum = lax.psum_scatter(
        jnp.dot(attended_low, out_flat, preferred_element_type=jnp.float32).astype(jnp.bfloat16),
        "mp",
        scatter_dimension=0,
        tiled=True,
    ).astype(jnp.float32)
    mid = inputs + attn_sum
    normed_two = layer_norm(mid, second_norm_gain).astype(jnp.bfloat16)
    grad_out = cotangent.astype(jnp.float32) * valid_here
    grad_out_low = grad_out.astype(jnp.bfloat16)
    rows_two_all = lax.all_gather(normed_two, "mp", axis=0, tiled=True)
    hidden_pre = contract_last(rows_two_all, up_matrix)
    hidden_low = gelu_tanh(hidden_pre).astype(jnp.bfloat16)
    mlp_sum = lax.psum_scatter(
        jnp.dot(hidden_low, down_matrix, preferred_element_type=jnp.float32).astype(jnp.bfloat16),
        "mp",
        scatter_dimension=0,
        tiled=True,
    ).astype(jnp.float32)
    grad_rows_two_all = lax.all_gather(grad_out_low, "mp", axis=0, tiled=True)
    grad_hidden = contract_last(grad_rows_two_all, down_matrix)
    gelu_unused, gelu_back = jax.vjp(gelu_tanh, hidden_pre)
    grad_pre_low = gelu_back(grad_hidden)[0].astype(jnp.bfloat16)
    grad_normed_two = lax.psum_scatter(
        jnp.dot(grad_pre_low, up_matrix, preferred_element_type=jnp.float32).astype(jnp.bfloat16),
        "mp",
        scatter_dimension=0,
        tiled=True,
    ).astype(jnp.float32)
    output = ((mid + mlp_sum) * valid_here).astype(jnp.bfloat16)
    norm_unused, norm_two_back = jax.vjp(lambda values: layer_norm(values, second_norm_gain), mid)
    grad_mid = grad_out + norm_two_back(grad_normed_two)[0]
    grad_mid_low = grad_mid.astype(jnp.bfloat16)
    grad_rows_one_all = lax.all_gather(grad_mid_low, "mp", axis=0, tiled=True)
    grad_attended = (
        contract_last(grad_rows_one_all, out_flat)
        .astype(jnp.bfloat16)
        .reshape(rows_of_group, heads_here, head_size)
    )
    grad_query_parts = []
    grad_key_parts = []
    grad_value_parts = []
    row_start = 0
    for (length, number, offset), log_total in zip(bucket_table(), log_totals):
        allowed = allowed_pairs(take_region(valid_all, row_start, length, number), length)
        grad_query, grad_key, grad_value = region_backward(
            take_region(query_low, row_start, length, number),
            take_region(key_low, row_start, length, number),
            take_region(value_low, row_start, length, number),
            take_region(grad_attended, row_start, length, number),
            log_total,
            allowed,
            scale,
        )
        grad_query_parts.append(grad_query.reshape(length * number, heads_here, head_size))
        grad_key_parts.append(grad_key.reshape(length * number, heads_here, head_size))
        grad_value_parts.append(grad_value.reshape(length * number, heads_here, head_size))
        row_start = row_start + length * number
    grad_query_low = jnp.concatenate(grad_query_parts, axis=0).astype(jnp.bfloat16)
    grad_key_low = jnp.concatenate(grad_key_parts, axis=0).astype(jnp.bfloat16)
    grad_value_low = jnp.concatenate(grad_value_parts, axis=0).astype(jnp.bfloat16)
    grad_query_flat = grad_query_low.reshape(rows_of_group, head_columns)
    grad_value_flat = grad_value_low.reshape(rows_of_group, head_columns)
    query_reduced_gradient = adapter_scale * jnp.dot(
        grad_query_flat,
        query_up_factor.T,
        precision=top_precision,
        preferred_element_type=jnp.float32,
    )
    value_reduced_gradient = adapter_scale * jnp.dot(
        grad_value_flat,
        value_up_factor.T,
        precision=top_precision,
        preferred_element_type=jnp.float32,
    )
    grad_lowrank = jnp.concatenate([query_reduced_gradient, value_reduced_gradient], axis=1)
    grad_qkv_low = jnp.stack([grad_query_low, grad_key_low, grad_value_low], axis=2).reshape(
        rows_of_group, heads_here * 3 * head_size
    )
    partial_rows = contract_last(grad_qkv_low, flat_qkv)
    grad_normed_one = lax.psum_scatter(
        (
            partial_rows
            + jnp.dot(
                grad_lowrank,
                adapter_down.T,
                precision=top_precision,
                preferred_element_type=jnp.float32,
            )
        ).astype(jnp.bfloat16),
        "mp",
        scatter_dimension=0,
        tiled=True,
    ).astype(jnp.float32)
    grad_a_part = lax.dot_general(
        rows_one_all,
        grad_lowrank,
        (((0,), (0,)), ((), ())),
        precision=top_precision,
        preferred_element_type=jnp.float32,
    )
    query_up_gradient_share = adapter_scale * lax.dot_general(
        lowrank[:, :adapter_inner_rank],
        grad_query_flat,
        (((0,), (0,)), ((), ())),
        precision=top_precision,
        preferred_element_type=jnp.float32,
    )
    value_up_gradient_share = adapter_scale * lax.dot_general(
        lowrank[:, adapter_inner_rank:],
        grad_value_flat,
        (((0,), (0,)), ((), ())),
        precision=top_precision,
        preferred_element_type=jnp.float32,
    )
    zero_cols = jnp.zeros((adapter_inner_rank, model_width), jnp.float32)
    grad_bq_full = lax.dynamic_update_slice_in_dim(
        zero_cols, query_up_gradient_share, column_begin, 1
    )
    grad_bv_full = lax.dynamic_update_slice_in_dim(
        zero_cols, value_up_gradient_share, column_begin, 1
    )
    grad_a_all, grad_bq_all, grad_bv_all = lax.psum(
        (grad_a_part, grad_bq_full, grad_bv_full), ("dp", "mp")
    )
    norm_unused, norm_one_back = jax.vjp(lambda values: layer_norm(values, first_norm_gain), inputs)
    input_grad = (grad_mid + norm_one_back(grad_normed_one)[0]).astype(jnp.bfloat16)
    return (
        output,
        input_grad,
        grad_a_all[:, :adapter_inner_rank],
        grad_bq_all,
        grad_a_all[:, adapter_inner_rank:],
        grad_bv_all,
    )


def solution(mesh):
    in_specs = (
        P(("dp", "mp"), None),
        P(("dp", "mp"), None),
        P(),
        P(None, "mp", None),
        P("mp", None, None),
        P(),
        P("mp", None),
        P("mp", None),
        P(),
        P(),
        P(),
        P(),
        P("dp", None),
        P("dp", None),
    )
    out_specs = (P(("dp", "mp"), None), P(("dp", "mp"), None), P(), P(), P(), P())
    whole_items = slot_begins().shape[0] // mesh.shape["mp"] == 8 * BASE_LEN and mesh.shape["dp"] == 4
    return jax.shard_map(
        whole_item_shards if whole_items else split_item_shards,
        mesh=mesh,
        in_specs=in_specs,
        out_specs=out_specs,
        check_vma=False,
    )
```

```python
import functools
import math

import jax
import jax.numpy as jnp
import numpy as np
from jax import lax
from jax.experimental import pallas as pl
from jax.experimental.pallas import tpu as pltpu
from jax.sharding import PartitionSpec as P

BASE_LEN = 128
ITEMS = 4
BLOCK = 256
VMEM_LIMIT = 62 * 1024 * 1024

norm_eps = 1e-05
adapter_scale = 8.0
top_precision = lax.Precision.HIGHEST
masked_score = -1e30
f32 = jnp.float32
bf16 = jnp.bfloat16


def bucket_table():
    return [
        (8 * BASE_LEN, ITEMS, 0),
        (4 * BASE_LEN, ITEMS, ITEMS),
        (2 * BASE_LEN, ITEMS, 2 * ITEMS),
        (BASE_LEN, 2 * ITEMS, 3 * ITEMS),
    ]


def dot_nn(a, b):
    return lax.dot_general(a, b, (((1,), (0,)), ((), ())), preferred_element_type=f32)


def dot_nt(a, b):
    return lax.dot_general(a, b, (((1,), (1,)), ((), ())), preferred_element_type=f32)


def dot_tn(a, b):
    return lax.dot_general(a, b, (((0,), (0,)), ((), ())), preferred_element_type=f32)


def split_hi_lo(v):
    hi = v.astype(bf16)
    return hi, (v - hi.astype(f32)).astype(bf16)


def whole(a):
    return pl.BlockSpec(a.shape, lambda *i: (0,) * a.ndim)


def params():
    return pltpu.CompilerParams(vmem_limit_bytes=VMEM_LIMIT)


def cost(us):
    return pl.CostEstimate(flops=int(us * 1e9), bytes_accessed=int(us * 2e6), transcendentals=0)


def slot_of(place):
    bucket = slot = inside = number = jnp.zeros_like(place)
    at = 0
    for t, (length, count, offset) in enumerate(bucket_table()):
        here = (place >= at) & (place < at + length * count)
        rel = place - at
        bucket = jnp.where(here, t, bucket)
        slot = jnp.where(here, rel // length, slot)
        inside = jnp.where(here, rel % length, inside)
        number = jnp.where(here, offset + rel // length, number)
        at += length * count
    return bucket, slot, inside, number


def prologue_kernel(at_ref, counts_ref, lengths_ref, x_ref, c_ref, gain_ref, dq_ref, dv_ref, qu_ref, vu_ref, n_ref, g_ref, lr_ref, lrs_ref, bias_ref, kaug_ref, qaug_ref, valid_ref, e_ref, et_ref):
    rows, width = x_ref.shape
    place = lax.broadcasted_iota(jnp.int32, (8, rows), 1)
    bucket, slot, inside, number = slot_of(at_ref[0] * rows + place)
    length = jnp.zeros_like(place)
    offset = 0
    for t, (_, count, offset) in enumerate(bucket_table()):
        for k in range(count):
            taken = jnp.where(k < counts_ref[0, t], lengths_ref[0, offset + k], 0)
            length = jnp.where(number == offset + k, taken, length)
    valid = jnp.where(inside < length, 1.0, 0.0).astype(f32)
    begin = place - inside
    valid_t = jnp.transpose(valid)[:, :1]
    valid_ref[...] = valid_t
    block = place // BLOCK
    row = lax.broadcasted_iota(jnp.int32, (8, rows), 0)
    first = jnp.zeros_like(place)
    for ib in range(rows // BLOCK):
        key = lax.broadcasted_iota(jnp.int32, (BLOCK, BLOCK), 0)
        query = lax.broadcasted_iota(jnp.int32, (BLOCK, BLOCK), 1)
        here = slice(ib * BLOCK, (ib + 1) * BLOCK)
        allowed = (
            (key <= query)
            & (key + ib * BLOCK >= begin[:1, here])
            & ((valid_t[here] > 0.0) | (key == query))
        )
        bias_ref[ib] = jnp.where(allowed, 0.0, masked_score).astype(f32)
        first = jnp.where(row == ib, begin[:, ib * BLOCK : ib * BLOCK + 1], first)
    own = block == row
    open_pair = own | ((place >= first) & (valid > 0.0)) | (row >= rows // BLOCK)
    zero = jnp.zeros((8, rows), f32)
    kaug_ref[...] = jnp.concatenate([jnp.where(open_pair, 0.0, masked_score), zero], axis=0).astype(bf16)
    qaug_ref[...] = jnp.concatenate([jnp.where(own, 1.0, 0.0), zero], axis=0).astype(bf16)

    @pl.loop(0, rows // BLOCK)
    def _(b):
        at = pl.ds(pl.multiple_of(b * BLOCK, BLOCK), BLOCK)
        n, _ = norm_stats(x_ref[at, :].astype(f32))
        n_ref[at, :] = (n * gain_ref[...]).astype(bf16)
        g_ref[at, :] = (c_ref[at, :].astype(f32) * valid_ref[at, :]).astype(bf16)

    hi, lo = split_hi_lo(jnp.concatenate([dq_ref[...], dv_ref[...]], axis=0))
    low = dot_nt(jnp.concatenate([hi, lo], axis=0), n_ref[...])
    hi, lo = split_hi_lo(low[:8] + low[8:])
    lr_ref[...] = jnp.concatenate([hi, lo, hi, jnp.zeros_like(hi)], axis=0)
    lrs_ref[...] = jnp.concatenate([hi, lo], axis=0)
    none = jnp.zeros((4, width), f32)
    for part, rows_of in ((0, [qu_ref[...], none]), (64, [none, vu_ref[...]])):
        hi, lo = split_hi_lo(adapter_scale * jnp.concatenate(rows_of, axis=0))
        full = jnp.concatenate([hi, hi, lo, jnp.zeros_like(hi)], axis=0).astype(f32)
        e_ref[:, part : part + 32, :] = jnp.transpose(full).astype(bf16).reshape(width // 32, 32, 32)
        pair = jnp.concatenate([hi, lo], axis=0).astype(f32)
        for p in range(width // 32):
            et_ref[p, :, part : part + 32] = pair[:, p * 32 : p * 32 + 32].astype(bf16)
    e_ref[:, 32:64, :] = jnp.zeros((width // 32, 32, 32), bf16)
    for p in range(width // 32):
        et_ref[p, :, 32:64] = jnp.zeros((16, 32), bf16)


def prologue(at, counts, lengths, x, c, gain, dq, dv, qu, vu):
    rows, width = x.shape
    smem = pl.BlockSpec(memory_space=pltpu.SMEM)
    return pl.pallas_call(
        prologue_kernel,
        in_specs=[smem, smem, smem] + [pl.BlockSpec(memory_space=pltpu.VMEM)] * 7,
        out_shape=[
            jax.ShapeDtypeStruct(shape, kind)
            for shape, kind in (
                ((rows, width), bf16),
                ((rows, width), bf16),
                ((32, rows), bf16),
                ((16, rows), bf16),
                ((rows // BLOCK, BLOCK, BLOCK), f32),
                ((16, rows), bf16),
                ((16, rows), bf16),
                ((rows, 1), f32),
                ((width // 32, 96, 32), bf16),
                ((width // 32, 16, 96), bf16),
            )
        ],
        compiler_params=params(),
        cost_estimate=cost(10),
    )(at, counts, lengths, x, c, gain, dq, dv, qu, vu)


def pipeline(number, *stages):
    held = {}
    for t in range(number + len(stages) - 1):
        for k, stage in enumerate(stages):
            unit = t - k
            if 0 <= unit < number:
                held[unit] = stage(unit, *held.pop(unit, ()))


def score_block(ka, qa, bias_ref, ib):
    s = dot_tn(ka[:, : (ib + 1) * BLOCK], qa[:, ib * BLOCK : (ib + 1) * BLOCK])
    diag = s[ib * BLOCK :] + bias_ref[ib]
    return jnp.concatenate([s[: ib * BLOCK], diag], axis=0) if ib else diag


def attn_fwd_kernel(ids_ref, n_ref, w0_ref, w1_ref, w2_ref, w3_ref, e_ref, lr_ref, kaug_ref, qaug_ref, bias_ref, *refs, first):
    qkv_ref, o_ref, lse_ref, w_ref, wo_ref = refs[-5:]
    rows, width = n_ref.shape
    unit = first + pl.program_id(0)
    pieces = [ref[...].reshape(128, width) for ref in (w0_ref, w1_ref, w2_ref, w3_ref)]
    w = jnp.concatenate([p[:96] for p in pieces], axis=0)
    w_ref[0] = w
    wo_ref[0] = jnp.concatenate([p[96:] for p in pieces], axis=0)
    e = jnp.concatenate([e_ref[ids_ref[4 * unit + r]] for r in range(4)], axis=0)
    low = (dot_nt(w, n_ref[...]) + dot_nn(e, lr_ref[...])).astype(bf16)
    heads = []
    for h in range(2):
        a, b = h * 192, h * 192 + 96
        q = jnp.concatenate([low[a : a + 32], low[b : b + 32]], axis=0) * bf16(0.125)
        k = jnp.concatenate([low[a + 32 : a + 64], low[b + 32 : b + 64]], axis=0)
        v = jnp.concatenate([low[a + 64 : a + 96], low[b + 64 : b + 96]], axis=0)
        for t, part in enumerate((q, k, v)):
            qkv_ref[0, h * 192 + t * 64 : h * 192 + t * 64 + 64] = part
        heads.append((jnp.concatenate([q, qaug_ref[...]], axis=0), jnp.concatenate([k, kaug_ref[...]], axis=0), v))
    units = [(h, ib) for ib in range(rows // BLOCK) for h in range(2)]

    def scores(t):
        h, ib = units[t]
        return (score_block(heads[h][1], heads[h][0], bias_ref, ib),)

    def softmax(t, s):
        h, ib = units[t]
        top = jnp.max(s, axis=0, keepdims=True)
        p = jnp.exp(s - top)
        total = jnp.sum(p, axis=0, keepdims=True)
        lse_ref[0, h : h + 1, ib * BLOCK : (ib + 1) * BLOCK] = top + jnp.log(total)
        return p.astype(bf16), 1.0 / total

    def attend(t, p, share):
        h, ib = units[t]
        o = dot_nn(heads[h][2][:, : (ib + 1) * BLOCK], p) * share
        o_ref[0, h * 64 : (h + 1) * 64, ib * BLOCK : (ib + 1) * BLOCK] = o.astype(bf16)

    pipeline(len(units), scores, softmax, attend)


def attn_fwd(ids, normed, pieces, e, lr, kaug, qaug, bias, unit, number, units, kept=None, events=()):
    rows, width = normed.shape
    whole_shard = len(pieces) == 1

    def piece(r):
        if whole_shard:
            return pl.BlockSpec((1, 128, width), lambda i, ids: (ids[4 * unit + r] % 4, 0, 0))
        return pl.BlockSpec((1, 128, width), lambda i, ids: (i, 0, 0))

    def fixed(a):
        return pl.BlockSpec(a.shape, lambda i, ids: (0,) * len(a.shape))

    def placed(*shape):
        return pl.BlockSpec((1,) + shape, lambda i, ids: (unit + i,) + (0,) * len(shape))

    shapes = [((384, rows), bf16), ((128, rows), bf16), ((2, rows), f32), ((384, width), bf16), ((128, width), bf16)]
    kept = [] if kept is None else list(kept)
    return pl.pallas_call(
        functools.partial(attn_fwd_kernel, first=unit),
        grid_spec=pltpu.PrefetchScalarGridSpec(
            num_scalar_prefetch=1,
            grid=(number,),
            in_specs=[fixed(normed)]
            + [piece(r) for r in range(4)]
            + [fixed(e), fixed(lr), fixed(kaug), fixed(qaug), fixed(bias)]
            + [pl.BlockSpec(memory_space=pl.ANY) for _ in (*kept, *events)],
            out_specs=[placed(*shape) for shape, _ in shapes],
        ),
        out_shape=[jax.ShapeDtypeStruct((units,) + shape, kind) for shape, kind in shapes],
        input_output_aliases={11 + t: t for t in range(len(kept))},
        compiler_params=params(),
        cost_estimate=cost(2 + 4 * number),
    )(ids, normed, *(pieces * 4 if whole_shard else pieces), e, lr, kaug, qaug, bias, *kept, *events)


def stack_kernel(*refs):
    out_ref = refs[-1]
    at = 0
    for ref in refs[:-1]:
        out_ref[at : at + ref.shape[0]] = ref[...]
        at += ref.shape[0]


def stack_now(*parts):
    out = jax.ShapeDtypeStruct((sum(a.shape[0] for a in parts),) + parts[0].shape[1:], parts[0].dtype)
    return pl.pallas_call(stack_kernel, out_shape=out, compiler_params=params(), cost_estimate=cost(1))(*parts)


def norm_stats(v):
    center = v - jnp.mean(v, axis=-1, keepdims=True)
    r = lax.rsqrt(jnp.mean(center * center, axis=-1, keepdims=True) + norm_eps)
    return center * r, r


def norm_back(n, r, f):
    return r * (f - jnp.mean(f, axis=-1, keepdims=True) - n * jnp.mean(f * n, axis=-1, keepdims=True))


def out_proj_kernel(o_ref, w_ref, x_ref, gain_ref, *refs):
    mid_ref, n_ref = refs[-2:]
    width = x_ref.shape[1]
    o = o_ref[...].reshape(width, BLOCK)
    w = w_ref[...].reshape(width, width)
    mid = x_ref[...].astype(f32) + dot_tn(o, w)
    n, r = norm_stats(mid)
    mid_ref[...] = mid
    n_ref[...] = (n * gain_ref[...]).astype(bf16)


def out_proj(o, w, x, gain, events=()):
    rows, width = x.shape
    shards = o.shape[0]
    blk = pl.BlockSpec((BLOCK, width), lambda i: (i, 0))
    return pl.pallas_call(
        out_proj_kernel,
        grid=(rows // BLOCK,),
        in_specs=[pl.BlockSpec((shards, 128, BLOCK), lambda i: (0, 0, i)), whole(w), blk, whole(gain)]
        + [pl.BlockSpec(memory_space=pl.ANY) for _ in events],
        out_specs=[blk, blk],
        out_shape=[jax.ShapeDtypeStruct((rows, width), f32), jax.ShapeDtypeStruct((rows, width), bf16)],
        compiler_params=params(),
        cost_estimate=cost(7),
    )(o, w, x, gain, *events)


GELU_C = math.sqrt(2.0 / math.pi)


def mlp_kernel(n_ref, g_ref, *refs, sources, resumed, events, last):
    pieces, refs = refs[:sources], refs[sources:]
    if resumed:
        mlp_in, gnt_in, refs = refs[0], refs[1], refs[2:]
    refs = refs[events:]
    fetched = []
    if last:
        mid_in, wo_in, valid_ref, gain_ref, out_ref, gmid_ref, do_ref, mlp_acc, gnt_acc, mid_ref, wo_ref = refs[:11]
        refs = refs[11:]
        fetched += [(mid_in, mid_ref), (wo_in, wo_ref)]
    else:
        mlp_acc, gnt_acc = refs[:2]
        refs = refs[2:]
    if resumed:
        mlp_was, gnt_was, sems = refs
        fetched += [(mlp_in, mlp_was), (gnt_in, gnt_was)]
    step = pl.program_id(0)
    width = n_ref.shape[1]
    copies = [pltpu.make_async_copy(src, dst, sems.at[t]) for t, (src, dst) in enumerate(fetched)]

    @pl.when(step == 0)
    def _():
        for c in copies:
            c.start()
        mlp_acc[...] = jnp.zeros_like(mlp_acc)
        gnt_acc[...] = jnp.zeros_like(gnt_acc)

    held = [ref[...].reshape(-1, 128, width) for ref in pieces]
    up = jnp.concatenate([p[:, :64].reshape(-1, width) for p in held], axis=0)
    down = jnp.concatenate([p[:, 64:].reshape(-1, width) for p in held], axis=0)
    u = dot_nt(n_ref[...], up)
    gh = dot_nt(g_ref[...], down)
    uu = u * u
    th = jnp.tanh(u * (GELU_C + (GELU_C * 0.044715) * uu))
    half = 0.5 + 0.5 * th
    hidden = u * half
    slope = half + (0.5 * u) * (1.0 - th * th) * (GELU_C + (3.0 * 0.044715 * GELU_C) * uu)
    mlp_acc[...] += dot_nn(hidden.astype(bf16), down)
    gnt_acc[...] += dot_nn((gh * slope).astype(bf16), up)

    if copies:

        @pl.when(step == pl.num_programs(0) - 1)
        def _():
            for c in copies:
                c.wait()
            if not last:
                mlp_acc[...] += mlp_was[...]
                gnt_acc[...] += gnt_was[...]
            else:
                finish_rows(
                    g_ref, valid_ref, gain_ref, out_ref, gmid_ref, do_ref, mlp_acc, gnt_acc, mid_ref, wo_ref, mlp_was, gnt_was
                )


def finish_rows(g_ref, valid_ref, gain_ref, out_ref, gmid_ref, do_ref, mlp_acc, gnt_acc, mid_ref, wo_ref, mlp_was, gnt_was):
    rows, width = g_ref.shape
    wo = wo_ref[...].reshape(width, width)

    def norm(c):
        at = slice(c * BLOCK, (c + 1) * BLOCK)
        mid = mid_ref[at, :]
        out_ref[at, :] = ((mid + (mlp_acc[at, :] + mlp_was[at, :])) * valid_ref[at, :]).astype(bf16)
        n, r = norm_stats(mid)
        grad = (gnt_acc[at, :] + gnt_was[at, :]) * gain_ref[...]
        gmid = g_ref[at, :].astype(f32) + norm_back(n, r, grad)
        gmid_ref[at, :] = gmid
        return (gmid.astype(bf16),)

    def attend(c, low):
        do_ref[:, :, c * BLOCK : (c + 1) * BLOCK] = dot_nt(wo, low).astype(bf16).reshape(do_ref.shape[0], 128, BLOCK)

    pipeline(rows // BLOCK, norm, attend)


def mlp(normed, g, pieces, steps, kept=None, final=None, events=()):
    rows, width = normed.shape
    acc = jax.ShapeDtypeStruct((rows, width), f32)
    kept = [] if kept is None else list(kept)
    total = pltpu.VMEM((rows, width), f32)

    def taken(a):
        return pl.BlockSpec((a.shape[0] // steps,) + a.shape[1:], lambda i: (i,) + (0,) * (a.ndim - 1))

    def once(a):
        return pl.BlockSpec(a.shape, lambda i: (0,) * len(a.shape), pipeline_mode=pl.Buffered(1))

    if final is None:
        extra, extra_specs, out_shape, scratch = [], [], [acc, acc], []
    else:
        mid, wo, valid, gain = extra = list(final)
        extra_specs = [pl.BlockSpec(memory_space=pl.ANY)] * 2 + [once(valid), once(gain)]
        out_shape = [
            jax.ShapeDtypeStruct((rows, width), bf16),
            acc,
            jax.ShapeDtypeStruct((wo.shape[0], 128, rows), bf16),
        ]
        scratch = [total, total, pltpu.VMEM(mid.shape, f32), pltpu.VMEM(wo.shape, bf16)]
    if kept:
        scratch += [total, total, pltpu.SemaphoreType.DMA((4,))]
    return pl.pallas_call(
        functools.partial(mlp_kernel, sources=len(pieces), resumed=bool(kept), events=len(events), last=final is not None),
        grid=(steps,),
        in_specs=[once(normed), once(g)]
        + [taken(a) for a in pieces]
        + [pl.BlockSpec(memory_space=pl.ANY) for _ in (*kept, *events)]
        + extra_specs,
        out_specs=[once(a) for a in out_shape],
        out_shape=out_shape,
        scratch_shapes=scratch,
        compiler_params=params(),
        cost_estimate=cost(4 + 5 * steps),
    )(normed, g, *pieces, *kept, *events, *extra)


def attn_bwd_kernel(ids_ref, qkv_ref, o_ref, do_ref, lse_ref, kaug_ref, qaug_ref, bias_ref, et_ref, lrs_ref, n_ref, d_ref, gl_ref, sum_ref, dk_acc, dv_acc, gb_acc):
    rows = qkv_ref.shape[2]
    step = pl.program_id(0)
    heads = []
    for h in range(2):
        q, k, v = (qkv_ref[0, h * 192 + 64 * t : h * 192 + 64 * t + 64] for t in range(3))
        heads.append((q, k, v, jnp.concatenate([q, qaug_ref[...]], axis=0), jnp.concatenate([k, kaug_ref[...]], axis=0)))
    units = [(h, ib) for h in range(2) for ib in range(rows // BLOCK)]

    def products(t):
        h, ib = units[t]
        q, k, v, qa, ka = heads[h]
        here = slice(ib * BLOCK, (ib + 1) * BLOCK)
        do, o = (ref[0, h * 64 : (h + 1) * 64, here] for ref in (do_ref, o_ref))
        inner = jnp.sum(do.astype(f32) * o.astype(f32), axis=0, keepdims=True)
        return do, inner, score_block(ka, qa, bias_ref, ib), dot_tn(v[:, : (ib + 1) * BLOCK], do)

    def scores(t, do, inner, s, dp):
        h, ib = units[t]
        p = jnp.exp(s - lse_ref[0, h : h + 1, ib * BLOCK : (ib + 1) * BLOCK])
        return do, (p * (dp - inner)).astype(bf16), p.astype(bf16)

    def grads(t, do, ds, p):
        h, ib = units[t]
        c = h * 192
        q, k = heads[h][:2]
        before, here = slice(0, ib * BLOCK), slice(ib * BLOCK, (ib + 1) * BLOCK)
        dq = (dot_nn(k[:, : (ib + 1) * BLOCK], ds) * 0.125).astype(bf16)
        d_ref[0, c : c + 32, here] = dq[:32]
        d_ref[0, c + 96 : c + 128, here] = dq[32:]
        for acc, part in ((dk_acc, dot_nt(q[:, here], ds)), (dv_acc, dot_nt(do, p))):
            if ib:
                acc[h, :, before] += part[:, before]
            acc[h, :, here] = part[:, here]

    pipeline(len(units), products, scores, grads)
    for h in range(2):
        c = h * 192
        for t, acc in ((32, dk_acc), (64, dv_acc)):
            low = acc[h].astype(bf16)
            d_ref[0, c + t : c + t + 32] = low[:32]
            d_ref[0, c + 96 + t : c + 128 + t] = low[32:]
    gl = jnp.zeros((16, rows), f32)
    for r in range(4):
        d = d_ref[0, r * 96 : r * 96 + 96]
        gl += dot_nn(et_ref[ids_ref[4 * step + r]], d)
        gb = dot_nt(lrs_ref[...], d)
        gb = adapter_scale * (gb[:8] + gb[8:])
        is_query = lax.broadcasted_iota(jnp.int32, (8, 32), 0) < 4
        gb_acc[ids_ref[4 * step + r]] = jnp.where(is_query, gb[:, :32], gb[:, 64:96])
    gl = gl[:8] + gl[8:]

    @pl.when(step == 0)
    def _():
        gl_ref[...] = gl

    @pl.when(step > 0)
    def _():
        gl_ref[...] += gl

    @pl.when(step == pl.num_programs(0) - 1)
    def _():
        hi, lo = split_hi_lo(gl_ref[...])
        sum_ref[:8] = dot_nn(hi, n_ref[...]) + dot_nn(lo, n_ref[...])
        sum_ref[8:] = jnp.concatenate([gb_acc[t] for t in range(gb_acc.shape[0])], axis=1)


def attn_bwd(ids, qkv, o, do, lse, kaug, qaug, bias, et, lrs, normed):
    shards, _, rows = qkv.shape
    width = normed.shape[1]

    def fixed(*shape):
        return pl.BlockSpec(shape, lambda i, ids: (0,) * len(shape))

    def rel(*shape):
        return pl.BlockSpec((1,) + shape, lambda i, ids: (i,) + (0,) * len(shape))

    return pl.pallas_call(
        attn_bwd_kernel,
        grid_spec=pltpu.PrefetchScalarGridSpec(
            num_scalar_prefetch=1,
            grid=(shards,),
            in_specs=[
                rel(384, rows), rel(128, rows), rel(128, rows), rel(2, rows),
                fixed(*kaug.shape), fixed(*qaug.shape), fixed(*bias.shape),
                fixed(*et.shape), fixed(*lrs.shape), fixed(*normed.shape),
            ],
            out_specs=[rel(384, rows), fixed(8, rows), fixed(16, width)],
            scratch_shapes=[pltpu.VMEM((2, 64, rows), f32)] * 2 + [pltpu.VMEM((4 * shards, 8, 32), f32)],
        ),
        out_shape=[
            jax.ShapeDtypeStruct((shards, 384, rows), bf16),
            jax.ShapeDtypeStruct((8, rows), f32),
            jax.ShapeDtypeStruct((16, width), f32),
        ],
        compiler_params=params(),
        cost_estimate=cost(35),
    )(ids, qkv, o, do, lse, kaug, qaug, bias, et, lrs, normed)


def input_grad_kernel(d_ref, w_ref, gl_ref, dq_ref, dv_ref, x_ref, gmid_ref, gain_ref, event_ref, out_ref):
    width = x_ref.shape[1]
    d = d_ref[...].reshape(-1, BLOCK)
    w = w_ref[...].reshape(-1, width)
    hi, lo = split_hi_lo(gl_ref[...])
    dhi, dlo = split_hi_lo(jnp.concatenate([dq_ref[...], dv_ref[...]], axis=0))
    g = dot_tn(d, w)
    g += dot_tn(jnp.concatenate([hi, lo, hi], axis=0), jnp.concatenate([dhi, dhi, dlo], axis=0))
    n, r = norm_stats(x_ref[...].astype(f32))
    out_ref[...] = (gmid_ref[...] + norm_back(n, r, g * gain_ref[...])).astype(bf16)


def input_grad_rows(d, w, gl, down_q, down_v, x, gmid, gain, event):
    rows, width = x.shape
    shards = d.shape[0]
    blk = pl.BlockSpec((BLOCK, width), lambda i: (i, 0))
    return pl.pallas_call(
        input_grad_kernel,
        grid=(rows // BLOCK,),
        in_specs=[
            pl.BlockSpec((shards, 384, BLOCK), lambda i: (0, 0, i)),
            whole(w),
            pl.BlockSpec((8, BLOCK), lambda i: (0, i)),
            whole(down_q), whole(down_v),
            blk, blk,
            whole(gain),
            pl.BlockSpec(memory_space=pl.ANY),
        ],
        out_specs=blk,
        out_shape=jax.ShapeDtypeStruct((rows, width), bf16),
        compiler_params=params(),
        cost_estimate=cost(13),
    )(d, w, gl, down_q, down_v, x, gmid, gain, event)


def token_valid(counts, lengths):
    pieces = []
    for bucket, (length, number, offset) in enumerate(bucket_table()):
        slot_ids = jnp.arange(number, dtype=jnp.int32)
        living = slot_ids < counts[bucket]
        places = jnp.arange(length, dtype=jnp.int32)
        inside = places[None, :] < lengths[offset : offset + number][:, None]
        pieces.append(jnp.logical_and(living[:, None], inside).reshape(-1))
    return jnp.concatenate(pieces).astype(jnp.float32)


def slot_begins():
    begins = []
    at = 0
    for length, number, _ in bucket_table():
        for _ in range(number):
            begins.append(np.full((length,), at, np.int32))
            at += length
    return np.concatenate(begins)


def unit_pieces():
    full = [(flip, slot) for flip in range(2) for slot in range(4)]
    cut = [(flip ^ k, slot) for slots in ((0, 1), (2, 3)) for flip in (4, 2, 6) for k in (0, 1) for slot in slots]
    return full + cut


def flip_send(v, axis, bits):
    return lax.ppermute(v, axis, [(i, i ^ bits) for i in range(lax.axis_size(axis))])


def flip_sum(v, axis, flips):
    return sum([flip_send(v, axis, k) for k in flips], v)


def whole_item_shards(
    tokens,
    cotangent,
    first_norm_gain,
    query_key_value_weight,
    output_matrix,
    second_norm_gain,
    up_matrix,
    down_matrix,
    query_down_factor,
    query_adapter_up,
    value_down_factor,
    value_adapter_up,
    counts,
    lengths,
):
    rows, width = tokens.shape
    heads_here = query_key_value_weight.shape[1]
    dp_size = lax.axis_size("dp")
    mp_size = lax.axis_size("mp")
    model_index = lax.axis_index("mp")
    group_index = lax.axis_index("dp")
    shards = mp_size
    qkv_own = jnp.transpose(query_key_value_weight.reshape(width, 2, 3, 2, 32), (1, 3, 2, 4, 0))
    a_own = jnp.concatenate([qkv_own.reshape(4, 96, width), output_matrix.reshape(4, 32, width)], axis=1)
    up_parts, down_parts = up_matrix.reshape(4, 2, 64, width), down_matrix.reshape(4, 2, 64, width)
    swapped = (group_index % 2) * 2 + group_index // 2
    quarter_own = jnp.where(model_index % 2 == 1, swapped, group_index)

    def b_quarter(half):
        at = (quarter_own, half, 0, 0)
        parts = [lax.dynamic_slice(a, at, (1, 1, 64, width)).reshape(1, 64, width) for a in (up_parts, down_parts)]
        return jnp.concatenate(parts, axis=1)

    def together(*arrays):
        return lax.optimization_barrier(arrays)

    def stack(*parts):
        return jnp.concatenate(parts, axis=0)

    def core(v):
        return flip_send(v, "mp", 1)

    def in_plane(v, turn):
        flips = (1, 2) if turn == 0 else (2, 1)
        pairs = [(d * mp_size + i, (d ^ flips[i % 2]) * mp_size + i) for d in range(dp_size) for i in range(mp_size)]
        return lax.ppermute(v, ("dp", "mp"), pairs)

    flips, slots = (jnp.asarray(np.array(t, np.int32)) for t in zip(*unit_pieces()))
    shard_of = model_index ^ flips
    ids = shard_of * 4 + (jnp.where(shard_of % 2 == 1, swapped, group_index) ^ slots)

    gain_one = first_norm_gain[None, :]
    gain_two = second_norm_gain[None, :]
    down_q, down_v = query_down_factor.T, value_down_factor.T
    normed, grad_out_low, lr, lrs, bias, kaug, qaug, valid_col, e, et = prologue(
        model_index.reshape(1).astype(jnp.int32),
        counts,
        lengths,
        tokens,
        cotangent,
        gain_one,
        down_q,
        down_v,
        query_adapter_up,
        value_adapter_up,
    )
    def z_near(v):
        return flip_send(v, "mp", 2)

    def z_far(v):
        return flip_send(v, "mp", 4)

    def heads(pieces, unit, number, kept=None, events=()):
        return attn_fwd(ids, normed, pieces, e, lr, kaug, qaug, bias, unit, number, shards, kept, events)

    a_mine = lax.dynamic_slice_in_dim(a_own, quarter_own, 1, 0)
    a_f = z_far(a_mine)
    a_n = z_near(a_mine)
    a_core = core(a_own)
    b_own = jnp.concatenate([up_parts, down_parts], axis=2)
    a_f, a_n, b_mine, c_mine, b_own, normed = together(a_f, a_n, b_quarter(0), b_quarter(1), b_own, normed)
    a_fn, b_mine = together(z_near(a_f), b_mine)
    a_s = stack_now(a_f, a_n, a_fn)
    a_x = in_plane(a_s, 0)
    a_sc = core(a_s)
    b_f = z_far(b_mine)
    kept = heads([a_own], 0, 1, None, (a_s,))
    kept = heads([a_core], 1, 1, kept)
    a_s, a_x, a_sc, b_f, b_mine, c_mine, *kept = together(a_s, a_x, a_sc, b_f, b_mine, c_mine, *kept)
    a_xc = core(a_x)
    a_y, a_d = in_plane(a_s, 1), in_plane(a_x, 1)
    b_n = z_near(stack(b_mine, b_f))
    c_f = z_far(c_mine)
    kept = heads([a_s, a_x, a_sc, a_xc], 2, 3, kept)
    a_y, a_d, b_n, c_f, b_own, *kept = together(a_y, a_d, b_n, c_f, b_own, *kept)
    a_yc, a_dc = core(a_y), core(a_d)
    b_s = stack(b_f, b_n)
    b_x = in_plane(b_s, 0)
    c_n = z_near(stack(c_mine, c_f))
    b_core = core(b_own)
    kept = heads([a_y, a_d, a_yc, a_dc], 5, 3, kept)
    b_s, b_x, c_n, b_core, *kept = together(b_s, b_x, c_n, b_core, *kept)
    qkv, attended, lse, w_all, wo_all = kept
    b_y, b_d = in_plane(b_s, 1), in_plane(b_x, 1)
    b_xc = core(b_x)
    c_s = stack(c_f, c_n)
    c_x = in_plane(c_s, 0)
    mid, normed_two = out_proj(attended, wo_all, tokens, gain_two, (c_s,))
    b_xc, b_s, normed_two = together(b_xc, b_s, normed_two)
    b_sc = core(b_s)
    sums = mlp(normed_two, grad_out_low, [b_own.reshape(8, 128, width), b_core.reshape(8, 128, width)], 2)
    b_y, b_d, b_sc, c_x, c_s, *sums = together(b_y, b_d, b_sc, c_x, c_s, *sums)
    b_yc, b_dc = core(b_y), core(b_d)
    c_y, c_d = in_plane(c_s, 1), in_plane(c_x, 1)
    b_yc, b_dc, c_s, c_x = together(b_yc, b_dc, c_s, c_x)
    c_xc, c_sc = core(c_x), core(c_s)
    sums = mlp(normed_two, grad_out_low, [b_s, b_x, b_y, b_d, b_sc, b_xc, b_yc, b_dc], 3, sums)
    c_y, c_d, c_xc, c_sc, *sums = together(c_y, c_d, c_xc, c_sc, *sums)
    c_yc, c_dc = core(c_y), core(c_d)
    output, grad_mid, grad_attended = mlp(
        normed_two,
        grad_out_low,
        [c_s, c_x, c_y, c_d, c_sc, c_xc, c_yc, c_dc],
        3,
        sums,
        (mid, wo_all, valid_col, gain_two),
    )
    d, gl, packed = attn_bwd(ids, qkv, attended, grad_attended, lse, kaug, qaug, bias, et, lrs, normed)
    packed = flip_sum(packed, "mp", (1,))
    packed = flip_sum(packed, "mp", (2, 4, 6))
    event = packed
    packed = flip_sum(packed, "dp", tuple(range(1, dp_size)))
    input_grad = input_grad_rows(d, w_all, gl, down_q, down_v, tokens, grad_mid, gain_one, event)
    return (
        output,
        input_grad,
        packed[0:4].T,
        packed[8:12],
        packed[4:8].T,
        packed[12:16],
    )


def layer_norm(values, norm_gain):
    center = values - jnp.mean(values, axis=-1, keepdims=True)
    spread = jnp.mean(center * center, axis=-1, keepdims=True)
    return center * lax.rsqrt(spread + norm_eps) * norm_gain


def gelu_tanh(values):
    return jax.nn.gelu(values, approximate=True)


def contract_last(left, right):
    return lax.dot_general(
        left, right, (((1,), (1,)), ((), ())), preferred_element_type=jnp.float32
    )


def take_region(array, row_start, length, number):
    region = lax.slice_in_dim(array, row_start, row_start + length * number)
    return region.reshape((number, length) + array.shape[1:])


def allowed_pairs(valid_rows, length):
    places = jnp.arange(length, dtype=jnp.int32)
    causal = places[:, None] >= places[None, :]
    diagonal = places[:, None] == places[None, :]
    return jnp.logical_and(
        causal[None], jnp.logical_or(valid_rows[:, None, :] > 0.0, diagonal[None])
    )


def masked_scores(query_blk, key_blk, allowed, scale):
    scores = (
        jnp.einsum("nqhd,nkhd->nhqk", query_blk, key_blk, preferred_element_type=jnp.float32)
        * scale
    )
    return jnp.where(allowed[:, None], scores, masked_score)


def region_forward(query_blk, key_blk, value_blk, allowed, scale):
    scores = masked_scores(query_blk, key_blk, allowed, scale)
    row_max = jnp.max(scores, axis=-1, keepdims=True)
    raised = jnp.exp(scores - row_max)
    running = jnp.sum(raised, axis=-1, keepdims=True)
    probs_low = (raised / running).astype(jnp.bfloat16)
    attended = jnp.einsum(
        "nhqk,nkhd->nqhd", probs_low, value_blk, preferred_element_type=jnp.float32
    )
    return (attended, row_max + jnp.log(running))


def region_backward(query_blk, key_blk, value_blk, grad_blk, log_total, allowed, scale):
    scores = masked_scores(query_blk, key_blk, allowed, scale)
    probs = jnp.exp(scores - log_total)
    probs_low = probs.astype(jnp.bfloat16)
    grad_probs = jnp.einsum(
        "nqhd,nkhd->nhqk", grad_blk, value_blk, preferred_element_type=jnp.float32
    )
    inner = jnp.sum(grad_probs * probs, axis=-1, keepdims=True)
    grad_scores = (probs * (grad_probs - inner)).astype(jnp.bfloat16)
    grad_query = (
        jnp.einsum("nhqk,nkhd->nqhd", grad_scores, key_blk, preferred_element_type=jnp.float32)
        * scale
    )
    grad_key = (
        jnp.einsum("nhqk,nqhd->nkhd", grad_scores, query_blk, preferred_element_type=jnp.float32)
        * scale
    )
    grad_value = jnp.einsum(
        "nhqk,nqhd->nkhd", probs_low, grad_blk, preferred_element_type=jnp.float32
    )
    return (grad_query, grad_key, grad_value)


def split_item_shards(
    tokens,
    cotangent,
    first_norm_gain,
    query_key_value_weight,
    output_matrix,
    second_norm_gain,
    up_matrix,
    down_matrix,
    query_down_factor,
    query_adapter_up,
    value_down_factor,
    value_adapter_up,
    counts,
    lengths,
):
    local_rows = tokens.shape[0]
    model_width = tokens.shape[1]
    model_index = lax.axis_index("mp")
    heads_here = query_key_value_weight.shape[1]
    head_size = query_key_value_weight.shape[2] // 3
    head_columns = heads_here * head_size
    adapter_inner_rank = query_down_factor.shape[1]
    scale = 1.0 / math.sqrt(head_size)
    valid_all = token_valid(counts[0], lengths[0])
    rows_of_group = valid_all.shape[0]
    valid_here = lax.dynamic_slice_in_dim(valid_all, model_index * local_rows, local_rows)[:, None]
    adapter_down = jnp.concatenate([query_down_factor, value_down_factor], axis=1)
    inputs = tokens.astype(jnp.float32)
    first_normed = layer_norm(inputs, first_norm_gain).astype(jnp.bfloat16)
    rows_one_all = lax.all_gather(first_normed, "mp", axis=0, tiled=True)
    flat_qkv = query_key_value_weight.reshape(model_width, heads_here * 3 * head_size)
    projected_rows = jnp.dot(rows_one_all, flat_qkv, preferred_element_type=jnp.float32).reshape(
        rows_of_group, heads_here, 3, head_size
    )
    lowrank = jnp.dot(
        rows_one_all, adapter_down, precision=top_precision, preferred_element_type=jnp.float32
    )
    column_begin = model_index * head_columns
    query_up_factor = lax.dynamic_slice_in_dim(query_adapter_up, column_begin, head_columns, 1)
    value_up_factor = lax.dynamic_slice_in_dim(value_adapter_up, column_begin, head_columns, 1)
    query_vectors = projected_rows[:, :, 0] + adapter_scale * jnp.dot(
        lowrank[:, :adapter_inner_rank], query_up_factor, precision=top_precision
    ).reshape(rows_of_group, heads_here, head_size)
    rows_of_values = projected_rows[:, :, 2] + adapter_scale * jnp.dot(
        lowrank[:, adapter_inner_rank:], value_up_factor, precision=top_precision
    ).reshape(rows_of_group, heads_here, head_size)
    query_low = query_vectors.astype(jnp.bfloat16)
    key_low = projected_rows[:, :, 1].astype(jnp.bfloat16)
    value_low = rows_of_values.astype(jnp.bfloat16)
    attended_parts = []
    log_totals = []
    row_start = 0
    for length, number, offset in bucket_table():
        allowed = allowed_pairs(take_region(valid_all, row_start, length, number), length)
        attended, log_total = region_forward(
            take_region(query_low, row_start, length, number),
            take_region(key_low, row_start, length, number),
            take_region(value_low, row_start, length, number),
            allowed,
            scale,
        )
        attended_parts.append(attended.reshape(length * number, head_columns))
        log_totals.append(log_total)
        row_start = row_start + length * number
    attended_low = jnp.concatenate(attended_parts, axis=0).astype(jnp.bfloat16)
    out_flat = output_matrix.reshape(head_columns, model_width)
    attn_sum = lax.psum_scatter(
        jnp.dot(attended_low, out_flat, preferred_element_type=jnp.float32).astype(jnp.bfloat16),
        "mp",
        scatter_dimension=0,
        tiled=True,
    ).astype(jnp.float32)
    mid = inputs + attn_sum
    normed_two = layer_norm(mid, second_norm_gain).astype(jnp.bfloat16)
    grad_out = cotangent.astype(jnp.float32) * valid_here
    grad_out_low = grad_out.astype(jnp.bfloat16)
    rows_two_all = lax.all_gather(normed_two, "mp", axis=0, tiled=True)
    hidden_pre = contract_last(rows_two_all, up_matrix)
    hidden_low = gelu_tanh(hidden_pre).astype(jnp.bfloat16)
    mlp_sum = lax.psum_scatter(
        jnp.dot(hidden_low, down_matrix, preferred_element_type=jnp.float32).astype(jnp.bfloat16),
        "mp",
        scatter_dimension=0,
        tiled=True,
    ).astype(jnp.float32)
    grad_rows_two_all = lax.all_gather(grad_out_low, "mp", axis=0, tiled=True)
    grad_hidden = contract_last(grad_rows_two_all, down_matrix)
    gelu_unused, gelu_back = jax.vjp(gelu_tanh, hidden_pre)
    grad_pre_low = gelu_back(grad_hidden)[0].astype(jnp.bfloat16)
    grad_normed_two = lax.psum_scatter(
        jnp.dot(grad_pre_low, up_matrix, preferred_element_type=jnp.float32).astype(jnp.bfloat16),
        "mp",
        scatter_dimension=0,
        tiled=True,
    ).astype(jnp.float32)
    output = ((mid + mlp_sum) * valid_here).astype(jnp.bfloat16)
    norm_unused, norm_two_back = jax.vjp(lambda values: layer_norm(values, second_norm_gain), mid)
    grad_mid = grad_out + norm_two_back(grad_normed_two)[0]
    grad_mid_low = grad_mid.astype(jnp.bfloat16)
    grad_rows_one_all = lax.all_gather(grad_mid_low, "mp", axis=0, tiled=True)
    grad_attended = (
        contract_last(grad_rows_one_all, out_flat)
        .astype(jnp.bfloat16)
        .reshape(rows_of_group, heads_here, head_size)
    )
    grad_query_parts = []
    grad_key_parts = []
    grad_value_parts = []
    row_start = 0
    for (length, number, offset), log_total in zip(bucket_table(), log_totals):
        allowed = allowed_pairs(take_region(valid_all, row_start, length, number), length)
        grad_query, grad_key, grad_value = region_backward(
            take_region(query_low, row_start, length, number),
            take_region(key_low, row_start, length, number),
            take_region(value_low, row_start, length, number),
            take_region(grad_attended, row_start, length, number),
            log_total,
            allowed,
            scale,
        )
        grad_query_parts.append(grad_query.reshape(length * number, heads_here, head_size))
        grad_key_parts.append(grad_key.reshape(length * number, heads_here, head_size))
        grad_value_parts.append(grad_value.reshape(length * number, heads_here, head_size))
        row_start = row_start + length * number
    grad_query_low = jnp.concatenate(grad_query_parts, axis=0).astype(jnp.bfloat16)
    grad_key_low = jnp.concatenate(grad_key_parts, axis=0).astype(jnp.bfloat16)
    grad_value_low = jnp.concatenate(grad_value_parts, axis=0).astype(jnp.bfloat16)
    grad_query_flat = grad_query_low.reshape(rows_of_group, head_columns)
    grad_value_flat = grad_value_low.reshape(rows_of_group, head_columns)
    query_reduced_gradient = adapter_scale * jnp.dot(
        grad_query_flat,
        query_up_factor.T,
        precision=top_precision,
        preferred_element_type=jnp.float32,
    )
    value_reduced_gradient = adapter_scale * jnp.dot(
        grad_value_flat,
        value_up_factor.T,
        precision=top_precision,
        preferred_element_type=jnp.float32,
    )
    grad_lowrank = jnp.concatenate([query_reduced_gradient, value_reduced_gradient], axis=1)
    grad_qkv_low = jnp.stack([grad_query_low, grad_key_low, grad_value_low], axis=2).reshape(
        rows_of_group, heads_here * 3 * head_size
    )
    partial_rows = contract_last(grad_qkv_low, flat_qkv)
    grad_normed_one = lax.psum_scatter(
        (
            partial_rows
            + jnp.dot(
                grad_lowrank,
                adapter_down.T,
                precision=top_precision,
                preferred_element_type=jnp.float32,
            )
        ).astype(jnp.bfloat16),
        "mp",
        scatter_dimension=0,
        tiled=True,
    ).astype(jnp.float32)
    grad_a_part = lax.dot_general(
        rows_one_all,
        grad_lowrank,
        (((0,), (0,)), ((), ())),
        precision=top_precision,
        preferred_element_type=jnp.float32,
    )
    query_up_gradient_share = adapter_scale * lax.dot_general(
        lowrank[:, :adapter_inner_rank],
        grad_query_flat,
        (((0,), (0,)), ((), ())),
        precision=top_precision,
        preferred_element_type=jnp.float32,
    )
    value_up_gradient_share = adapter_scale * lax.dot_general(
        lowrank[:, adapter_inner_rank:],
        grad_value_flat,
        (((0,), (0,)), ((), ())),
        precision=top_precision,
        preferred_element_type=jnp.float32,
    )
    zero_cols = jnp.zeros((adapter_inner_rank, model_width), jnp.float32)
    grad_bq_full = lax.dynamic_update_slice_in_dim(
        zero_cols, query_up_gradient_share, column_begin, 1
    )
    grad_bv_full = lax.dynamic_update_slice_in_dim(
        zero_cols, value_up_gradient_share, column_begin, 1
    )
    grad_a_all, grad_bq_all, grad_bv_all = lax.psum(
        (grad_a_part, grad_bq_full, grad_bv_full), ("dp", "mp")
    )
    norm_unused, norm_one_back = jax.vjp(lambda values: layer_norm(values, first_norm_gain), inputs)
    input_grad = (grad_mid + norm_one_back(grad_normed_one)[0]).astype(jnp.bfloat16)
    return (
        output,
        input_grad,
        grad_a_all[:, :adapter_inner_rank],
        grad_bq_all,
        grad_a_all[:, adapter_inner_rank:],
        grad_bv_all,
    )


def solution(mesh):
    in_specs = (
        P(("dp", "mp"), None),
        P(("dp", "mp"), None),
        P(),
        P(None, "mp", None),
        P("mp", None, None),
        P(),
        P("mp", None),
        P("mp", None),
        P(),
        P(),
        P(),
        P(),
        P("dp", None),
        P("dp", None),
    )
    out_specs = (P(("dp", "mp"), None), P(("dp", "mp"), None), P(), P(), P(), P())
    whole_items = slot_begins().shape[0] // mesh.shape["mp"] == 8 * BASE_LEN and mesh.shape["dp"] == 4
    return jax.shard_map(
        whole_item_shards if whole_items else split_item_shards,
        mesh=mesh,
        in_specs=in_specs,
        out_specs=out_specs,
        check_vma=False,
    )
```

```python
import functools
import math

import jax
import jax.numpy as jnp
import numpy as np
from jax import lax
from jax.experimental import pallas as pl
from jax.experimental.pallas import tpu as pltpu
from jax.sharding import PartitionSpec as P

BASE_LEN = 128
ITEMS = 4
BLOCK = 256
VMEM_LIMIT = 62 * 1024 * 1024

norm_eps = 1e-05
adapter_scale = 8.0
top_precision = lax.Precision.HIGHEST
masked_score = -1e30
f32 = jnp.float32
bf16 = jnp.bfloat16


def bucket_table():
    return [
        (8 * BASE_LEN, ITEMS, 0),
        (4 * BASE_LEN, ITEMS, ITEMS),
        (2 * BASE_LEN, ITEMS, 2 * ITEMS),
        (BASE_LEN, 2 * ITEMS, 3 * ITEMS),
    ]


def dot_nn(a, b):
    return lax.dot_general(a, b, (((1,), (0,)), ((), ())), preferred_element_type=f32)


def dot_nt(a, b):
    return lax.dot_general(a, b, (((1,), (1,)), ((), ())), preferred_element_type=f32)


def dot_tn(a, b):
    return lax.dot_general(a, b, (((0,), (0,)), ((), ())), preferred_element_type=f32)


def split_hi_lo(v):
    hi = v.astype(bf16)
    return hi, (v - hi.astype(f32)).astype(bf16)


def whole(a):
    return pl.BlockSpec(a.shape, lambda *i: (0,) * a.ndim)


def params():
    return pltpu.CompilerParams(vmem_limit_bytes=VMEM_LIMIT)


def cost(us):
    return pl.CostEstimate(flops=int(us * 1e9), bytes_accessed=int(us * 2e6), transcendentals=0)


def slot_of(place):
    bucket = slot = inside = number = jnp.zeros_like(place)
    at = 0
    for t, (length, count, offset) in enumerate(bucket_table()):
        here = (place >= at) & (place < at + length * count)
        rel = place - at
        bucket = jnp.where(here, t, bucket)
        slot = jnp.where(here, rel // length, slot)
        inside = jnp.where(here, rel % length, inside)
        number = jnp.where(here, offset + rel // length, number)
        at += length * count
    return bucket, slot, inside, number


def prologue_kernel(at_ref, counts_ref, lengths_ref, x_ref, c_ref, gain_ref, dq_ref, dv_ref, qu_ref, vu_ref, n_ref, g_ref, lr_ref, lrs_ref, bias_ref, kaug_ref, qaug_ref, valid_ref, e_ref, et_ref):
    rows, width = x_ref.shape
    place = lax.broadcasted_iota(jnp.int32, (8, rows), 1)
    bucket, slot, inside, number = slot_of(at_ref[0] * rows + place)
    length = jnp.zeros_like(place)
    offset = 0
    for t, (_, count, offset) in enumerate(bucket_table()):
        for k in range(count):
            taken = jnp.where(k < counts_ref[0, t], lengths_ref[0, offset + k], 0)
            length = jnp.where(number == offset + k, taken, length)
    valid = jnp.where(inside < length, 1.0, 0.0).astype(f32)
    begin = place - inside
    valid_t = jnp.transpose(valid)[:, :1]
    valid_ref[...] = valid_t
    block = place // BLOCK
    row = lax.broadcasted_iota(jnp.int32, (8, rows), 0)
    first = jnp.zeros_like(place)
    for ib in range(rows // BLOCK):
        key = lax.broadcasted_iota(jnp.int32, (BLOCK, BLOCK), 0)
        query = lax.broadcasted_iota(jnp.int32, (BLOCK, BLOCK), 1)
        here = slice(ib * BLOCK, (ib + 1) * BLOCK)
        allowed = (
            (key <= query)
            & (key + ib * BLOCK >= begin[:1, here])
            & ((valid_t[here] > 0.0) | (key == query))
        )
        bias_ref[ib] = jnp.where(allowed, 0.0, masked_score).astype(f32)
        first = jnp.where(row == ib, begin[:, ib * BLOCK : ib * BLOCK + 1], first)
    own = block == row
    open_pair = own | ((place >= first) & (valid > 0.0)) | (row >= rows // BLOCK)
    zero = jnp.zeros((8, rows), f32)
    kaug_ref[...] = jnp.concatenate([jnp.where(open_pair, 0.0, masked_score), zero], axis=0).astype(bf16)
    qaug_ref[...] = jnp.concatenate([jnp.where(own, 1.0, 0.0), zero], axis=0).astype(bf16)

    @pl.loop(0, rows // BLOCK)
    def _(b):
        at = pl.ds(pl.multiple_of(b * BLOCK, BLOCK), BLOCK)
        n, _ = norm_stats(x_ref[at, :].astype(f32))
        n_ref[at, :] = (n * gain_ref[...]).astype(bf16)
        g_ref[at, :] = (c_ref[at, :].astype(f32) * valid_ref[at, :]).astype(bf16)

    hi, lo = split_hi_lo(jnp.concatenate([dq_ref[...], dv_ref[...]], axis=0))
    low = dot_nt(jnp.concatenate([hi, lo], axis=0), n_ref[...])
    hi, lo = split_hi_lo(low[:8] + low[8:])
    lr_ref[...] = jnp.concatenate([hi, lo, hi, jnp.zeros_like(hi)], axis=0)
    lrs_ref[...] = jnp.concatenate([hi, lo], axis=0)
    none = jnp.zeros((4, width), f32)
    for part, rows_of in ((0, [qu_ref[...], none]), (64, [none, vu_ref[...]])):
        hi, lo = split_hi_lo(adapter_scale * jnp.concatenate(rows_of, axis=0))
        full = jnp.concatenate([hi, hi, lo, jnp.zeros_like(hi)], axis=0).astype(f32)
        e_ref[:, part : part + 32, :] = jnp.transpose(full).astype(bf16).reshape(width // 32, 32, 32)
        pair = jnp.concatenate([hi, lo], axis=0).astype(f32)
        for p in range(width // 32):
            et_ref[p, :, part : part + 32] = pair[:, p * 32 : p * 32 + 32].astype(bf16)
    e_ref[:, 32:64, :] = jnp.zeros((width // 32, 32, 32), bf16)
    for p in range(width // 32):
        et_ref[p, :, 32:64] = jnp.zeros((16, 32), bf16)


def prologue(at, counts, lengths, x, c, gain, dq, dv, qu, vu):
    rows, width = x.shape
    smem = pl.BlockSpec(memory_space=pltpu.SMEM)
    return pl.pallas_call(
        prologue_kernel,
        in_specs=[smem, smem, smem] + [pl.BlockSpec(memory_space=pltpu.VMEM)] * 7,
        out_shape=[
            jax.ShapeDtypeStruct(shape, kind)
            for shape, kind in (
                ((rows, width), bf16),
                ((rows, width), bf16),
                ((32, rows), bf16),
                ((16, rows), bf16),
                ((rows // BLOCK, BLOCK, BLOCK), f32),
                ((16, rows), bf16),
                ((16, rows), bf16),
                ((rows, 1), f32),
                ((width // 32, 96, 32), bf16),
                ((width // 32, 16, 96), bf16),
            )
        ],
        compiler_params=params(),
        cost_estimate=cost(10),
    )(at, counts, lengths, x, c, gain, dq, dv, qu, vu)


def pipeline(number, *stages):
    held = {}
    for t in range(number + len(stages) - 1):
        for k, stage in enumerate(stages):
            unit = t - k
            if 0 <= unit < number:
                held[unit] = stage(unit, *held.pop(unit, ()))


def score_block(ka, qa, bias_ref, ib):
    s = dot_tn(ka[:, : (ib + 1) * BLOCK], qa[:, ib * BLOCK : (ib + 1) * BLOCK])
    diag = s[ib * BLOCK :] + bias_ref[ib]
    return jnp.concatenate([s[: ib * BLOCK], diag], axis=0) if ib else diag


def attn_fwd_kernel(ids_ref, n_ref, w0_ref, w1_ref, w2_ref, w3_ref, e_ref, lr_ref, kaug_ref, qaug_ref, bias_ref, *refs, first):
    qkv_ref, o_ref, lse_ref, w_ref, wo_ref = refs[-5:]
    rows, width = n_ref.shape
    unit = first + pl.program_id(0)
    pieces = [ref[...].reshape(128, width) for ref in (w0_ref, w1_ref, w2_ref, w3_ref)]
    w = jnp.concatenate([p[:96] for p in pieces], axis=0)
    w_ref[0] = w
    wo_ref[0] = jnp.concatenate([p[96:] for p in pieces], axis=0)
    e = jnp.concatenate([e_ref[ids_ref[4 * unit + r]] for r in range(4)], axis=0)
    low = (dot_nt(w, n_ref[...]) + dot_nn(e, lr_ref[...])).astype(bf16)
    heads = []
    for h in range(2):
        a, b = h * 192, h * 192 + 96
        q = jnp.concatenate([low[a : a + 32], low[b : b + 32]], axis=0) * bf16(0.125)
        k = jnp.concatenate([low[a + 32 : a + 64], low[b + 32 : b + 64]], axis=0)
        v = jnp.concatenate([low[a + 64 : a + 96], low[b + 64 : b + 96]], axis=0)
        for t, part in enumerate((q, k, v)):
            qkv_ref[0, h * 192 + t * 64 : h * 192 + t * 64 + 64] = part
        heads.append((jnp.concatenate([q, qaug_ref[...]], axis=0), jnp.concatenate([k, kaug_ref[...]], axis=0), v))
    units = [(h, ib) for ib in range(rows // BLOCK) for h in range(2)]

    def scores(t):
        h, ib = units[t]
        return (score_block(heads[h][1], heads[h][0], bias_ref, ib),)

    def softmax(t, s):
        h, ib = units[t]
        top = jnp.max(s, axis=0, keepdims=True)
        p = jnp.exp(s - top)
        total = jnp.sum(p, axis=0, keepdims=True)
        lse_ref[0, h : h + 1, ib * BLOCK : (ib + 1) * BLOCK] = top + jnp.log(total)
        return p.astype(bf16), 1.0 / total

    def attend(t, p, share):
        h, ib = units[t]
        o = dot_nn(heads[h][2][:, : (ib + 1) * BLOCK], p) * share
        o_ref[0, h * 64 : (h + 1) * 64, ib * BLOCK : (ib + 1) * BLOCK] = o.astype(bf16)

    pipeline(len(units), scores, softmax, attend)


def attn_fwd(ids, normed, pieces, e, lr, kaug, qaug, bias, unit, number, units, kept=None, events=()):
    rows, width = normed.shape
    whole_shard = len(pieces) == 1

    def piece(r):
        if whole_shard:
            return pl.BlockSpec((1, 128, width), lambda i, ids: (ids[4 * unit + r] % 4, 0, 0))
        return pl.BlockSpec((1, 128, width), lambda i, ids: (i, 0, 0))

    def fixed(a):
        return pl.BlockSpec(a.shape, lambda i, ids: (0,) * len(a.shape))

    def placed(*shape):
        return pl.BlockSpec((1,) + shape, lambda i, ids: (unit + i,) + (0,) * len(shape))

    shapes = [((384, rows), bf16), ((128, rows), bf16), ((2, rows), f32), ((384, width), bf16), ((128, width), bf16)]
    kept = [] if kept is None else list(kept)
    return pl.pallas_call(
        functools.partial(attn_fwd_kernel, first=unit),
        grid_spec=pltpu.PrefetchScalarGridSpec(
            num_scalar_prefetch=1,
            grid=(number,),
            in_specs=[fixed(normed)]
            + [piece(r) for r in range(4)]
            + [fixed(e), fixed(lr), fixed(kaug), fixed(qaug), fixed(bias)]
            + [pl.BlockSpec(memory_space=pl.ANY) for _ in (*kept, *events)],
            out_specs=[placed(*shape) for shape, _ in shapes],
        ),
        out_shape=[jax.ShapeDtypeStruct((units,) + shape, kind) for shape, kind in shapes],
        input_output_aliases={11 + t: t for t in range(len(kept))},
        compiler_params=params(),
        cost_estimate=cost(2 + 4 * number),
    )(ids, normed, *(pieces * 4 if whole_shard else pieces), e, lr, kaug, qaug, bias, *kept, *events)


def stack_kernel(*refs):
    out_ref = refs[-1]
    at = 0
    for ref in refs[:-1]:
        out_ref[at : at + ref.shape[0]] = ref[...]
        at += ref.shape[0]


def stack_now(*parts):
    out = jax.ShapeDtypeStruct((sum(a.shape[0] for a in parts),) + parts[0].shape[1:], parts[0].dtype)
    return pl.pallas_call(stack_kernel, out_shape=out, compiler_params=params(), cost_estimate=cost(1))(*parts)


def norm_stats(v):
    center = v - jnp.mean(v, axis=-1, keepdims=True)
    r = lax.rsqrt(jnp.mean(center * center, axis=-1, keepdims=True) + norm_eps)
    return center * r, r


def norm_back(n, r, f):
    return r * (f - jnp.mean(f, axis=-1, keepdims=True) - n * jnp.mean(f * n, axis=-1, keepdims=True))


def out_proj_kernel(o_ref, w_ref, x_ref, gain_ref, *refs):
    mid_ref, n_ref = refs[-2:]
    number, width = x_ref.shape
    w = w_ref[...].reshape(width, width)

    def product(c):
        return (dot_tn(o_ref[:, :, c * BLOCK : (c + 1) * BLOCK].reshape(width, BLOCK), w),)

    def norm(c, attn_sum):
        at = slice(c * BLOCK, (c + 1) * BLOCK)
        mid = x_ref[at, :].astype(f32) + attn_sum
        n, _ = norm_stats(mid)
        mid_ref[at, :] = mid
        n_ref[at, :] = (n * gain_ref[...]).astype(bf16)

    pipeline(number // BLOCK, product, norm)


def out_proj(o, w, x, gain, events=()):
    rows, width = x.shape
    shards = o.shape[0]
    at_once = 2 * BLOCK
    blk = pl.BlockSpec((at_once, width), lambda i: (i, 0))
    return pl.pallas_call(
        out_proj_kernel,
        grid=(rows // at_once,),
        in_specs=[pl.BlockSpec((shards, 128, at_once), lambda i: (0, 0, i)), whole(w), blk, whole(gain)]
        + [pl.BlockSpec(memory_space=pl.ANY) for _ in events],
        out_specs=[blk, blk],
        out_shape=[jax.ShapeDtypeStruct((rows, width), f32), jax.ShapeDtypeStruct((rows, width), bf16)],
        compiler_params=params(),
        cost_estimate=cost(7),
    )(o, w, x, gain, *events)


GELU_C = math.sqrt(2.0 / math.pi)


def mlp_kernel(n_ref, g_ref, *refs, sources, resumed, events, last):
    pieces, refs = refs[:sources], refs[sources:]
    if resumed:
        mlp_in, gnt_in, refs = refs[0], refs[1], refs[2:]
    refs = refs[events:]
    fetched = []
    if last:
        mid_in, wo_in, valid_ref, gain_ref, out_ref, gmid_ref, do_ref, mlp_acc, gnt_acc, mid_ref, wo_ref = refs[:11]
        refs = refs[11:]
        fetched += [(mid_in, mid_ref), (wo_in, wo_ref)]
    else:
        mlp_acc, gnt_acc = refs[:2]
        refs = refs[2:]
    if resumed:
        mlp_was, gnt_was, sems = refs
        fetched += [(mlp_in, mlp_was), (gnt_in, gnt_was)]
    step = pl.program_id(0)
    width = n_ref.shape[1]
    copies = [pltpu.make_async_copy(src, dst, sems.at[t]) for t, (src, dst) in enumerate(fetched)]

    @pl.when(step == 0)
    def _():
        for c in copies:
            c.start()
        mlp_acc[...] = jnp.zeros_like(mlp_acc)
        gnt_acc[...] = jnp.zeros_like(gnt_acc)

    held = [ref[...].reshape(-1, 128, width) for ref in pieces]
    up = jnp.concatenate([p[:, :64].reshape(-1, width) for p in held], axis=0)
    down = jnp.concatenate([p[:, 64:].reshape(-1, width) for p in held], axis=0)
    u = dot_nt(n_ref[...], up)
    gh = dot_nt(g_ref[...], down)
    uu = u * u
    th = jnp.tanh(u * (GELU_C + (GELU_C * 0.044715) * uu))
    half = 0.5 + 0.5 * th
    hidden = u * half
    slope = half + (0.5 * u) * (1.0 - th * th) * (GELU_C + (3.0 * 0.044715 * GELU_C) * uu)
    mlp_acc[...] += dot_nn(hidden.astype(bf16), down)
    gnt_acc[...] += dot_nn((gh * slope).astype(bf16), up)

    if copies:

        @pl.when(step == pl.num_programs(0) - 1)
        def _():
            for c in copies:
                c.wait()
            if not last:
                mlp_acc[...] += mlp_was[...]
                gnt_acc[...] += gnt_was[...]
            else:
                finish_rows(
                    g_ref, valid_ref, gain_ref, out_ref, gmid_ref, do_ref, mlp_acc, gnt_acc, mid_ref, wo_ref, mlp_was, gnt_was
                )


def finish_rows(g_ref, valid_ref, gain_ref, out_ref, gmid_ref, do_ref, mlp_acc, gnt_acc, mid_ref, wo_ref, mlp_was, gnt_was):
    rows, width = g_ref.shape
    wo = wo_ref[...].reshape(width, width)

    def norm(c):
        at = slice(c * BLOCK, (c + 1) * BLOCK)
        mid = mid_ref[at, :]
        out_ref[at, :] = ((mid + (mlp_acc[at, :] + mlp_was[at, :])) * valid_ref[at, :]).astype(bf16)
        n, r = norm_stats(mid)
        grad = (gnt_acc[at, :] + gnt_was[at, :]) * gain_ref[...]
        gmid = g_ref[at, :].astype(f32) + norm_back(n, r, grad)
        gmid_ref[at, :] = gmid
        return (gmid.astype(bf16),)

    def attend(c, low):
        do_ref[:, :, c * BLOCK : (c + 1) * BLOCK] = dot_nt(wo, low).astype(bf16).reshape(do_ref.shape[0], 128, BLOCK)

    pipeline(rows // BLOCK, norm, attend)


def mlp(normed, g, pieces, steps, kept=None, final=None, events=()):
    rows, width = normed.shape
    acc = jax.ShapeDtypeStruct((rows, width), f32)
    kept = [] if kept is None else list(kept)
    total = pltpu.VMEM((rows, width), f32)

    def taken(a):
        return pl.BlockSpec((a.shape[0] // steps,) + a.shape[1:], lambda i: (i,) + (0,) * (a.ndim - 1))

    def once(a):
        return pl.BlockSpec(a.shape, lambda i: (0,) * len(a.shape), pipeline_mode=pl.Buffered(1))

    if final is None:
        extra, extra_specs, out_shape, scratch = [], [], [acc, acc], []
    else:
        mid, wo, valid, gain = extra = list(final)
        extra_specs = [pl.BlockSpec(memory_space=pl.ANY)] * 2 + [once(valid), once(gain)]
        out_shape = [
            jax.ShapeDtypeStruct((rows, width), bf16),
            acc,
            jax.ShapeDtypeStruct((wo.shape[0], 128, rows), bf16),
        ]
        scratch = [total, total, pltpu.VMEM(mid.shape, f32), pltpu.VMEM(wo.shape, bf16)]
    if kept:
        scratch += [total, total, pltpu.SemaphoreType.DMA((4,))]
    return pl.pallas_call(
        functools.partial(mlp_kernel, sources=len(pieces), resumed=bool(kept), events=len(events), last=final is not None),
        grid=(steps,),
        in_specs=[once(normed), once(g)]
        + [taken(a) for a in pieces]
        + [pl.BlockSpec(memory_space=pl.ANY) for _ in (*kept, *events)]
        + extra_specs,
        out_specs=[once(a) for a in out_shape],
        out_shape=out_shape,
        scratch_shapes=scratch,
        compiler_params=params(),
        cost_estimate=cost(4 + 5 * steps),
    )(normed, g, *pieces, *kept, *events, *extra)


def attn_bwd_kernel(ids_ref, qkv_ref, o_ref, do_ref, lse_ref, kaug_ref, qaug_ref, bias_ref, et_ref, lrs_ref, n_ref, d_ref, gl_ref, sum_ref, dk_acc, dv_acc, gb_acc):
    rows = qkv_ref.shape[2]
    step = pl.program_id(0)
    heads = []
    for h in range(2):
        q, k, v = (qkv_ref[0, h * 192 + 64 * t : h * 192 + 64 * t + 64] for t in range(3))
        heads.append((q, k, v, jnp.concatenate([q, qaug_ref[...]], axis=0), jnp.concatenate([k, kaug_ref[...]], axis=0)))
    units = [(h, ib) for h in range(2) for ib in range(rows // BLOCK)]

    def products(t):
        h, ib = units[t]
        q, k, v, qa, ka = heads[h]
        here = slice(ib * BLOCK, (ib + 1) * BLOCK)
        do, o = (ref[0, h * 64 : (h + 1) * 64, here] for ref in (do_ref, o_ref))
        inner = jnp.sum(do.astype(f32) * o.astype(f32), axis=0, keepdims=True)
        return do, inner, score_block(ka, qa, bias_ref, ib), dot_tn(v[:, : (ib + 1) * BLOCK], do)

    def scores(t, do, inner, s, dp):
        h, ib = units[t]
        p = jnp.exp(s - lse_ref[0, h : h + 1, ib * BLOCK : (ib + 1) * BLOCK])
        return do, (p * (dp - inner)).astype(bf16), p.astype(bf16)

    def grads(t, do, ds, p):
        h, ib = units[t]
        c = h * 192
        q, k = heads[h][:2]
        before, here = slice(0, ib * BLOCK), slice(ib * BLOCK, (ib + 1) * BLOCK)
        dq = (dot_nn(k[:, : (ib + 1) * BLOCK], ds) * 0.125).astype(bf16)
        d_ref[0, c : c + 32, here] = dq[:32]
        d_ref[0, c + 96 : c + 128, here] = dq[32:]
        for acc, part in ((dk_acc, dot_nt(q[:, here], ds)), (dv_acc, dot_nt(do, p))):
            if ib:
                acc[h, :, before] += part[:, before]
            acc[h, :, here] = part[:, here]

    pipeline(len(units), products, scores, grads)
    for h in range(2):
        c = h * 192
        for t, acc in ((32, dk_acc), (64, dv_acc)):
            low = acc[h].astype(bf16)
            d_ref[0, c + t : c + t + 32] = low[:32]
            d_ref[0, c + 96 + t : c + 128 + t] = low[32:]
    gl = jnp.zeros((16, rows), f32)
    for r in range(4):
        d = d_ref[0, r * 96 : r * 96 + 96]
        gl += dot_nn(et_ref[ids_ref[4 * step + r]], d)
    gl = gl[:8] + gl[8:]
    gb = dot_nt(lrs_ref[...], d_ref[0])
    gb = adapter_scale * (gb[:8] + gb[8:])
    is_query = lax.broadcasted_iota(jnp.int32, (8, 32), 0) < 4
    for r in range(4):
        gb_acc[ids_ref[4 * step + r]] = jnp.where(
            is_query, gb[:, r * 96 : r * 96 + 32], gb[:, r * 96 + 64 : r * 96 + 96]
        )

    @pl.when(step == 0)
    def _():
        gl_ref[...] = gl

    @pl.when(step > 0)
    def _():
        gl_ref[...] += gl

    @pl.when(step == pl.num_programs(0) - 1)
    def _():
        hi, lo = split_hi_lo(gl_ref[...])
        sum_ref[:8] = dot_nn(hi, n_ref[...]) + dot_nn(lo, n_ref[...])
        sum_ref[8:] = jnp.concatenate([gb_acc[t] for t in range(gb_acc.shape[0])], axis=1)


def attn_bwd(ids, qkv, o, do, lse, kaug, qaug, bias, et, lrs, normed):
    shards, _, rows = qkv.shape
    width = normed.shape[1]

    def fixed(*shape):
        return pl.BlockSpec(shape, lambda i, ids: (0,) * len(shape))

    def rel(*shape):
        return pl.BlockSpec((1,) + shape, lambda i, ids: (i,) + (0,) * len(shape))

    return pl.pallas_call(
        attn_bwd_kernel,
        grid_spec=pltpu.PrefetchScalarGridSpec(
            num_scalar_prefetch=1,
            grid=(shards,),
            in_specs=[
                rel(384, rows), rel(128, rows), rel(128, rows), rel(2, rows),
                fixed(*kaug.shape), fixed(*qaug.shape), fixed(*bias.shape),
                fixed(*et.shape), fixed(*lrs.shape), fixed(*normed.shape),
            ],
            out_specs=[rel(384, rows), fixed(8, rows), fixed(16, width)],
            scratch_shapes=[pltpu.VMEM((2, 64, rows), f32)] * 2 + [pltpu.VMEM((4 * shards, 8, 32), f32)],
        ),
        out_shape=[
            jax.ShapeDtypeStruct((shards, 384, rows), bf16),
            jax.ShapeDtypeStruct((8, rows), f32),
            jax.ShapeDtypeStruct((16, width), f32),
        ],
        compiler_params=params(),
        cost_estimate=cost(35),
    )(ids, qkv, o, do, lse, kaug, qaug, bias, et, lrs, normed)


def input_grad_kernel(d_ref, w_ref, gl_ref, dq_ref, dv_ref, x_ref, gmid_ref, gain_ref, event_ref, out_ref):
    width = x_ref.shape[1]
    d = d_ref[...].reshape(-1, BLOCK)
    w = w_ref[...].reshape(-1, width)
    hi, lo = split_hi_lo(gl_ref[...])
    dhi, dlo = split_hi_lo(jnp.concatenate([dq_ref[...], dv_ref[...]], axis=0))
    g = dot_tn(d, w)
    g += dot_tn(jnp.concatenate([hi, lo, hi], axis=0), jnp.concatenate([dhi, dhi, dlo], axis=0))
    n, r = norm_stats(x_ref[...].astype(f32))
    out_ref[...] = (gmid_ref[...] + norm_back(n, r, g * gain_ref[...])).astype(bf16)


def input_grad_rows(d, w, gl, down_q, down_v, x, gmid, gain, event):
    rows, width = x.shape
    shards = d.shape[0]
    blk = pl.BlockSpec((BLOCK, width), lambda i: (i, 0))
    return pl.pallas_call(
        input_grad_kernel,
        grid=(rows // BLOCK,),
        in_specs=[
            pl.BlockSpec((shards, 384, BLOCK), lambda i: (0, 0, i)),
            whole(w),
            pl.BlockSpec((8, BLOCK), lambda i: (0, i)),
            whole(down_q), whole(down_v),
            blk, blk,
            whole(gain),
            pl.BlockSpec(memory_space=pl.ANY),
        ],
        out_specs=blk,
        out_shape=jax.ShapeDtypeStruct((rows, width), bf16),
        compiler_params=params(),
        cost_estimate=cost(13),
    )(d, w, gl, down_q, down_v, x, gmid, gain, event)


def token_valid(counts, lengths):
    pieces = []
    for bucket, (length, number, offset) in enumerate(bucket_table()):
        slot_ids = jnp.arange(number, dtype=jnp.int32)
        living = slot_ids < counts[bucket]
        places = jnp.arange(length, dtype=jnp.int32)
        inside = places[None, :] < lengths[offset : offset + number][:, None]
        pieces.append(jnp.logical_and(living[:, None], inside).reshape(-1))
    return jnp.concatenate(pieces).astype(jnp.float32)


def slot_begins():
    begins = []
    at = 0
    for length, number, _ in bucket_table():
        for _ in range(number):
            begins.append(np.full((length,), at, np.int32))
            at += length
    return np.concatenate(begins)


def unit_pieces():
    full = [(flip, slot) for flip in range(2) for slot in range(4)]
    cut = [(flip ^ k, slot) for slots in ((0, 1), (2, 3)) for flip in (4, 2, 6) for k in (0, 1) for slot in slots]
    return full + cut


def flip_send(v, axis, bits):
    return lax.ppermute(v, axis, [(i, i ^ bits) for i in range(lax.axis_size(axis))])


def flip_sum(v, axis, flips):
    return sum([flip_send(v, axis, k) for k in flips], v)


def whole_item_shards(
    tokens,
    cotangent,
    first_norm_gain,
    query_key_value_weight,
    output_matrix,
    second_norm_gain,
    up_matrix,
    down_matrix,
    query_down_factor,
    query_adapter_up,
    value_down_factor,
    value_adapter_up,
    counts,
    lengths,
):
    rows, width = tokens.shape
    heads_here = query_key_value_weight.shape[1]
    dp_size = lax.axis_size("dp")
    mp_size = lax.axis_size("mp")
    model_index = lax.axis_index("mp")
    group_index = lax.axis_index("dp")
    shards = mp_size
    qkv_own = jnp.transpose(query_key_value_weight.reshape(width, 2, 3, 2, 32), (1, 3, 2, 4, 0))
    a_own = jnp.concatenate([qkv_own.reshape(4, 96, width), output_matrix.reshape(4, 32, width)], axis=1)
    up_parts, down_parts = up_matrix.reshape(4, 2, 64, width), down_matrix.reshape(4, 2, 64, width)
    swapped = (group_index % 2) * 2 + group_index // 2
    quarter_own = jnp.where(model_index % 2 == 1, swapped, group_index)

    def b_quarter(half):
        at = (quarter_own, half, 0, 0)
        parts = [lax.dynamic_slice(a, at, (1, 1, 64, width)).reshape(1, 64, width) for a in (up_parts, down_parts)]
        return jnp.concatenate(parts, axis=1)

    def together(*arrays):
        return lax.optimization_barrier(arrays)

    def stack(*parts):
        return jnp.concatenate(parts, axis=0)

    def core(v):
        return flip_send(v, "mp", 1)

    def in_plane(v, turn):
        flips = (1, 2) if turn == 0 else (2, 1)
        pairs = [(d * mp_size + i, (d ^ flips[i % 2]) * mp_size + i) for d in range(dp_size) for i in range(mp_size)]
        return lax.ppermute(v, ("dp", "mp"), pairs)

    flips, slots = (jnp.asarray(np.array(t, np.int32)) for t in zip(*unit_pieces()))
    shard_of = model_index ^ flips
    ids = shard_of * 4 + (jnp.where(shard_of % 2 == 1, swapped, group_index) ^ slots)

    gain_one = first_norm_gain[None, :]
    gain_two = second_norm_gain[None, :]
    down_q, down_v = query_down_factor.T, value_down_factor.T
    normed, grad_out_low, lr, lrs, bias, kaug, qaug, valid_col, e, et = prologue(
        model_index.reshape(1).astype(jnp.int32),
        counts,
        lengths,
        tokens,
        cotangent,
        gain_one,
        down_q,
        down_v,
        query_adapter_up,
        value_adapter_up,
    )
    def z_near(v):
        return flip_send(v, "mp", 2)

    def z_far(v):
        return flip_send(v, "mp", 4)

    def heads(pieces, unit, number, kept=None, events=()):
        return attn_fwd(ids, normed, pieces, e, lr, kaug, qaug, bias, unit, number, shards, kept, events)

    a_mine = lax.dynamic_slice_in_dim(a_own, quarter_own, 1, 0)
    a_f = z_far(a_mine)
    a_n = z_near(a_mine)
    a_core = core(a_own)
    b_own = jnp.concatenate([up_parts, down_parts], axis=2)
    a_f, a_n, b_mine, c_mine, b_own, normed = together(a_f, a_n, b_quarter(0), b_quarter(1), b_own, normed)
    a_fn, b_mine = together(z_near(a_f), b_mine)
    a_s = stack_now(a_f, a_n, a_fn)
    a_x = in_plane(a_s, 0)
    a_sc = core(a_s)
    b_f = z_far(b_mine)
    b_nm = z_near(b_mine)
    kept = heads([a_own], 0, 1, None, (a_s,))
    kept = heads([a_core], 1, 1, kept)
    a_s, a_x, a_sc, b_f, b_nm, c_mine, *kept = together(a_s, a_x, a_sc, b_f, b_nm, c_mine, *kept)
    a_xc = core(a_x)
    a_y, a_d = in_plane(a_s, 1), in_plane(a_x, 1)
    b_n = z_near(b_f)
    c_f = z_far(c_mine)
    kept = heads([a_s, a_x, a_sc, a_xc], 2, 3, kept)
    a_y, a_d, b_n, c_f, b_own, *kept = together(a_y, a_d, b_n, c_f, b_own, *kept)
    a_yc, a_dc = core(a_y), core(a_d)
    b_s = stack(b_f, b_nm, b_n)
    b_x = in_plane(b_s, 0)
    c_n = z_near(stack(c_mine, c_f))
    b_core = core(b_own)
    kept = heads([a_y, a_d, a_yc, a_dc], 5, 3, kept)
    b_s, b_x, c_n, b_core, *kept = together(b_s, b_x, c_n, b_core, *kept)
    qkv, attended, lse, w_all, wo_all = kept
    b_y, b_d = in_plane(b_s, 1), in_plane(b_x, 1)
    b_xc = core(b_x)
    c_s = stack(c_f, c_n)
    c_x = in_plane(c_s, 0)
    mid, normed_two = out_proj(attended, wo_all, tokens, gain_two, (c_s,))
    b_xc, b_s, normed_two = together(b_xc, b_s, normed_two)
    b_sc = core(b_s)
    sums = mlp(normed_two, grad_out_low, [b_own.reshape(8, 128, width), b_core.reshape(8, 128, width)], 2)
    b_y, b_d, b_sc, c_x, c_s, *sums = together(b_y, b_d, b_sc, c_x, c_s, *sums)
    b_yc, b_dc = core(b_y), core(b_d)
    c_y, c_d = in_plane(c_s, 1), in_plane(c_x, 1)
    b_yc, b_dc, c_s, c_x = together(b_yc, b_dc, c_s, c_x)
    c_xc, c_sc = core(c_x), core(c_s)
    sums = mlp(normed_two, grad_out_low, [b_s, b_x, b_y, b_d, b_sc, b_xc, b_yc, b_dc], 3, sums)
    c_y, c_d, c_xc, c_sc, *sums = together(c_y, c_d, c_xc, c_sc, *sums)
    c_yc, c_dc = core(c_y), core(c_d)
    output, grad_mid, grad_attended = mlp(
        normed_two,
        grad_out_low,
        [c_s, c_x, c_y, c_d, c_sc, c_xc, c_yc, c_dc],
        3,
        sums,
        (mid, wo_all, valid_col, gain_two),
    )
    d, gl, packed = attn_bwd(ids, qkv, attended, grad_attended, lse, kaug, qaug, bias, et, lrs, normed)
    packed = flip_sum(packed, "mp", (1,))
    packed = flip_sum(packed, "mp", (2, 4, 6))
    event = packed
    packed = flip_sum(packed, "dp", tuple(range(1, dp_size)))
    input_grad = input_grad_rows(d, w_all, gl, down_q, down_v, tokens, grad_mid, gain_one, event)
    return (
        output,
        input_grad,
        packed[0:4].T,
        packed[8:12],
        packed[4:8].T,
        packed[12:16],
    )


def layer_norm(values, norm_gain):
    center = values - jnp.mean(values, axis=-1, keepdims=True)
    spread = jnp.mean(center * center, axis=-1, keepdims=True)
    return center * lax.rsqrt(spread + norm_eps) * norm_gain


def gelu_tanh(values):
    return jax.nn.gelu(values, approximate=True)


def contract_last(left, right):
    return lax.dot_general(
        left, right, (((1,), (1,)), ((), ())), preferred_element_type=jnp.float32
    )


def take_region(array, row_start, length, number):
    region = lax.slice_in_dim(array, row_start, row_start + length * number)
    return region.reshape((number, length) + array.shape[1:])


def allowed_pairs(valid_rows, length):
    places = jnp.arange(length, dtype=jnp.int32)
    causal = places[:, None] >= places[None, :]
    diagonal = places[:, None] == places[None, :]
    return jnp.logical_and(
        causal[None], jnp.logical_or(valid_rows[:, None, :] > 0.0, diagonal[None])
    )


def masked_scores(query_blk, key_blk, allowed, scale):
    scores = (
        jnp.einsum("nqhd,nkhd->nhqk", query_blk, key_blk, preferred_element_type=jnp.float32)
        * scale
    )
    return jnp.where(allowed[:, None], scores, masked_score)


def region_forward(query_blk, key_blk, value_blk, allowed, scale):
    scores = masked_scores(query_blk, key_blk, allowed, scale)
    row_max = jnp.max(scores, axis=-1, keepdims=True)
    raised = jnp.exp(scores - row_max)
    running = jnp.sum(raised, axis=-1, keepdims=True)
    probs_low = (raised / running).astype(jnp.bfloat16)
    attended = jnp.einsum(
        "nhqk,nkhd->nqhd", probs_low, value_blk, preferred_element_type=jnp.float32
    )
    return (attended, row_max + jnp.log(running))


def region_backward(query_blk, key_blk, value_blk, grad_blk, log_total, allowed, scale):
    scores = masked_scores(query_blk, key_blk, allowed, scale)
    probs = jnp.exp(scores - log_total)
    probs_low = probs.astype(jnp.bfloat16)
    grad_probs = jnp.einsum(
        "nqhd,nkhd->nhqk", grad_blk, value_blk, preferred_element_type=jnp.float32
    )
    inner = jnp.sum(grad_probs * probs, axis=-1, keepdims=True)
    grad_scores = (probs * (grad_probs - inner)).astype(jnp.bfloat16)
    grad_query = (
        jnp.einsum("nhqk,nkhd->nqhd", grad_scores, key_blk, preferred_element_type=jnp.float32)
        * scale
    )
    grad_key = (
        jnp.einsum("nhqk,nqhd->nkhd", grad_scores, query_blk, preferred_element_type=jnp.float32)
        * scale
    )
    grad_value = jnp.einsum(
        "nhqk,nqhd->nkhd", probs_low, grad_blk, preferred_element_type=jnp.float32
    )
    return (grad_query, grad_key, grad_value)


def split_item_shards(
    tokens,
    cotangent,
    first_norm_gain,
    query_key_value_weight,
    output_matrix,
    second_norm_gain,
    up_matrix,
    down_matrix,
    query_down_factor,
    query_adapter_up,
    value_down_factor,
    value_adapter_up,
    counts,
    lengths,
):
    local_rows = tokens.shape[0]
    model_width = tokens.shape[1]
    model_index = lax.axis_index("mp")
    heads_here = query_key_value_weight.shape[1]
    head_size = query_key_value_weight.shape[2] // 3
    head_columns = heads_here * head_size
    adapter_inner_rank = query_down_factor.shape[1]
    scale = 1.0 / math.sqrt(head_size)
    valid_all = token_valid(counts[0], lengths[0])
    rows_of_group = valid_all.shape[0]
    valid_here = lax.dynamic_slice_in_dim(valid_all, model_index * local_rows, local_rows)[:, None]
    adapter_down = jnp.concatenate([query_down_factor, value_down_factor], axis=1)
    inputs = tokens.astype(jnp.float32)
    first_normed = layer_norm(inputs, first_norm_gain).astype(jnp.bfloat16)
    rows_one_all = lax.all_gather(first_normed, "mp", axis=0, tiled=True)
    flat_qkv = query_key_value_weight.reshape(model_width, heads_here * 3 * head_size)
    projected_rows = jnp.dot(rows_one_all, flat_qkv, preferred_element_type=jnp.float32).reshape(
        rows_of_group, heads_here, 3, head_size
    )
    lowrank = jnp.dot(
        rows_one_all, adapter_down, precision=top_precision, preferred_element_type=jnp.float32
    )
    column_begin = model_index * head_columns
    query_up_factor = lax.dynamic_slice_in_dim(query_adapter_up, column_begin, head_columns, 1)
    value_up_factor = lax.dynamic_slice_in_dim(value_adapter_up, column_begin, head_columns, 1)
    query_vectors = projected_rows[:, :, 0] + adapter_scale * jnp.dot(
        lowrank[:, :adapter_inner_rank], query_up_factor, precision=top_precision
    ).reshape(rows_of_group, heads_here, head_size)
    rows_of_values = projected_rows[:, :, 2] + adapter_scale * jnp.dot(
        lowrank[:, adapter_inner_rank:], value_up_factor, precision=top_precision
    ).reshape(rows_of_group, heads_here, head_size)
    query_low = query_vectors.astype(jnp.bfloat16)
    key_low = projected_rows[:, :, 1].astype(jnp.bfloat16)
    value_low = rows_of_values.astype(jnp.bfloat16)
    attended_parts = []
    log_totals = []
    row_start = 0
    for length, number, offset in bucket_table():
        allowed = allowed_pairs(take_region(valid_all, row_start, length, number), length)
        attended, log_total = region_forward(
            take_region(query_low, row_start, length, number),
            take_region(key_low, row_start, length, number),
            take_region(value_low, row_start, length, number),
            allowed,
            scale,
        )
        attended_parts.append(attended.reshape(length * number, head_columns))
        log_totals.append(log_total)
        row_start = row_start + length * number
    attended_low = jnp.concatenate(attended_parts, axis=0).astype(jnp.bfloat16)
    out_flat = output_matrix.reshape(head_columns, model_width)
    attn_sum = lax.psum_scatter(
        jnp.dot(attended_low, out_flat, preferred_element_type=jnp.float32).astype(jnp.bfloat16),
        "mp",
        scatter_dimension=0,
        tiled=True,
    ).astype(jnp.float32)
    mid = inputs + attn_sum
    normed_two = layer_norm(mid, second_norm_gain).astype(jnp.bfloat16)
    grad_out = cotangent.astype(jnp.float32) * valid_here
    grad_out_low = grad_out.astype(jnp.bfloat16)
    rows_two_all = lax.all_gather(normed_two, "mp", axis=0, tiled=True)
    hidden_pre = contract_last(rows_two_all, up_matrix)
    hidden_low = gelu_tanh(hidden_pre).astype(jnp.bfloat16)
    mlp_sum = lax.psum_scatter(
        jnp.dot(hidden_low, down_matrix, preferred_element_type=jnp.float32).astype(jnp.bfloat16),
        "mp",
        scatter_dimension=0,
        tiled=True,
    ).astype(jnp.float32)
    grad_rows_two_all = lax.all_gather(grad_out_low, "mp", axis=0, tiled=True)
    grad_hidden = contract_last(grad_rows_two_all, down_matrix)
    gelu_unused, gelu_back = jax.vjp(gelu_tanh, hidden_pre)
    grad_pre_low = gelu_back(grad_hidden)[0].astype(jnp.bfloat16)
    grad_normed_two = lax.psum_scatter(
        jnp.dot(grad_pre_low, up_matrix, preferred_element_type=jnp.float32).astype(jnp.bfloat16),
        "mp",
        scatter_dimension=0,
        tiled=True,
    ).astype(jnp.float32)
    output = ((mid + mlp_sum) * valid_here).astype(jnp.bfloat16)
    norm_unused, norm_two_back = jax.vjp(lambda values: layer_norm(values, second_norm_gain), mid)
    grad_mid = grad_out + norm_two_back(grad_normed_two)[0]
    grad_mid_low = grad_mid.astype(jnp.bfloat16)
    grad_rows_one_all = lax.all_gather(grad_mid_low, "mp", axis=0, tiled=True)
    grad_attended = (
        contract_last(grad_rows_one_all, out_flat)
        .astype(jnp.bfloat16)
        .reshape(rows_of_group, heads_here, head_size)
    )
    grad_query_parts = []
    grad_key_parts = []
    grad_value_parts = []
    row_start = 0
    for (length, number, offset), log_total in zip(bucket_table(), log_totals):
        allowed = allowed_pairs(take_region(valid_all, row_start, length, number), length)
        grad_query, grad_key, grad_value = region_backward(
            take_region(query_low, row_start, length, number),
            take_region(key_low, row_start, length, number),
            take_region(value_low, row_start, length, number),
            take_region(grad_attended, row_start, length, number),
            log_total,
            allowed,
            scale,
        )
        grad_query_parts.append(grad_query.reshape(length * number, heads_here, head_size))
        grad_key_parts.append(grad_key.reshape(length * number, heads_here, head_size))
        grad_value_parts.append(grad_value.reshape(length * number, heads_here, head_size))
        row_start = row_start + length * number
    grad_query_low = jnp.concatenate(grad_query_parts, axis=0).astype(jnp.bfloat16)
    grad_key_low = jnp.concatenate(grad_key_parts, axis=0).astype(jnp.bfloat16)
    grad_value_low = jnp.concatenate(grad_value_parts, axis=0).astype(jnp.bfloat16)
    grad_query_flat = grad_query_low.reshape(rows_of_group, head_columns)
    grad_value_flat = grad_value_low.reshape(rows_of_group, head_columns)
    query_reduced_gradient = adapter_scale * jnp.dot(
        grad_query_flat,
        query_up_factor.T,
        precision=top_precision,
        preferred_element_type=jnp.float32,
    )
    value_reduced_gradient = adapter_scale * jnp.dot(
        grad_value_flat,
        value_up_factor.T,
        precision=top_precision,
        preferred_element_type=jnp.float32,
    )
    grad_lowrank = jnp.concatenate([query_reduced_gradient, value_reduced_gradient], axis=1)
    grad_qkv_low = jnp.stack([grad_query_low, grad_key_low, grad_value_low], axis=2).reshape(
        rows_of_group, heads_here * 3 * head_size
    )
    partial_rows = contract_last(grad_qkv_low, flat_qkv)
    grad_normed_one = lax.psum_scatter(
        (
            partial_rows
            + jnp.dot(
                grad_lowrank,
                adapter_down.T,
                precision=top_precision,
                preferred_element_type=jnp.float32,
            )
        ).astype(jnp.bfloat16),
        "mp",
        scatter_dimension=0,
        tiled=True,
    ).astype(jnp.float32)
    grad_a_part = lax.dot_general(
        rows_one_all,
        grad_lowrank,
        (((0,), (0,)), ((), ())),
        precision=top_precision,
        preferred_element_type=jnp.float32,
    )
    query_up_gradient_share = adapter_scale * lax.dot_general(
        lowrank[:, :adapter_inner_rank],
        grad_query_flat,
        (((0,), (0,)), ((), ())),
        precision=top_precision,
        preferred_element_type=jnp.float32,
    )
    value_up_gradient_share = adapter_scale * lax.dot_general(
        lowrank[:, adapter_inner_rank:],
        grad_value_flat,
        (((0,), (0,)), ((), ())),
        precision=top_precision,
        preferred_element_type=jnp.float32,
    )
    zero_cols = jnp.zeros((adapter_inner_rank, model_width), jnp.float32)
    grad_bq_full = lax.dynamic_update_slice_in_dim(
        zero_cols, query_up_gradient_share, column_begin, 1
    )
    grad_bv_full = lax.dynamic_update_slice_in_dim(
        zero_cols, value_up_gradient_share, column_begin, 1
    )
    grad_a_all, grad_bq_all, grad_bv_all = lax.psum(
        (grad_a_part, grad_bq_full, grad_bv_full), ("dp", "mp")
    )
    norm_unused, norm_one_back = jax.vjp(lambda values: layer_norm(values, first_norm_gain), inputs)
    input_grad = (grad_mid + norm_one_back(grad_normed_one)[0]).astype(jnp.bfloat16)
    return (
        output,
        input_grad,
        grad_a_all[:, :adapter_inner_rank],
        grad_bq_all,
        grad_a_all[:, adapter_inner_rank:],
        grad_bv_all,
    )


def solution(mesh):
    in_specs = (
        P(("dp", "mp"), None),
        P(("dp", "mp"), None),
        P(),
        P(None, "mp", None),
        P("mp", None, None),
        P(),
        P("mp", None),
        P("mp", None),
        P(),
        P(),
        P(),
        P(),
        P("dp", None),
        P("dp", None),
    )
    out_specs = (P(("dp", "mp"), None), P(("dp", "mp"), None), P(), P(), P(), P())
    whole_items = slot_begins().shape[0] // mesh.shape["mp"] == 8 * BASE_LEN and mesh.shape["dp"] == 4
    return jax.shard_map(
        whole_item_shards if whole_items else split_item_shards,
        mesh=mesh,
        in_specs=in_specs,
        out_specs=out_specs,
        check_vma=False,
    )
```

```python
import functools
import math

import jax
import jax.numpy as jnp
import numpy as np
from jax import lax
from jax.experimental import pallas as pl
from jax.experimental.pallas import tpu as pltpu
from jax.sharding import PartitionSpec as P

BASE_LEN = 128
ITEMS = 4
BLOCK = 256
VMEM_LIMIT = 62 * 1024 * 1024

norm_eps = 1e-05
adapter_scale = 8.0
top_precision = lax.Precision.HIGHEST
masked_score = -1e30
f32 = jnp.float32
bf16 = jnp.bfloat16


def bucket_table():
    return [
        (8 * BASE_LEN, ITEMS, 0),
        (4 * BASE_LEN, ITEMS, ITEMS),
        (2 * BASE_LEN, ITEMS, 2 * ITEMS),
        (BASE_LEN, 2 * ITEMS, 3 * ITEMS),
    ]


def dot_nn(a, b):
    return lax.dot_general(a, b, (((1,), (0,)), ((), ())), preferred_element_type=f32)


def dot_nt(a, b):
    return lax.dot_general(a, b, (((1,), (1,)), ((), ())), preferred_element_type=f32)


def dot_tn(a, b):
    return lax.dot_general(a, b, (((0,), (0,)), ((), ())), preferred_element_type=f32)


def split_hi_lo(v):
    hi = v.astype(bf16)
    return hi, (v - hi.astype(f32)).astype(bf16)


def whole(a):
    return pl.BlockSpec(a.shape, lambda *i: (0,) * a.ndim)


def params():
    return pltpu.CompilerParams(vmem_limit_bytes=VMEM_LIMIT)


def cost(us):
    return pl.CostEstimate(flops=int(us * 1e9), bytes_accessed=int(us * 2e6), transcendentals=0)


def slot_of(place):
    bucket = slot = inside = number = jnp.zeros_like(place)
    at = 0
    for t, (length, count, offset) in enumerate(bucket_table()):
        here = (place >= at) & (place < at + length * count)
        rel = place - at
        bucket = jnp.where(here, t, bucket)
        slot = jnp.where(here, rel // length, slot)
        inside = jnp.where(here, rel % length, inside)
        number = jnp.where(here, offset + rel // length, number)
        at += length * count
    return bucket, slot, inside, number


def prologue_kernel(at_ref, counts_ref, lengths_ref, x_ref, c_ref, gain_ref, dq_ref, dv_ref, qu_ref, vu_ref, n_ref, g_ref, lr_ref, lrs_ref, bias_ref, kaug_ref, qaug_ref, valid_ref, e_ref, et_ref):
    rows, width = x_ref.shape
    place = lax.broadcasted_iota(jnp.int32, (8, rows), 1)
    bucket, slot, inside, number = slot_of(at_ref[0] * rows + place)
    length = jnp.zeros_like(place)
    offset = 0
    for t, (_, count, offset) in enumerate(bucket_table()):
        for k in range(count):
            taken = jnp.where(k < counts_ref[0, t], lengths_ref[0, offset + k], 0)
            length = jnp.where(number == offset + k, taken, length)
    valid = jnp.where(inside < length, 1.0, 0.0).astype(f32)
    begin = place - inside
    valid_t = jnp.transpose(valid)[:, :1]
    valid_ref[...] = valid_t
    block = place // BLOCK
    row = lax.broadcasted_iota(jnp.int32, (8, rows), 0)
    first = jnp.zeros_like(place)
    for ib in range(rows // BLOCK):
        key = lax.broadcasted_iota(jnp.int32, (BLOCK, BLOCK), 0)
        query = lax.broadcasted_iota(jnp.int32, (BLOCK, BLOCK), 1)
        here = slice(ib * BLOCK, (ib + 1) * BLOCK)
        allowed = (
            (key <= query)
            & (key + ib * BLOCK >= begin[:1, here])
            & ((valid_t[here] > 0.0) | (key == query))
        )
        bias_ref[ib] = jnp.where(allowed, 0.0, masked_score).astype(f32)
        first = jnp.where(row == ib, begin[:, ib * BLOCK : ib * BLOCK + 1], first)
    own = block == row
    open_pair = own | ((place >= first) & (valid > 0.0)) | (row >= rows // BLOCK)
    zero = jnp.zeros((8, rows), f32)
    kaug_ref[...] = jnp.concatenate([jnp.where(open_pair, 0.0, masked_score), zero], axis=0).astype(bf16)
    qaug_ref[...] = jnp.concatenate([jnp.where(own, 1.0, 0.0), zero], axis=0).astype(bf16)

    @pl.loop(0, rows // BLOCK)
    def _(b):
        at = pl.ds(pl.multiple_of(b * BLOCK, BLOCK), BLOCK)
        n, _ = norm_stats(x_ref[at, :].astype(f32))
        n_ref[at, :] = (n * gain_ref[...]).astype(bf16)
        g_ref[at, :] = (c_ref[at, :].astype(f32) * valid_ref[at, :]).astype(bf16)

    hi, lo = split_hi_lo(jnp.concatenate([dq_ref[...], dv_ref[...]], axis=0))
    low = dot_nt(jnp.concatenate([hi, lo], axis=0), n_ref[...])
    hi, lo = split_hi_lo(low[:8] + low[8:])
    lr_ref[...] = jnp.concatenate([hi, lo, hi, jnp.zeros_like(hi)], axis=0)
    lrs_ref[...] = jnp.concatenate([hi, lo], axis=0)
    none = jnp.zeros((4, width), f32)
    for part, rows_of in ((0, [qu_ref[...], none]), (64, [none, vu_ref[...]])):
        hi, lo = split_hi_lo(adapter_scale * jnp.concatenate(rows_of, axis=0))
        full = jnp.concatenate([hi, hi, lo, jnp.zeros_like(hi)], axis=0).astype(f32)
        e_ref[:, part : part + 32, :] = jnp.transpose(full).astype(bf16).reshape(width // 32, 32, 32)
        pair = jnp.concatenate([hi, lo], axis=0).astype(f32)
        for p in range(width // 32):
            et_ref[p, :, part : part + 32] = pair[:, p * 32 : p * 32 + 32].astype(bf16)
    e_ref[:, 32:64, :] = jnp.zeros((width // 32, 32, 32), bf16)
    for p in range(width // 32):
        et_ref[p, :, 32:64] = jnp.zeros((16, 32), bf16)


def prologue(at, counts, lengths, x, c, gain, dq, dv, qu, vu):
    rows, width = x.shape
    smem = pl.BlockSpec(memory_space=pltpu.SMEM)
    return pl.pallas_call(
        prologue_kernel,
        in_specs=[smem, smem, smem] + [pl.BlockSpec(memory_space=pltpu.VMEM)] * 7,
        out_shape=[
            jax.ShapeDtypeStruct(shape, kind)
            for shape, kind in (
                ((rows, width), bf16),
                ((rows, width), bf16),
                ((32, rows), bf16),
                ((16, rows), bf16),
                ((rows // BLOCK, BLOCK, BLOCK), f32),
                ((16, rows), bf16),
                ((16, rows), bf16),
                ((rows, 1), f32),
                ((width // 32, 96, 32), bf16),
                ((width // 32, 16, 96), bf16),
            )
        ],
        compiler_params=params(),
        cost_estimate=cost(10),
    )(at, counts, lengths, x, c, gain, dq, dv, qu, vu)


def pipeline(number, *stages):
    held = {}
    for t in range(number + len(stages) - 1):
        for k, stage in enumerate(stages):
            unit = t - k
            if 0 <= unit < number:
                held[unit] = stage(unit, *held.pop(unit, ()))


def score_block(ka, qa, bias_ref, ib):
    s = dot_tn(ka[:, : (ib + 1) * BLOCK], qa[:, ib * BLOCK : (ib + 1) * BLOCK])
    diag = s[ib * BLOCK :] + bias_ref[ib]
    return jnp.concatenate([s[: ib * BLOCK], diag], axis=0) if ib else diag


def attn_fwd_kernel(ids_ref, n_ref, w0_ref, w1_ref, w2_ref, w3_ref, e_ref, lr_ref, kaug_ref, qaug_ref, bias_ref, *refs, first):
    qkv_ref, o_ref, lse_ref, w_ref, wo_ref = refs[-5:]
    rows, width = n_ref.shape
    unit = first + pl.program_id(0)
    pieces = [ref[...].reshape(128, width) for ref in (w0_ref, w1_ref, w2_ref, w3_ref)]
    w = jnp.concatenate([p[:96] for p in pieces], axis=0)
    w_ref[0] = w
    wo_ref[0] = jnp.concatenate([p[96:] for p in pieces], axis=0)
    e = jnp.concatenate([e_ref[ids_ref[4 * unit + r]] for r in range(4)], axis=0)
    low = (dot_nt(w, n_ref[...]) + dot_nn(e, lr_ref[...])).astype(bf16)
    heads = []
    for h in range(2):
        a, b = h * 192, h * 192 + 96
        q = jnp.concatenate([low[a : a + 32], low[b : b + 32]], axis=0) * bf16(0.125)
        k = jnp.concatenate([low[a + 32 : a + 64], low[b + 32 : b + 64]], axis=0)
        v = jnp.concatenate([low[a + 64 : a + 96], low[b + 64 : b + 96]], axis=0)
        for t, part in enumerate((q, k, v)):
            qkv_ref[0, h * 192 + t * 64 : h * 192 + t * 64 + 64] = part
        heads.append((jnp.concatenate([q, qaug_ref[...]], axis=0), jnp.concatenate([k, kaug_ref[...]], axis=0), v))
    units = [(h, ib) for ib in range(rows // BLOCK) for h in range(2)]

    def scores(t):
        h, ib = units[t]
        return (score_block(heads[h][1], heads[h][0], bias_ref, ib),)

    def softmax(t, s):
        h, ib = units[t]
        top = jnp.max(s, axis=0, keepdims=True)
        p = jnp.exp(s - top)
        total = jnp.sum(p, axis=0, keepdims=True)
        lse_ref[0, h : h + 1, ib * BLOCK : (ib + 1) * BLOCK] = top + jnp.log(total)
        return p.astype(bf16), 1.0 / total

    def attend(t, p, share):
        h, ib = units[t]
        o = dot_nn(heads[h][2][:, : (ib + 1) * BLOCK], p) * share
        o_ref[0, h * 64 : (h + 1) * 64, ib * BLOCK : (ib + 1) * BLOCK] = o.astype(bf16)

    pipeline(len(units), scores, softmax, attend)


def attn_fwd(ids, normed, pieces, e, lr, kaug, qaug, bias, unit, number, units, kept=None, events=()):
    rows, width = normed.shape
    whole_shard = len(pieces) == 1

    def piece(r):
        if whole_shard:
            return pl.BlockSpec((1, 128, width), lambda i, ids: (ids[4 * unit + r] % 4, 0, 0))
        return pl.BlockSpec((1, 128, width), lambda i, ids: (i, 0, 0))

    def fixed(a):
        return pl.BlockSpec(a.shape, lambda i, ids: (0,) * len(a.shape))

    def placed(*shape):
        return pl.BlockSpec((1,) + shape, lambda i, ids: (unit + i,) + (0,) * len(shape))

    shapes = [((384, rows), bf16), ((128, rows), bf16), ((2, rows), f32), ((384, width), bf16), ((128, width), bf16)]
    kept = [] if kept is None else list(kept)
    return pl.pallas_call(
        functools.partial(attn_fwd_kernel, first=unit),
        grid_spec=pltpu.PrefetchScalarGridSpec(
            num_scalar_prefetch=1,
            grid=(number,),
            in_specs=[fixed(normed)]
            + [piece(r) for r in range(4)]
            + [fixed(e), fixed(lr), fixed(kaug), fixed(qaug), fixed(bias)]
            + [pl.BlockSpec(memory_space=pl.ANY) for _ in (*kept, *events)],
            out_specs=[placed(*shape) for shape, _ in shapes],
        ),
        out_shape=[jax.ShapeDtypeStruct((units,) + shape, kind) for shape, kind in shapes],
        input_output_aliases={11 + t: t for t in range(len(kept))},
        compiler_params=params(),
        cost_estimate=cost(2 + 4 * number),
    )(ids, normed, *(pieces * 4 if whole_shard else pieces), e, lr, kaug, qaug, bias, *kept, *events)


def stack_kernel(*refs):
    out_ref = refs[-1]
    at = 0
    for ref in refs[:-1]:
        out_ref[at : at + ref.shape[0]] = ref[...]
        at += ref.shape[0]


def stack_now(*parts):
    out = jax.ShapeDtypeStruct((sum(a.shape[0] for a in parts),) + parts[0].shape[1:], parts[0].dtype)
    return pl.pallas_call(stack_kernel, out_shape=out, compiler_params=params(), cost_estimate=cost(1))(*parts)


def norm_stats(v):
    center = v - jnp.mean(v, axis=-1, keepdims=True)
    r = lax.rsqrt(jnp.mean(center * center, axis=-1, keepdims=True) + norm_eps)
    return center * r, r


def norm_back(n, r, f):
    return r * (f - jnp.mean(f, axis=-1, keepdims=True) - n * jnp.mean(f * n, axis=-1, keepdims=True))


def out_proj_kernel(o_ref, w_ref, x_ref, gain_ref, *refs):
    mid_ref, n_ref = refs[-2:]
    number, width = x_ref.shape
    w = w_ref[...].reshape(width, width)

    def product(c):
        return (dot_tn(o_ref[:, :, c * BLOCK : (c + 1) * BLOCK].reshape(width, BLOCK), w),)

    def norm(c, attn_sum):
        at = slice(c * BLOCK, (c + 1) * BLOCK)
        mid = x_ref[at, :].astype(f32) + attn_sum
        n, _ = norm_stats(mid)
        mid_ref[at, :] = mid
        n_ref[at, :] = (n * gain_ref[...]).astype(bf16)

    pipeline(number // BLOCK, product, norm)


def out_proj(o, w, x, gain, events=()):
    rows, width = x.shape
    shards = o.shape[0]
    at_once = 2 * BLOCK
    blk = pl.BlockSpec((at_once, width), lambda i: (i, 0))
    return pl.pallas_call(
        out_proj_kernel,
        grid=(rows // at_once,),
        in_specs=[pl.BlockSpec((shards, 128, at_once), lambda i: (0, 0, i)), whole(w), blk, whole(gain)]
        + [pl.BlockSpec(memory_space=pl.ANY) for _ in events],
        out_specs=[blk, blk],
        out_shape=[jax.ShapeDtypeStruct((rows, width), f32), jax.ShapeDtypeStruct((rows, width), bf16)],
        compiler_params=params(),
        cost_estimate=cost(7),
    )(o, w, x, gain, *events)


GELU_C = math.sqrt(2.0 / math.pi)


def mlp_kernel(n_ref, g_ref, *refs, sources, resumed, events, last):
    pieces, refs = refs[:sources], refs[sources:]
    if resumed:
        mlp_in, gnt_in, refs = refs[0], refs[1], refs[2:]
    refs = refs[events:]
    fetched = []
    if last:
        mid_in, wo_in, valid_ref, gain_ref, out_ref, gmid_ref, do_ref, mlp_acc, gnt_acc, mid_ref, wo_ref = refs[:11]
        refs = refs[11:]
        fetched += [(mid_in, mid_ref), (wo_in, wo_ref)]
    else:
        mlp_acc, gnt_acc = refs[:2]
        refs = refs[2:]
    if resumed:
        mlp_was, gnt_was, sems = refs
        fetched += [(mlp_in, mlp_was), (gnt_in, gnt_was)]
    step = pl.program_id(0)
    width = n_ref.shape[1]
    copies = [pltpu.make_async_copy(src, dst, sems.at[t]) for t, (src, dst) in enumerate(fetched)]

    @pl.when(step == 0)
    def _():
        for c in copies:
            c.start()
        mlp_acc[...] = jnp.zeros_like(mlp_acc)
        gnt_acc[...] = jnp.zeros_like(gnt_acc)

    held = [ref[...].reshape(-1, 128, width) for ref in pieces]
    up = jnp.concatenate([p[:, :64].reshape(-1, width) for p in held], axis=0)
    down = jnp.concatenate([p[:, 64:].reshape(-1, width) for p in held], axis=0)
    u = dot_nt(n_ref[...], up)
    gh = dot_nt(g_ref[...], down)
    uu = u * u
    th = jnp.tanh(u * (GELU_C + (GELU_C * 0.044715) * uu))
    half = 0.5 + 0.5 * th
    hidden = u * half
    slope = half + (0.5 * u) * (1.0 - th * th) * (GELU_C + (3.0 * 0.044715 * GELU_C) * uu)
    mlp_acc[...] += dot_nn(hidden.astype(bf16), down)
    gnt_acc[...] += dot_nn((gh * slope).astype(bf16), up)

    if copies:

        @pl.when(step == pl.num_programs(0) - 1)
        def _():
            for c in copies:
                c.wait()
            if not last:
                mlp_acc[...] += mlp_was[...]
                gnt_acc[...] += gnt_was[...]
            else:
                finish_rows(
                    g_ref, valid_ref, gain_ref, out_ref, gmid_ref, do_ref, mlp_acc, gnt_acc, mid_ref, wo_ref, mlp_was, gnt_was
                )


def finish_rows(g_ref, valid_ref, gain_ref, out_ref, gmid_ref, do_ref, mlp_acc, gnt_acc, mid_ref, wo_ref, mlp_was, gnt_was):
    rows, width = g_ref.shape
    wo = wo_ref[...].reshape(width, width)

    def norm(c):
        at = slice(c * BLOCK, (c + 1) * BLOCK)
        mid = mid_ref[at, :]
        out_ref[at, :] = ((mid + (mlp_acc[at, :] + mlp_was[at, :])) * valid_ref[at, :]).astype(bf16)
        n, r = norm_stats(mid)
        grad = (gnt_acc[at, :] + gnt_was[at, :]) * gain_ref[...]
        gmid = g_ref[at, :].astype(f32) + norm_back(n, r, grad)
        gmid_ref[at, :] = gmid
        return (gmid.astype(bf16),)

    def attend(c, low):
        do_ref[:, :, c * BLOCK : (c + 1) * BLOCK] = dot_nt(wo, low).astype(bf16).reshape(do_ref.shape[0], 128, BLOCK)

    pipeline(rows // BLOCK, norm, attend)


def mlp(normed, g, pieces, steps, kept=None, final=None, events=()):
    rows, width = normed.shape
    acc = jax.ShapeDtypeStruct((rows, width), f32)
    kept = [] if kept is None else list(kept)
    total = pltpu.VMEM((rows, width), f32)

    def taken(a):
        return pl.BlockSpec((a.shape[0] // steps,) + a.shape[1:], lambda i: (i,) + (0,) * (a.ndim - 1))

    def once(a):
        return pl.BlockSpec(a.shape, lambda i: (0,) * len(a.shape), pipeline_mode=pl.Buffered(1))

    if final is None:
        extra, extra_specs, out_shape, scratch = [], [], [acc, acc], []
    else:
        mid, wo, valid, gain = extra = list(final)
        extra_specs = [pl.BlockSpec(memory_space=pl.ANY)] * 2 + [once(valid), once(gain)]
        out_shape = [
            jax.ShapeDtypeStruct((rows, width), bf16),
            acc,
            jax.ShapeDtypeStruct((wo.shape[0], 128, rows), bf16),
        ]
        scratch = [total, total, pltpu.VMEM(mid.shape, f32), pltpu.VMEM(wo.shape, bf16)]
    if kept:
        scratch += [total, total, pltpu.SemaphoreType.DMA((4,))]
    return pl.pallas_call(
        functools.partial(mlp_kernel, sources=len(pieces), resumed=bool(kept), events=len(events), last=final is not None),
        grid=(steps,),
        in_specs=[once(normed), once(g)]
        + [taken(a) for a in pieces]
        + [pl.BlockSpec(memory_space=pl.ANY) for _ in (*kept, *events)]
        + extra_specs,
        out_specs=[once(a) for a in out_shape],
        out_shape=out_shape,
        scratch_shapes=scratch,
        compiler_params=params(),
        cost_estimate=cost(4 + 5 * steps),
    )(normed, g, *pieces, *kept, *events, *extra)


def attn_bwd_kernel(ids_ref, qkv_ref, o_ref, do_ref, lse_ref, kaug_ref, qaug_ref, bias_ref, et_ref, lrs_ref, n_ref, d_ref, gl_ref, sum_ref, dk_acc, dv_acc, gb_acc):
    rows = qkv_ref.shape[2]
    step = pl.program_id(0)
    heads = []
    for h in range(2):
        q, k, v = (qkv_ref[0, h * 192 + 64 * t : h * 192 + 64 * t + 64] for t in range(3))
        heads.append((q, k, v, jnp.concatenate([q, qaug_ref[...]], axis=0), jnp.concatenate([k, kaug_ref[...]], axis=0)))
    units = [(h, ib) for h in range(2) for ib in range(rows // BLOCK)]

    def products(t):
        h, ib = units[t]
        q, k, v, qa, ka = heads[h]
        here = slice(ib * BLOCK, (ib + 1) * BLOCK)
        do, o = (ref[0, h * 64 : (h + 1) * 64, here] for ref in (do_ref, o_ref))
        inner = jnp.sum(do.astype(f32) * o.astype(f32), axis=0, keepdims=True)
        return do, inner, score_block(ka, qa, bias_ref, ib), dot_tn(v[:, : (ib + 1) * BLOCK], do)

    def scores(t, do, inner, s, dp):
        h, ib = units[t]
        p = jnp.exp(s - lse_ref[0, h : h + 1, ib * BLOCK : (ib + 1) * BLOCK])
        return do, (p * (dp - inner)).astype(bf16), p.astype(bf16)

    def grads(t, do, ds, p):
        h, ib = units[t]
        c = h * 192
        q, k = heads[h][:2]
        before, here = slice(0, ib * BLOCK), slice(ib * BLOCK, (ib + 1) * BLOCK)
        dq = (dot_nn(k[:, : (ib + 1) * BLOCK], ds) * 0.125).astype(bf16)
        d_ref[0, c : c + 32, here] = dq[:32]
        d_ref[0, c + 96 : c + 128, here] = dq[32:]
        for acc, part in ((dk_acc, dot_nt(q[:, here], ds)), (dv_acc, dot_nt(do, p))):
            if ib:
                acc[h, :, before] += part[:, before]
            acc[h, :, here] = part[:, here]

    pipeline(len(units), products, scores, grads)
    for h in range(2):
        c = h * 192
        for t, acc in ((32, dk_acc), (64, dv_acc)):
            low = acc[h].astype(bf16)
            d_ref[0, c + t : c + t + 32] = low[:32]
            d_ref[0, c + 96 + t : c + 128 + t] = low[32:]
    gl = jnp.zeros((16, rows), f32)
    for r in range(4):
        d = d_ref[0, r * 96 : r * 96 + 96]
        gl += dot_nn(et_ref[ids_ref[4 * step + r]], d)
    gl = gl[:8] + gl[8:]
    gb = dot_nt(lrs_ref[...], d_ref[0])
    gb = adapter_scale * (gb[:8] + gb[8:])
    is_query = lax.broadcasted_iota(jnp.int32, (8, 32), 0) < 4
    for r in range(4):
        gb_acc[ids_ref[4 * step + r]] = jnp.where(
            is_query, gb[:, r * 96 : r * 96 + 32], gb[:, r * 96 + 64 : r * 96 + 96]
        )

    @pl.when(step == 0)
    def _():
        gl_ref[...] = gl

    @pl.when(step > 0)
    def _():
        gl_ref[...] += gl

    @pl.when(step == pl.num_programs(0) - 1)
    def _():
        hi, lo = split_hi_lo(gl_ref[...])
        sum_ref[:8] = dot_nn(hi, n_ref[...]) + dot_nn(lo, n_ref[...])
        sum_ref[8:] = jnp.concatenate([gb_acc[t] for t in range(gb_acc.shape[0])], axis=1)


def attn_bwd(ids, qkv, o, do, lse, kaug, qaug, bias, et, lrs, normed):
    shards, _, rows = qkv.shape
    width = normed.shape[1]

    def fixed(*shape):
        return pl.BlockSpec(shape, lambda i, ids: (0,) * len(shape))

    def rel(*shape):
        return pl.BlockSpec((1,) + shape, lambda i, ids: (i,) + (0,) * len(shape))

    return pl.pallas_call(
        attn_bwd_kernel,
        grid_spec=pltpu.PrefetchScalarGridSpec(
            num_scalar_prefetch=1,
            grid=(shards,),
            in_specs=[
                rel(384, rows), rel(128, rows), rel(128, rows), rel(2, rows),
                fixed(*kaug.shape), fixed(*qaug.shape), fixed(*bias.shape),
                fixed(*et.shape), fixed(*lrs.shape), fixed(*normed.shape),
            ],
            out_specs=[rel(384, rows), fixed(8, rows), fixed(16, width)],
            scratch_shapes=[pltpu.VMEM((2, 64, rows), f32)] * 2 + [pltpu.VMEM((4 * shards, 8, 32), f32)],
        ),
        out_shape=[
            jax.ShapeDtypeStruct((shards, 384, rows), bf16),
            jax.ShapeDtypeStruct((8, rows), f32),
            jax.ShapeDtypeStruct((16, width), f32),
        ],
        compiler_params=params(),
        cost_estimate=cost(35),
    )(ids, qkv, o, do, lse, kaug, qaug, bias, et, lrs, normed)


def input_grad_kernel(d_ref, w_ref, gl_ref, dq_ref, dv_ref, x_ref, gmid_ref, gain_ref, event_ref, out_ref):
    width = x_ref.shape[1]
    d = d_ref[...].reshape(-1, BLOCK)
    w = w_ref[...].reshape(-1, width)
    hi, lo = split_hi_lo(gl_ref[...])
    dhi, dlo = split_hi_lo(jnp.concatenate([dq_ref[...], dv_ref[...]], axis=0))
    g = dot_tn(d, w)
    g += dot_tn(jnp.concatenate([hi, lo, hi], axis=0), jnp.concatenate([dhi, dhi, dlo], axis=0))
    n, r = norm_stats(x_ref[...].astype(f32))
    out_ref[...] = (gmid_ref[...] + norm_back(n, r, g * gain_ref[...])).astype(bf16)


def input_grad_rows(d, w, gl, down_q, down_v, x, gmid, gain, event):
    rows, width = x.shape
    shards = d.shape[0]
    blk = pl.BlockSpec((BLOCK, width), lambda i: (i, 0))
    return pl.pallas_call(
        input_grad_kernel,
        grid=(rows // BLOCK,),
        in_specs=[
            pl.BlockSpec((shards, 384, BLOCK), lambda i: (0, 0, i)),
            whole(w),
            pl.BlockSpec((8, BLOCK), lambda i: (0, i)),
            whole(down_q), whole(down_v),
            blk, blk,
            whole(gain),
            pl.BlockSpec(memory_space=pl.ANY),
        ],
        out_specs=blk,
        out_shape=jax.ShapeDtypeStruct((rows, width), bf16),
        compiler_params=params(),
        cost_estimate=cost(13),
    )(d, w, gl, down_q, down_v, x, gmid, gain, event)


def token_valid(counts, lengths):
    pieces = []
    for bucket, (length, number, offset) in enumerate(bucket_table()):
        slot_ids = jnp.arange(number, dtype=jnp.int32)
        living = slot_ids < counts[bucket]
        places = jnp.arange(length, dtype=jnp.int32)
        inside = places[None, :] < lengths[offset : offset + number][:, None]
        pieces.append(jnp.logical_and(living[:, None], inside).reshape(-1))
    return jnp.concatenate(pieces).astype(jnp.float32)


def slot_begins():
    begins = []
    at = 0
    for length, number, _ in bucket_table():
        for _ in range(number):
            begins.append(np.full((length,), at, np.int32))
            at += length
    return np.concatenate(begins)


def unit_pieces():
    full = [(flip, slot) for flip in range(2) for slot in range(4)]
    cut = [(flip ^ k, slot) for slots in ((0, 1), (2, 3)) for flip in (4, 2, 6) for k in (0, 1) for slot in slots]
    return full + cut


def flip_send(v, axis, bits):
    return lax.ppermute(v, axis, [(i, i ^ bits) for i in range(lax.axis_size(axis))])


def flip_sum(v, axis, flips):
    return sum([flip_send(v, axis, k) for k in flips], v)


def whole_item_shards(
    tokens,
    cotangent,
    first_norm_gain,
    query_key_value_weight,
    output_matrix,
    second_norm_gain,
    up_matrix,
    down_matrix,
    query_down_factor,
    query_adapter_up,
    value_down_factor,
    value_adapter_up,
    counts,
    lengths,
):
    rows, width = tokens.shape
    heads_here = query_key_value_weight.shape[1]
    dp_size = lax.axis_size("dp")
    mp_size = lax.axis_size("mp")
    model_index = lax.axis_index("mp")
    group_index = lax.axis_index("dp")
    shards = mp_size
    qkv_own = jnp.transpose(query_key_value_weight.reshape(width, 2, 3, 2, 32), (1, 3, 2, 4, 0))
    a_own = jnp.concatenate([qkv_own.reshape(4, 96, width), output_matrix.reshape(4, 32, width)], axis=1)
    up_parts, down_parts = up_matrix.reshape(4, 2, 64, width), down_matrix.reshape(4, 2, 64, width)
    swapped = (group_index % 2) * 2 + group_index // 2
    quarter_own = jnp.where(model_index % 2 == 1, swapped, group_index)

    def b_quarter(half):
        at = (quarter_own, half, 0, 0)
        parts = [lax.dynamic_slice(a, at, (1, 1, 64, width)).reshape(1, 64, width) for a in (up_parts, down_parts)]
        return jnp.concatenate(parts, axis=1)

    def together(*arrays):
        return lax.optimization_barrier(arrays)

    def stack(*parts):
        return jnp.concatenate(parts, axis=0)

    def core(v):
        return flip_send(v, "mp", 1)

    def in_plane(v, turn):
        flips = (1, 2) if turn == 0 else (2, 1)
        pairs = [(d * mp_size + i, (d ^ flips[i % 2]) * mp_size + i) for d in range(dp_size) for i in range(mp_size)]
        return lax.ppermute(v, ("dp", "mp"), pairs)

    flips, slots = (jnp.asarray(np.array(t, np.int32)) for t in zip(*unit_pieces()))
    shard_of = model_index ^ flips
    ids = shard_of * 4 + (jnp.where(shard_of % 2 == 1, swapped, group_index) ^ slots)

    gain_one = first_norm_gain[None, :]
    gain_two = second_norm_gain[None, :]
    down_q, down_v = query_down_factor.T, value_down_factor.T
    normed, grad_out_low, lr, lrs, bias, kaug, qaug, valid_col, e, et = prologue(
        model_index.reshape(1).astype(jnp.int32),
        counts,
        lengths,
        tokens,
        cotangent,
        gain_one,
        down_q,
        down_v,
        query_adapter_up,
        value_adapter_up,
    )
    def z_near(v):
        return flip_send(v, "mp", 2)

    def z_far(v):
        return flip_send(v, "mp", 4)

    def heads(pieces, unit, number, kept=None, events=()):
        return attn_fwd(ids, normed, pieces, e, lr, kaug, qaug, bias, unit, number, shards, kept, events)

    a_mine = lax.dynamic_slice_in_dim(a_own, quarter_own, 1, 0)
    a_f = z_far(a_mine)
    a_n = z_near(a_mine)
    a_core = core(a_own)
    b_own = jnp.concatenate([up_parts, down_parts], axis=2)
    a_f, a_n, b_mine, c_mine, b_own, normed = together(a_f, a_n, b_quarter(0), b_quarter(1), b_own, normed)
    a_fn, b_mine = together(z_near(a_f), b_mine)
    a_s = stack_now(a_f, a_n, a_fn)
    a_x = in_plane(a_s, 0)
    a_sc = core(a_s)
    b_f = z_far(b_mine)
    b_nm = z_near(b_mine)
    kept = heads([a_own], 0, 1, None, (a_s,))
    kept = heads([a_core], 1, 1, kept)
    a_s, a_x, a_sc, b_f, b_nm, c_mine, *kept = together(a_s, a_x, a_sc, b_f, b_nm, c_mine, *kept)
    a_xc = core(a_x)
    a_y, a_d = in_plane(a_s, 1), in_plane(a_x, 1)
    b_n = z_near(b_f)
    c_f = z_far(c_mine)
    kept = heads([a_s, a_x, a_sc, a_xc], 2, 3, kept)
    a_y, a_d, b_n, c_f, b_own, *kept = together(a_y, a_d, b_n, c_f, b_own, *kept)
    a_yc, a_dc = core(a_y), core(a_d)
    b_s = stack(b_f, b_nm, b_n)
    b_x = in_plane(b_s, 0)
    c_n = z_near(stack(c_mine, c_f))
    b_core = core(b_own)
    kept = heads([a_y, a_d, a_yc, a_dc], 5, 3, kept)
    b_s, b_x, c_n, b_core, *kept = together(b_s, b_x, c_n, b_core, *kept)
    qkv, attended, lse, w_all, wo_all = kept
    b_y, b_d = in_plane(b_s, 1), in_plane(b_x, 1)
    b_xc = core(b_x)
    c_s = stack(c_f, c_n)
    c_x = in_plane(c_s, 0)
    mid, normed_two = out_proj(attended, wo_all, tokens, gain_two, (c_s,))
    b_xc, b_s, normed_two = together(b_xc, b_s, normed_two)
    b_sc = core(b_s)
    sums = mlp(normed_two, grad_out_low, [b_own.reshape(8, 128, width), b_core.reshape(8, 128, width)], 2)
    b_y, b_d, b_sc, c_x, c_s, *sums = together(b_y, b_d, b_sc, c_x, c_s, *sums)
    b_yc, b_dc = core(b_y), core(b_d)
    c_y, c_d = in_plane(c_s, 1), in_plane(c_x, 1)
    b_yc, b_dc, c_s, c_x = together(b_yc, b_dc, c_s, c_x)
    c_xc, c_sc = core(c_x), core(c_s)
    sums = mlp(normed_two, grad_out_low, [b_s, b_x, b_y, b_d, b_sc, b_xc, b_yc, b_dc], 3, sums)
    c_y, c_d, c_xc, c_sc, *sums = together(c_y, c_d, c_xc, c_sc, *sums)
    c_yc, c_dc = core(c_y), core(c_d)
    output, grad_mid, grad_attended = mlp(
        normed_two,
        grad_out_low,
        [c_s, c_x, c_y, c_d, c_sc, c_xc, c_yc, c_dc],
        3,
        sums,
        (mid, wo_all, valid_col, gain_two),
    )
    d, gl, packed = attn_bwd(ids, qkv, attended, grad_attended, lse, kaug, qaug, bias, et, lrs, normed)
    packed = flip_sum(packed, "mp", (1,))
    input_grad = input_grad_rows(d, w_all, gl, down_q, down_v, tokens, grad_mid, gain_one, packed)
    packed, input_grad = together(flip_sum(packed, "mp", (2, 4, 6)), input_grad)
    packed = flip_sum(packed, "dp", tuple(range(1, dp_size)))
    return (
        output,
        input_grad,
        packed[0:4].T,
        packed[8:12],
        packed[4:8].T,
        packed[12:16],
    )


def layer_norm(values, norm_gain):
    center = values - jnp.mean(values, axis=-1, keepdims=True)
    spread = jnp.mean(center * center, axis=-1, keepdims=True)
    return center * lax.rsqrt(spread + norm_eps) * norm_gain


def gelu_tanh(values):
    return jax.nn.gelu(values, approximate=True)


def contract_last(left, right):
    return lax.dot_general(
        left, right, (((1,), (1,)), ((), ())), preferred_element_type=jnp.float32
    )


def take_region(array, row_start, length, number):
    region = lax.slice_in_dim(array, row_start, row_start + length * number)
    return region.reshape((number, length) + array.shape[1:])


def allowed_pairs(valid_rows, length):
    places = jnp.arange(length, dtype=jnp.int32)
    causal = places[:, None] >= places[None, :]
    diagonal = places[:, None] == places[None, :]
    return jnp.logical_and(
        causal[None], jnp.logical_or(valid_rows[:, None, :] > 0.0, diagonal[None])
    )


def masked_scores(query_blk, key_blk, allowed, scale):
    scores = (
        jnp.einsum("nqhd,nkhd->nhqk", query_blk, key_blk, preferred_element_type=jnp.float32)
        * scale
    )
    return jnp.where(allowed[:, None], scores, masked_score)


def region_forward(query_blk, key_blk, value_blk, allowed, scale):
    scores = masked_scores(query_blk, key_blk, allowed, scale)
    row_max = jnp.max(scores, axis=-1, keepdims=True)
    raised = jnp.exp(scores - row_max)
    running = jnp.sum(raised, axis=-1, keepdims=True)
    probs_low = (raised / running).astype(jnp.bfloat16)
    attended = jnp.einsum(
        "nhqk,nkhd->nqhd", probs_low, value_blk, preferred_element_type=jnp.float32
    )
    return (attended, row_max + jnp.log(running))


def region_backward(query_blk, key_blk, value_blk, grad_blk, log_total, allowed, scale):
    scores = masked_scores(query_blk, key_blk, allowed, scale)
    probs = jnp.exp(scores - log_total)
    probs_low = probs.astype(jnp.bfloat16)
    grad_probs = jnp.einsum(
        "nqhd,nkhd->nhqk", grad_blk, value_blk, preferred_element_type=jnp.float32
    )
    inner = jnp.sum(grad_probs * probs, axis=-1, keepdims=True)
    grad_scores = (probs * (grad_probs - inner)).astype(jnp.bfloat16)
    grad_query = (
        jnp.einsum("nhqk,nkhd->nqhd", grad_scores, key_blk, preferred_element_type=jnp.float32)
        * scale
    )
    grad_key = (
        jnp.einsum("nhqk,nqhd->nkhd", grad_scores, query_blk, preferred_element_type=jnp.float32)
        * scale
    )
    grad_value = jnp.einsum(
        "nhqk,nqhd->nkhd", probs_low, grad_blk, preferred_element_type=jnp.float32
    )
    return (grad_query, grad_key, grad_value)


def split_item_shards(
    tokens,
    cotangent,
    first_norm_gain,
    query_key_value_weight,
    output_matrix,
    second_norm_gain,
    up_matrix,
    down_matrix,
    query_down_factor,
    query_adapter_up,
    value_down_factor,
    value_adapter_up,
    counts,
    lengths,
):
    local_rows = tokens.shape[0]
    model_width = tokens.shape[1]
    model_index = lax.axis_index("mp")
    heads_here = query_key_value_weight.shape[1]
    head_size = query_key_value_weight.shape[2] // 3
    head_columns = heads_here * head_size
    adapter_inner_rank = query_down_factor.shape[1]
    scale = 1.0 / math.sqrt(head_size)
    valid_all = token_valid(counts[0], lengths[0])
    rows_of_group = valid_all.shape[0]
    valid_here = lax.dynamic_slice_in_dim(valid_all, model_index * local_rows, local_rows)[:, None]
    adapter_down = jnp.concatenate([query_down_factor, value_down_factor], axis=1)
    inputs = tokens.astype(jnp.float32)
    first_normed = layer_norm(inputs, first_norm_gain).astype(jnp.bfloat16)
    rows_one_all = lax.all_gather(first_normed, "mp", axis=0, tiled=True)
    flat_qkv = query_key_value_weight.reshape(model_width, heads_here * 3 * head_size)
    projected_rows = jnp.dot(rows_one_all, flat_qkv, preferred_element_type=jnp.float32).reshape(
        rows_of_group, heads_here, 3, head_size
    )
    lowrank = jnp.dot(
        rows_one_all, adapter_down, precision=top_precision, preferred_element_type=jnp.float32
    )
    column_begin = model_index * head_columns
    query_up_factor = lax.dynamic_slice_in_dim(query_adapter_up, column_begin, head_columns, 1)
    value_up_factor = lax.dynamic_slice_in_dim(value_adapter_up, column_begin, head_columns, 1)
    query_vectors = projected_rows[:, :, 0] + adapter_scale * jnp.dot(
        lowrank[:, :adapter_inner_rank], query_up_factor, precision=top_precision
    ).reshape(rows_of_group, heads_here, head_size)
    rows_of_values = projected_rows[:, :, 2] + adapter_scale * jnp.dot(
        lowrank[:, adapter_inner_rank:], value_up_factor, precision=top_precision
    ).reshape(rows_of_group, heads_here, head_size)
    query_low = query_vectors.astype(jnp.bfloat16)
    key_low = projected_rows[:, :, 1].astype(jnp.bfloat16)
    value_low = rows_of_values.astype(jnp.bfloat16)
    attended_parts = []
    log_totals = []
    row_start = 0
    for length, number, offset in bucket_table():
        allowed = allowed_pairs(take_region(valid_all, row_start, length, number), length)
        attended, log_total = region_forward(
            take_region(query_low, row_start, length, number),
            take_region(key_low, row_start, length, number),
            take_region(value_low, row_start, length, number),
            allowed,
            scale,
        )
        attended_parts.append(attended.reshape(length * number, head_columns))
        log_totals.append(log_total)
        row_start = row_start + length * number
    attended_low = jnp.concatenate(attended_parts, axis=0).astype(jnp.bfloat16)
    out_flat = output_matrix.reshape(head_columns, model_width)
    attn_sum = lax.psum_scatter(
        jnp.dot(attended_low, out_flat, preferred_element_type=jnp.float32).astype(jnp.bfloat16),
        "mp",
        scatter_dimension=0,
        tiled=True,
    ).astype(jnp.float32)
    mid = inputs + attn_sum
    normed_two = layer_norm(mid, second_norm_gain).astype(jnp.bfloat16)
    grad_out = cotangent.astype(jnp.float32) * valid_here
    grad_out_low = grad_out.astype(jnp.bfloat16)
    rows_two_all = lax.all_gather(normed_two, "mp", axis=0, tiled=True)
    hidden_pre = contract_last(rows_two_all, up_matrix)
    hidden_low = gelu_tanh(hidden_pre).astype(jnp.bfloat16)
    mlp_sum = lax.psum_scatter(
        jnp.dot(hidden_low, down_matrix, preferred_element_type=jnp.float32).astype(jnp.bfloat16),
        "mp",
        scatter_dimension=0,
        tiled=True,
    ).astype(jnp.float32)
    grad_rows_two_all = lax.all_gather(grad_out_low, "mp", axis=0, tiled=True)
    grad_hidden = contract_last(grad_rows_two_all, down_matrix)
    gelu_unused, gelu_back = jax.vjp(gelu_tanh, hidden_pre)
    grad_pre_low = gelu_back(grad_hidden)[0].astype(jnp.bfloat16)
    grad_normed_two = lax.psum_scatter(
        jnp.dot(grad_pre_low, up_matrix, preferred_element_type=jnp.float32).astype(jnp.bfloat16),
        "mp",
        scatter_dimension=0,
        tiled=True,
    ).astype(jnp.float32)
    output = ((mid + mlp_sum) * valid_here).astype(jnp.bfloat16)
    norm_unused, norm_two_back = jax.vjp(lambda values: layer_norm(values, second_norm_gain), mid)
    grad_mid = grad_out + norm_two_back(grad_normed_two)[0]
    grad_mid_low = grad_mid.astype(jnp.bfloat16)
    grad_rows_one_all = lax.all_gather(grad_mid_low, "mp", axis=0, tiled=True)
    grad_attended = (
        contract_last(grad_rows_one_all, out_flat)
        .astype(jnp.bfloat16)
        .reshape(rows_of_group, heads_here, head_size)
    )
    grad_query_parts = []
    grad_key_parts = []
    grad_value_parts = []
    row_start = 0
    for (length, number, offset), log_total in zip(bucket_table(), log_totals):
        allowed = allowed_pairs(take_region(valid_all, row_start, length, number), length)
        grad_query, grad_key, grad_value = region_backward(
            take_region(query_low, row_start, length, number),
            take_region(key_low, row_start, length, number),
            take_region(value_low, row_start, length, number),
            take_region(grad_attended, row_start, length, number),
            log_total,
            allowed,
            scale,
        )
        grad_query_parts.append(grad_query.reshape(length * number, heads_here, head_size))
        grad_key_parts.append(grad_key.reshape(length * number, heads_here, head_size))
        grad_value_parts.append(grad_value.reshape(length * number, heads_here, head_size))
        row_start = row_start + length * number
    grad_query_low = jnp.concatenate(grad_query_parts, axis=0).astype(jnp.bfloat16)
    grad_key_low = jnp.concatenate(grad_key_parts, axis=0).astype(jnp.bfloat16)
    grad_value_low = jnp.concatenate(grad_value_parts, axis=0).astype(jnp.bfloat16)
    grad_query_flat = grad_query_low.reshape(rows_of_group, head_columns)
    grad_value_flat = grad_value_low.reshape(rows_of_group, head_columns)
    query_reduced_gradient = adapter_scale * jnp.dot(
        grad_query_flat,
        query_up_factor.T,
        precision=top_precision,
        preferred_element_type=jnp.float32,
    )
    value_reduced_gradient = adapter_scale * jnp.dot(
        grad_value_flat,
        value_up_factor.T,
        precision=top_precision,
        preferred_element_type=jnp.float32,
    )
    grad_lowrank = jnp.concatenate([query_reduced_gradient, value_reduced_gradient], axis=1)
    grad_qkv_low = jnp.stack([grad_query_low, grad_key_low, grad_value_low], axis=2).reshape(
        rows_of_group, heads_here * 3 * head_size
    )
    partial_rows = contract_last(grad_qkv_low, flat_qkv)
    grad_normed_one = lax.psum_scatter(
        (
            partial_rows
            + jnp.dot(
                grad_lowrank,
                adapter_down.T,
                precision=top_precision,
                preferred_element_type=jnp.float32,
            )
        ).astype(jnp.bfloat16),
        "mp",
        scatter_dimension=0,
        tiled=True,
    ).astype(jnp.float32)
    grad_a_part = lax.dot_general(
        rows_one_all,
        grad_lowrank,
        (((0,), (0,)), ((), ())),
        precision=top_precision,
        preferred_element_type=jnp.float32,
    )
    query_up_gradient_share = adapter_scale * lax.dot_general(
        lowrank[:, :adapter_inner_rank],
        grad_query_flat,
        (((0,), (0,)), ((), ())),
        precision=top_precision,
        preferred_element_type=jnp.float32,
    )
    value_up_gradient_share = adapter_scale * lax.dot_general(
        lowrank[:, adapter_inner_rank:],
        grad_value_flat,
        (((0,), (0,)), ((), ())),
        precision=top_precision,
        preferred_element_type=jnp.float32,
    )
    zero_cols = jnp.zeros((adapter_inner_rank, model_width), jnp.float32)
    grad_bq_full = lax.dynamic_update_slice_in_dim(
        zero_cols, query_up_gradient_share, column_begin, 1
    )
    grad_bv_full = lax.dynamic_update_slice_in_dim(
        zero_cols, value_up_gradient_share, column_begin, 1
    )
    grad_a_all, grad_bq_all, grad_bv_all = lax.psum(
        (grad_a_part, grad_bq_full, grad_bv_full), ("dp", "mp")
    )
    norm_unused, norm_one_back = jax.vjp(lambda values: layer_norm(values, first_norm_gain), inputs)
    input_grad = (grad_mid + norm_one_back(grad_normed_one)[0]).astype(jnp.bfloat16)
    return (
        output,
        input_grad,
        grad_a_all[:, :adapter_inner_rank],
        grad_bq_all,
        grad_a_all[:, adapter_inner_rank:],
        grad_bv_all,
    )


def solution(mesh):
    in_specs = (
        P(("dp", "mp"), None),
        P(("dp", "mp"), None),
        P(),
        P(None, "mp", None),
        P("mp", None, None),
        P(),
        P("mp", None),
        P("mp", None),
        P(),
        P(),
        P(),
        P(),
        P("dp", None),
        P("dp", None),
    )
    out_specs = (P(("dp", "mp"), None), P(("dp", "mp"), None), P(), P(), P(), P())
    whole_items = slot_begins().shape[0] // mesh.shape["mp"] == 8 * BASE_LEN and mesh.shape["dp"] == 4
    return jax.shard_map(
        whole_item_shards if whole_items else split_item_shards,
        mesh=mesh,
        in_specs=in_specs,
        out_specs=out_specs,
        check_vma=False,
    )
```
